32 devices in a mesh: groups: 2 (over y), video: 4 (over x, core), frame: 4 (over z).
Axes of the slice: x: 2, y: 2, z: 4, core: 2. Of those that a mesh axis runs over, the one named last changes fastest.
Arguments:
- latents: bfloat16 [8, 4, 256, 320], P(('groups', 'video'), 'frame'), parts along dimension 0, may hold values from -6 to 6
- timesteps: int32 [8], P(('groups', 'video')), parts along dimension 0, may hold values from 0 to 999
- matchings: int32 [2, 8], P(None, 'groups'), parts along dimension 1, may hold values from 0 to 3, each once within a row
- tile_mask: int32 [2, 8, 2, 2], P(None, 'groups'), parts along dimension 1, may hold values from 0 to 1, as said below
- conv_first: bfloat16 [3, 3, 320, 320], replicated, may hold values from -0.109375 to 0.109375
- conv_second: bfloat16 [3, 3, 320, 320], replicated, may hold values from -0.109375 to 0.109375
- time_proj: bfloat16 [1280, 320], P('frame'), may hold values from -0.15625 to 0.15625
- epi_in: bfloat16 [3, 320, 320], P(None, 'frame'), may hold values from -48 to 48
- epi_out: bfloat16 [320, 320], P('frame'), may hold values from -0.3125 to 0.3125
- temp_in: bfloat16 [3, 320, 320], P(None, 'frame'), may hold values from -48 to 48
- temp_out: bfloat16 [320, 320], P('frame'), may hold values from -0.3125 to 0.3125
Outputs:
- denoised: bfloat16 [8, 4, 256, 320], P(('groups', 'video'), 'frame'), parts along dimension 0
The draws below stay inside these ranges and needn't reach their ends.
There are 2 independent parts, one for each index of `groups`. The reference program is written for one: setup_inputs(seed, part) draws one part's arguments, and reference() takes and returns one part's arrays. A program takes and returns all parts, laid end to end along the dimension named above; an argument that names none is the same for every part. Nothing has to cross between parts.
Inputs may be any that keep to these rules, and one draw needn't show every extreme that they name: Every row tile_mask[m, u, i, :] holds at least one 1.
All inputs are finite; a program needn't handle non-finite values.
Results may differ from the reference program's by a relative error of at most 0.035.
Values may be sent and summed in bfloat16 or wider, within the bound.
No kernel may reach another device: no remote copies, remote signals or barrier semaphores. Data moves between devices by JAX's collectives and lax.ppermute only.
A program may use at most 64 MiB of HBM per device.

```python
import math
import jax
import jax.numpy as jnp
from jax import lax

C = 320
HEADS = 8
NORM_GROUPS = 32
TEMB = 1280
H = 8
W = 32
TOKENS = 256
TILES = 2
VIDEOS = 4
FRAMES = 4


def draw_tile_mask(key, part):
    first_key, second_key = jax.random.split(jax.random.fold_in(key, 21))
    random_bits = jax.random.randint(first_key, (2, VIDEOS, TILES, TILES), 0, 2)
    forced = jax.random.randint(second_key, (2, VIDEOS, TILES, 1), 0, TILES)
    columns = jnp.arange(TILES, dtype=jnp.int32)
    return jnp.maximum(random_bits, (columns == forced).astype(jnp.int32)).astype(jnp.int32)


def projection_draw(key):
    base = jax.random.normal(key, (3, C, C), jnp.float32)
    base = jnp.clip(base, -6.0, 6.0) / jnp.sqrt(jnp.float32(C))
    boost = jnp.full((C,), 1.5, jnp.float32)
    factor = jnp.stack([boost, jnp.ones((C,), jnp.float32), jnp.ones((C,), jnp.float32)])
    return jnp.clip(base * factor[:, None, :], -48.0, 48.0).astype(jnp.bfloat16)


def draw_epi_in(key, part):
    return projection_draw(jax.random.fold_in(key, 11))


def draw_temp_in(key, part):
    return projection_draw(jax.random.fold_in(key, 12))


def set_ends(array, key, least, largest):
    extent = array.shape
    index_at = [jax.random.randint(jax.random.fold_in(key, axis), (), 0, extent[axis]) for axis in range(len(extent))]
    array = array.at[tuple(index_at)].set(least)
    longest = extent.index(max(extent))
    index_at[longest] = (index_at[longest] + 1) % extent[longest]
    return array.at[tuple(index_at)].set(largest)


def levels(key, extent, cuts, smallest, high):
    def one(position, parts):
        steps = jax.random.uniform(jax.random.fold_in(jax.random.fold_in(key, 6), position), (parts,), jnp.float32, smallest / len(cuts), high / len(cuts))
        return jnp.repeat(jnp.exp(steps), extent[position] // parts).reshape((-1,) + (1,) * (len(extent) - position - 1))

    factor_of = one(*cuts[0])
    for cut in cuts[1:]:
        factor_of = factor_of * one(*cut)
    return factor_of


def normal_values(stream_key, extent, scale, reach, pieces=(), kind=jnp.bfloat16):
    drawn = jax.random.normal(stream_key, extent, jnp.float32) * scale
    if len(pieces) > 0:
        drawn = levels(stream_key, extent, pieces, -0.22, 0.18) * drawn
    return jnp.clip(drawn, min=-reach, max=reach).astype(kind)


def setup_inputs(seed: int = 0, part: int = 0) -> dict:
    keys = jax.random.split(jax.random.key(seed), 12)
    own_keys = jax.random.split(jax.random.fold_in(keys[11], part), 12)
    return {
        "latents": normal_values(own_keys[0], (VIDEOS, FRAMES, TOKENS, C), 1.0, 6.0, ((0, 4), (1, 4))),
        "timesteps": set_ends(jax.random.randint(own_keys[1], (VIDEOS,), 0, 1000), jax.random.fold_in(own_keys[1], 1), 0, 999).astype(jnp.int32),
        "matchings": jax.vmap(lambda own: jax.random.permutation(own, VIDEOS))(jax.random.split(own_keys[2], 2)).reshape((2, VIDEOS)).astype(jnp.int32),
        "tile_mask": draw_tile_mask(jax.random.fold_in(jax.random.fold_in(keys[11], part), 71), part),
        "conv_first": normal_values(keys[4], (3, 3, C, C), (9 * C) ** -0.5, 0.109375),
        "conv_second": normal_values(keys[5], (3, 3, C, C), (9 * C) ** -0.5, 0.109375),
        "time_proj": normal_values(keys[6], (TEMB, C), TEMB ** -0.5, 0.15625, ((0, 4),)),
        "epi_in": draw_epi_in(jax.random.fold_in(keys[11], 71), part),
        "epi_out": normal_values(keys[8], (C, C), C ** -0.5, 0.3125, ((0, 4),)),
        "temp_in": draw_temp_in(jax.random.fold_in(keys[11], 71), part),
        "temp_out": normal_values(keys[10], (C, C), C ** -0.5, 0.3125, ((0, 4),)),
    }


epsilon = 1e-05
masked_fill = -1e+30

def group_norm(values):
    row_count, channels = values.shape
    grouped = values.reshape(row_count, NORM_GROUPS, channels // NORM_GROUPS)
    average = lax.optimization_barrier(jnp.mean(grouped, axis=(0, 2), keepdims=True))
    spread = lax.optimization_barrier(jnp.mean(jnp.square(grouped - average), axis=(0, 2), keepdims=True))
    return ((grouped - average) / jnp.sqrt(spread + epsilon)).reshape(row_count, channels)

def layer_norm(values):
    average = lax.optimization_barrier(jnp.mean(values, axis=-1, keepdims=True))
    spread = lax.optimization_barrier(jnp.mean(jnp.square(values - average), axis=-1, keepdims=True))
    return (values - average) / jnp.sqrt(spread + epsilon)

def convolve(activations, weight):
    channels = activations.shape[-1]
    planar = activations.reshape(H, W, channels)
    padded = jnp.pad(planar, ((1, 1), (1, 1), (0, 0)))
    totals = jnp.zeros((H * W, weight.shape[-1]), jnp.float32)
    for row_shift in range(3):
        for col_shift in range(3):
            window = padded[row_shift:row_shift + H, col_shift:col_shift + W].reshape(H * W, channels)
            totals = totals + jnp.dot(window, weight[row_shift, col_shift], preferred_element_type=jnp.float32)
    return totals

def sinusoid(timestep):
    half_width = TEMB // 2
    frequency = jnp.exp(-math.log(10000.0) * jnp.arange(half_width, dtype=jnp.float32) / half_width)
    angles = timestep.astype(jnp.float32)[:, None] * frequency[None, :]
    return jnp.concatenate([jnp.cos(angles), jnp.sin(angles)], axis=-1)

def softmax_last(scores):
    maxima = lax.optimization_barrier(jnp.max(scores, axis=-1, keepdims=True))
    powers = jnp.exp(scores - maxima)
    return powers / lax.optimization_barrier(jnp.sum(powers, axis=-1, keepdims=True))

def epipolar(queries, key_rows, value_rows, pair_mask):
    row_count, channels = queries.shape
    tiles = pair_mask.shape[0]
    width = row_count // tiles
    split = (row_count, HEADS, channels // HEADS)
    scaling = 1.0 / math.sqrt(channels // HEADS)
    scores = jnp.einsum('qhd,khd->hqk', queries.reshape(split).astype(jnp.float32), key_rows.reshape(split).astype(jnp.float32)) * scaling
    scores = scores.reshape(HEADS, tiles, width, tiles, width)
    scores = jnp.where(pair_mask[None, :, None, :, None] > 0, scores, masked_fill)
    weights = softmax_last(scores.reshape(HEADS, row_count, row_count)).astype(jnp.bfloat16)
    result = jnp.einsum('hqk,khd->qhd', weights.astype(jnp.float32), value_rows.reshape(split).astype(jnp.float32))
    return result.reshape(row_count, channels)

def frame_attention(queries, key_rows, value_rows):
    frames, pixels, channels = queries.shape
    split = (frames, pixels, HEADS, channels // HEADS)
    scaling = 1.0 / math.sqrt(channels // HEADS)
    scores = jnp.einsum('fphd,gphd->phfg', queries.reshape(split).astype(jnp.float32), key_rows.reshape(split).astype(jnp.float32)) * scaling
    weights = softmax_last(scores).astype(jnp.bfloat16)
    result = jnp.einsum('phfg,gphd->fphd', weights.astype(jnp.float32), value_rows.reshape(split).astype(jnp.float32))
    return result.astype(jnp.bfloat16).reshape(frames, pixels, channels)

def reference(latents, timesteps, matchings, tile_mask, conv_first, conv_second, time_proj, epi_in, epi_out, temp_in, temp_out):
    videos, frames = (latents.shape[0], latents.shape[1])
    time_act = jax.nn.silu(sinusoid(timesteps)).astype(jnp.bfloat16)
    time_bias = jnp.dot(time_act, time_proj, preferred_element_type=jnp.float32)
    bias_rows = jnp.repeat(time_bias, frames, axis=0)
    source_maps = latents.reshape(videos * frames, TOKENS, C)

    def residual_block(item):
        source, bias_row = item
        first_act = jax.nn.silu(group_norm(source.astype(jnp.float32))).astype(jnp.bfloat16)
        inner_sum = convolve(first_act, conv_first) + bias_row[None, :]
        second_act = jax.nn.silu(group_norm(inner_sum)).astype(jnp.bfloat16)
        hidden = (source.astype(jnp.float32) + convolve(second_act, conv_second)).astype(jnp.bfloat16)
        normed = layer_norm(hidden.astype(jnp.float32)).astype(jnp.bfloat16)
        return (hidden, normed)
    hidden, normed = lax.map(residual_block, (source_maps, bias_rows))
    normed_grid = normed.reshape(videos, frames, TOKENS, C)
    matched = jnp.stack([normed_grid[matchings[0]], normed_grid[matchings[1]]], axis=2).reshape(videos * frames, 2, TOKENS, C)
    pair_masks = jnp.repeat(jnp.transpose(tile_mask, (1, 0, 2, 3)), frames, axis=0)

    def cross_view(item):
        own_normed, own_hidden, pair_maps, masks_here = item
        queries = jnp.dot(own_normed, epi_in[0], preferred_element_type=jnp.float32).astype(jnp.bfloat16)
        summed = jnp.zeros((TOKENS, C), jnp.float32)
        for matching in range(2):
            key_rows = jnp.dot(pair_maps[matching], epi_in[1], preferred_element_type=jnp.float32).astype(jnp.bfloat16)
            value_rows = jnp.dot(pair_maps[matching], epi_in[2], preferred_element_type=jnp.float32).astype(jnp.bfloat16)
            summed = summed + epipolar(queries, key_rows, value_rows, masks_here[matching])
        mixture = summed.astype(jnp.bfloat16)
        return (own_hidden.astype(jnp.float32) + jnp.dot(mixture, epi_out, preferred_element_type=jnp.float32)).astype(jnp.bfloat16)
    second_hidden = lax.map(cross_view, (normed, hidden, matched, pair_masks)).reshape(videos, frames, TOKENS, C)

    def temporal(video_maps):
        flat_rows = video_maps.reshape(frames * TOKENS, C)
        temp_normed = layer_norm(flat_rows.astype(jnp.float32)).astype(jnp.bfloat16)
        frame_q = jnp.dot(temp_normed, temp_in[0], preferred_element_type=jnp.float32).astype(jnp.bfloat16).reshape(frames, TOKENS, C)
        frame_k = jnp.dot(temp_normed, temp_in[1], preferred_element_type=jnp.float32).astype(jnp.bfloat16).reshape(frames, TOKENS, C)
        frame_v = jnp.dot(temp_normed, temp_in[2], preferred_element_type=jnp.float32).astype(jnp.bfloat16).reshape(frames, TOKENS, C)
        attended = frame_attention(frame_q, frame_k, frame_v).reshape(frames * TOKENS, C)
        result = flat_rows.astype(jnp.float32) + jnp.dot(attended, temp_out, preferred_element_type=jnp.float32)
        return result.astype(jnp.bfloat16).reshape(frames, TOKENS, C)
    return lax.map(temporal, second_hidden)
```

```python
import functools
import math

import jax
import jax.numpy as jnp
from jax import lax
from jax.experimental import pallas as pl
from jax.experimental.pallas import tpu as pltpu
from jax.sharding import PartitionSpec as P

HEADS = 8
NORM_GROUPS = 32
TEMB = 1280
H = 8
W = 32

EPSILON = 1e-05
MASKED = -1e30
LOG2E = 1.4426950408889634

VMEM = pl.BlockSpec(memory_space=pltpu.VMEM)
SMEM = pl.BlockSpec(memory_space=pltpu.SMEM)
ANY = pl.BlockSpec(memory_space=pl.ANY)
f32 = jnp.float32
bf16 = jnp.bfloat16


def params():
    return pltpu.CompilerParams(vmem_limit_bytes=48 * 1024 * 1024)


def dot(a, b):
    return jnp.dot(a, b, preferred_element_type=f32)


def block_diagonal(size, width):
    rows = lax.broadcasted_iota(jnp.int32, (size, 1), 0).astype(f32)
    cols = lax.broadcasted_iota(jnp.int32, (1, size), 1).astype(f32)
    rows = jnp.floor((rows + 0.5) * (1.0 / width))
    cols = jnp.floor((cols + 0.5) * (1.0 / width))
    return (rows == cols).astype(f32).astype(bf16)


def group_sum(row, ones):
    first = row.astype(bf16).astype(f32)
    second = (row - first).astype(bf16).astype(f32)
    third = row - first - second
    index = lax.broadcasted_iota(jnp.int32, (16, row.shape[1]), 0)
    stacked = jnp.where(
        index == 0, first, jnp.where(index == 1, second, jnp.where(index == 2, third, 0.0))
    )
    return jnp.sum(dot(stacked.astype(bf16), ones), axis=0, keepdims=True)


def group_norm_silu(x):
    tokens, channels = x.shape
    width = channels // NORM_GROUPS
    ones = block_diagonal(channels, width)
    inverse = 1.0 / (tokens * width)
    average = group_sum(jnp.sum(x, axis=0, keepdims=True), ones) * inverse
    centred = x - average
    spread = group_sum(jnp.sum(centred * centred, axis=0, keepdims=True), ones) * inverse
    y = centred * lax.rsqrt(spread + EPSILON)
    return y / (1.0 + jnp.exp(-y))


def layer_norm(x):
    inverse = 1.0 / x.shape[1]
    average = jnp.sum(x, axis=1, keepdims=True) * inverse
    centred = x - average
    spread = jnp.sum(centred * centred, axis=1, keepdims=True) * inverse
    return centred * lax.rsqrt(spread + EPSILON)


def convolve(y, weight, padded):
    tokens, channels = y.shape
    column = lax.broadcasted_iota(jnp.int32, (tokens, 1), 0) & (W - 1)
    before = jnp.where(column == 0, 0.0, pltpu.roll(y, 1, 0))
    after = jnp.where(column == W - 1, 0.0, pltpu.roll(y, tokens - 1, 0))
    padded[pl.ds(0, W), :] = jnp.zeros((W, 3 * channels), bf16)
    padded[pl.ds(tokens + W, W), :] = jnp.zeros((W, 3 * channels), bf16)
    padded[pl.ds(W, tokens), :] = jnp.concatenate(
        [before.astype(bf16), y.astype(bf16), after.astype(bf16)], axis=1
    )
    total = dot(padded[pl.ds(0, tokens), :], weight[0])
    total += dot(padded[pl.ds(W, tokens), :], weight[1])
    total += dot(padded[pl.ds(2 * W, tokens), :], weight[2])
    return total


def first_kernel(source, weight_hbm, inner, weight, padded, sem):
    copy = pltpu.make_async_copy(weight_hbm, weight, sem)
    copy.start()
    y = group_norm_silu(source[...].astype(f32))
    copy.wait()
    inner[...] = convolve(y, weight, padded)


def second_kernel(source, inner, bias, weight_hbm, hidden, normed, weight, padded, sem):
    copy = pltpu.make_async_copy(weight_hbm, weight, sem)
    copy.start()
    y = group_norm_silu(inner[...] + bias[...])
    copy.wait()
    total = source[...].astype(f32) + convolve(y, weight, padded)
    rounded = total.astype(bf16)
    hidden[...] = rounded
    normed[...] = layer_norm(rounded.astype(f32)).astype(bf16)


def assemble(pieces, whole):
    parts, kinds, rows, _ = pieces.shape
    for part in range(parts):
        for kind in range(kinds):
            whole[kind, pl.ds(part * rows, rows), :] = pieces[part, kind]


def view_kernel(count, tiles, *refs):
    select, mask, me, hidden = refs[:4]
    maps = refs[4 : 4 + count]
    pieces, second, blocks, weights, chosen, totals = refs[4 + count :]
    tokens, channels = hidden.shape
    head = channels // HEADS
    width = tokens // tiles
    assemble(pieces, weights)
    scale = LOG2E / math.sqrt(head)
    queries = dot(maps[0][...], weights[0]).astype(bf16).astype(f32).T
    lane_tile = lax.broadcasted_iota(jnp.int32, (1, tokens), 1) // width
    windows = []
    for h in range(HEADS):
        low = h * head // 128 * 128
        high = min(channels, -(-(h + 1) * head // 128) * 128)
        row = lax.broadcasted_iota(jnp.int32, (high - low, 1), 0) + low
        inside = (row >= h * head) & (row < (h + 1) * head)
        windows.append((low, high, jnp.where(inside, queries[low:high], 0.0).astype(bf16)))
    for matching in range(2):
        for j in range(count):

            @pl.when(select[matching] == j)
            def _():
                chosen[...] = maps[j][...]

        other = chosen[...]
        keys = dot(other, weights[1]).astype(bf16)
        values = dot(other, weights[2]).T
        shifts = []
        for j in range(tiles):
            row = jnp.zeros((1, tokens), f32)
            for i in range(tiles):
                bit = mask[(matching * tiles + i) * tiles + j]
                row = jnp.where(lane_tile == i, jnp.where(bit > 0, 0.0, MASKED), row)
            shifts.append(row)
        for h in range(HEADS):
            low, high, wanted = windows[h]
            scores = dot(keys[:, low:high], wanted) * scale
            scores = jnp.concatenate(
                [scores[j * width : (j + 1) * width] + shifts[j] for j in range(tiles)], axis=0
            )
            powers = jnp.exp2(scores - jnp.max(scores, axis=0, keepdims=True))
            norm = 1.0 / jnp.sum(powers, axis=0, keepdims=True)
            part = dot(values[h * head : (h + 1) * head].astype(bf16), powers.astype(bf16)) * norm
            if matching == 0:
                totals[pl.ds(h * head, head), :] = part
            else:
                totals[pl.ds(h * head, head), :] += part
    mixture = totals[...].T.astype(bf16)
    result = (hidden[...].astype(f32) + dot(mixture, weights[3])).astype(bf16)
    second[...] = result
    blocks[...] = layer_norm(result.astype(f32)).astype(bf16)


def time_kernel(frames, *refs):
    blocks = refs[:frames]
    pieces = refs[frames]
    outs = refs[frames + 1 : 2 * frames + 1]
    weights, rows_in, attended = refs[2 * frames + 1 :]
    pixels, channels = blocks[0].shape
    head = channels // HEADS
    assemble(pieces, weights)
    for f in range(frames):
        rows_in[pl.ds(f * pixels, pixels), :] = blocks[f][...]
    rows = rows_in[...]
    ones = block_diagonal(channels, head)
    queries = dot(rows, weights[0]).astype(bf16).astype(f32)
    keys = dot(rows, weights[1]).astype(bf16).astype(f32).reshape(frames, pixels, channels)
    values = dot(rows, weights[2]).astype(bf16).astype(f32).reshape(frames, pixels, channels)
    scale = LOG2E / math.sqrt(head)
    for f in range(frames):
        one = queries[f * pixels : (f + 1) * pixels]
        products = (one[None] * keys).reshape(frames * pixels, channels)
        high = products.astype(bf16)
        low = (products - high.astype(f32)).astype(bf16)
        scores = (dot(high, ones) + dot(low, ones)) * scale
        scores = scores.reshape(frames, pixels, channels)
        powers = jnp.exp2(scores - jnp.max(scores, axis=0, keepdims=True))
        norm = 1.0 / jnp.sum(powers, axis=0, keepdims=True)
        probs = (powers * norm).astype(bf16).astype(f32)
        attended[pl.ds(f * pixels, pixels), :] = jnp.sum(probs * values, axis=0).astype(bf16)
    result = dot(attended[...], weights[3]).astype(bf16)
    for f in range(frames):
        outs[f][...] = result[f * pixels : (f + 1) * pixels]


def last_kernel(frames, *refs):
    where = refs[0]
    second = refs[1]
    blocks = refs[2 : 2 + frames]
    out = refs[2 + frames]
    pixels = blocks[0].shape[0]
    for k in range(frames):
        rows = pl.ds(pl.multiple_of(where[k] * pixels, 16), pixels)
        out[rows, :] = (second[rows, :].astype(f32) + blocks[k][...].astype(f32)).astype(bf16)


def is_power(n):
    return n & (n - 1) == 0


def partner_permutation(size, k):
    if is_power(size):
        return [(i, i ^ k) for i in range(size)]
    return [(i, (i + k) % size) for i in range(size)]


def partner(me, size, k, sign=1):
    if is_power(size):
        return me ^ k
    return (me + sign * k) % size


def gather_maps(own, axis, size):
    maps = {0: own}
    if is_power(size):
        bit = size // 2
        while bit:
            for k in list(maps):
                maps[k | bit] = lax.ppermute(maps[k], axis, partner_permutation(size, bit))
            bit //= 2
    else:
        for k in range(1, size):
            maps[k] = lax.ppermute(own, axis, partner_permutation(size, k))
    return [maps[k] for k in range(size)]


def sum_over(value, axis, size):
    if not is_power(size):
        return lax.psum(value, axis)
    bit = 1
    while bit < size:
        value = value + lax.ppermute(value, axis, partner_permutation(size, bit))
        bit *= 2
    return value


def gather_weights(three, one):
    own = jnp.concatenate([three, one[None]], axis=0)
    parts = lax.all_gather(own, "frame", axis=0)
    if own.shape[1] % 16:
        parts = parts.transpose(1, 0, 2, 3).reshape(1, 4, -1, own.shape[2])
    return parts


def per_device(
    latents,
    timesteps,
    matchings,
    tile_mask,
    conv_first,
    conv_second,
    time_proj,
    epi_in,
    epi_out,
    temp_in,
    temp_out,
):
    tokens, channels = latents.shape[2:]
    tiles = tile_mask.shape[2]
    frames = lax.axis_size("frame")
    videos = lax.axis_size("video")
    frame = lax.axis_index("frame")
    video = lax.axis_index("video")
    pixels = tokens // frames
    source = latents.reshape(tokens, channels)
    epi_parts = gather_weights(epi_in, epi_out)
    temp_parts = gather_weights(temp_in, temp_out)

    rows = time_proj.shape[0]
    half = rows * frames // 2
    index = frame * rows + jnp.arange(rows, dtype=jnp.int32)
    exponent = jnp.where(index < half, index, index - half).astype(f32)
    frequency = jnp.exp(-math.log(10000.0) * exponent / half)
    angles = timesteps.astype(f32)[:, None] * frequency[None, :]
    wave = jnp.where(index[None, :] < half, jnp.cos(angles), jnp.sin(angles))
    time_act = jax.nn.silu(wave).astype(bf16)
    bias = sum_over(dot(time_act, time_proj), "frame", frames)

    conv_scratch = [
        pltpu.VMEM((3, 3 * channels, channels), bf16),
        pltpu.VMEM((tokens + 2 * W, 3 * channels), bf16),
        pltpu.SemaphoreType.DMA,
    ]
    conv_cost = pl.CostEstimate(
        flops=2 * 9 * tokens * channels * channels,
        bytes_accessed=2 * 9 * channels * channels + 8 * tokens * channels,
        transcendentals=tokens * channels,
    )
    inner = pl.pallas_call(
        first_kernel,
        out_shape=jax.ShapeDtypeStruct((tokens, channels), f32),
        in_specs=[VMEM, ANY],
        out_specs=VMEM,
        scratch_shapes=conv_scratch,
        compiler_params=params(),
        cost_estimate=conv_cost,
        name="first_conv",
    )(source, conv_first.reshape(3, 3 * channels, channels))
    hidden, normed = pl.pallas_call(
        second_kernel,
        out_shape=[jax.ShapeDtypeStruct((tokens, channels), bf16)] * 2,
        in_specs=[VMEM, VMEM, VMEM, ANY],
        out_specs=[VMEM, VMEM],
        scratch_shapes=conv_scratch,
        compiler_params=params(),
        cost_estimate=conv_cost,
        name="second_conv",
    )(source, inner, bias, conv_second.reshape(3, 3 * channels, channels))

    maps = gather_maps(normed, "video", videos)
    targets = lax.dynamic_index_in_dim(matchings, video, 1, keepdims=False)
    if is_power(videos):
        select = video ^ targets
    else:
        select = (video - targets) % videos
    mask = lax.dynamic_index_in_dim(tile_mask, video, 1, keepdims=False).reshape(-1)
    second, blocks = pl.pallas_call(
        functools.partial(view_kernel, videos, tiles),
        out_shape=[jax.ShapeDtypeStruct((tokens, channels), bf16)] * 2,
        in_specs=[SMEM, SMEM, SMEM, VMEM] + [VMEM] * videos + [VMEM],
        out_specs=[VMEM, VMEM],
        scratch_shapes=[
            pltpu.VMEM((4, channels, channels), bf16),
            pltpu.VMEM((tokens, channels), bf16),
            pltpu.VMEM((channels, tokens), f32),
        ],
        compiler_params=params(),
        name="cross_view",
    )(select, mask, frame.reshape(1), hidden, *maps, epi_parts)

    split = blocks.reshape(frames, pixels, channels)
    received = []
    for k in range(frames):
        block = lax.dynamic_index_in_dim(split, partner(frame, frames, k), 0, keepdims=False)
        if k:
            block = lax.ppermute(block, "frame", partner_permutation(frames, k))
        received.append(block)
    outs = pl.pallas_call(
        functools.partial(time_kernel, frames),
        out_shape=[jax.ShapeDtypeStruct((pixels, channels), bf16)] * frames,
        in_specs=[VMEM] * (frames + 1),
        out_specs=[VMEM] * frames,
        scratch_shapes=[
            pltpu.VMEM((4, channels, channels), bf16),
            pltpu.VMEM((tokens, channels), bf16),
            pltpu.VMEM((tokens, channels), bf16),
        ],
        compiler_params=params(),
        name="temporal",
    )(*received, temp_parts)
    returned = [outs[0]]
    for k in range(1, frames):
        back = [(j, i) for i, j in partner_permutation(frames, k)]
        returned.append(lax.ppermute(outs[k], "frame", back))
    where = jnp.stack([partner(frame, frames, k) for k in range(frames)]).astype(jnp.int32)
    denoised = pl.pallas_call(
        functools.partial(last_kernel, frames),
        out_shape=jax.ShapeDtypeStruct((tokens, channels), bf16),
        in_specs=[SMEM] + [VMEM] * (frames + 1),
        out_specs=VMEM,
        compiler_params=params(),
        name="last",
    )(where, second, *returned)
    return denoised.reshape(1, 1, tokens, channels)


def solution(mesh):
    placed = (
        P(("groups", "video"), "frame", None, None),
        P(("groups", "video")),
        P(None, "groups"),
        P(None, "groups", None, None),
        P(),
        P(),
        P("frame", None),
        P(None, "frame", None),
        P("frame", None),
        P(None, "frame", None),
        P("frame", None),
    )
    return jax.shard_map(
        per_device,
        mesh=mesh,
        in_specs=placed,
        out_specs=P(("groups", "video"), "frame", None, None),
        check_vma=False,
    )
```

```python
import functools
import math

import jax
import jax.numpy as jnp
from jax import lax
from jax.experimental import pallas as pl
from jax.experimental.pallas import tpu as pltpu
from jax.sharding import PartitionSpec as P

HEADS = 8
NORM_GROUPS = 32
TEMB = 1280
H = 8
W = 32

EPSILON = 1e-05
MASKED = -1e30
LOG2E = 1.4426950408889634

VMEM = pl.BlockSpec(memory_space=pltpu.VMEM)
SMEM = pl.BlockSpec(memory_space=pltpu.SMEM)
ANY = pl.BlockSpec(memory_space=pl.ANY)
f32 = jnp.float32
bf16 = jnp.bfloat16


def params():
    return pltpu.CompilerParams(vmem_limit_bytes=48 * 1024 * 1024)


def dot(a, b):
    return jnp.dot(a, b, preferred_element_type=f32)


def block_diagonal(size, width):
    rows = lax.broadcasted_iota(jnp.int32, (size, 1), 0).astype(f32)
    cols = lax.broadcasted_iota(jnp.int32, (1, size), 1).astype(f32)
    rows = jnp.floor((rows + 0.5) * (1.0 / width))
    cols = jnp.floor((cols + 0.5) * (1.0 / width))
    return (rows == cols).astype(f32).astype(bf16)


def group_sum(row, ones):
    first = row.astype(bf16).astype(f32)
    second = (row - first).astype(bf16).astype(f32)
    third = row - first - second
    index = lax.broadcasted_iota(jnp.int32, (16, row.shape[1]), 0)
    stacked = jnp.where(
        index == 0, first, jnp.where(index == 1, second, jnp.where(index == 2, third, 0.0))
    )
    return jnp.sum(dot(stacked.astype(bf16), ones), axis=0, keepdims=True)


def group_norm_silu(x):
    tokens, channels = x.shape
    width = channels // NORM_GROUPS
    ones = block_diagonal(channels, width)
    inverse = 1.0 / (tokens * width)
    average = group_sum(jnp.sum(x, axis=0, keepdims=True), ones) * inverse
    centred = x - average
    spread = group_sum(jnp.sum(centred * centred, axis=0, keepdims=True), ones) * inverse
    y = centred * lax.rsqrt(spread + EPSILON)
    return y / (1.0 + jnp.exp(-y))


def layer_norm(x):
    inverse = 1.0 / x.shape[1]
    average = jnp.sum(x, axis=1, keepdims=True) * inverse
    centred = x - average
    spread = jnp.sum(centred * centred, axis=1, keepdims=True) * inverse
    return centred * lax.rsqrt(spread + EPSILON)


def convolve(y, weight, padded):
    tokens, channels = y.shape
    column = lax.broadcasted_iota(jnp.int32, (tokens, 1), 0) & (W - 1)
    before = jnp.where(column == 0, 0.0, pltpu.roll(y, 1, 0))
    after = jnp.where(column == W - 1, 0.0, pltpu.roll(y, tokens - 1, 0))
    padded[pl.ds(0, W), :] = jnp.zeros((W, 3 * channels), bf16)
    padded[pl.ds(tokens + W, W), :] = jnp.zeros((W, 3 * channels), bf16)
    padded[pl.ds(W, tokens), :] = jnp.concatenate(
        [before.astype(bf16), y.astype(bf16), after.astype(bf16)], axis=1
    )
    total = dot(padded[pl.ds(0, tokens), :], weight[0])
    total += dot(padded[pl.ds(W, tokens), :], weight[1])
    total += dot(padded[pl.ds(2 * W, tokens), :], weight[2])
    return total


def first_kernel(source, weight_hbm, inner, weight, padded, sem):
    copy = pltpu.make_async_copy(weight_hbm, weight, sem)
    copy.start()
    y = group_norm_silu(source[...].astype(f32).T)
    copy.wait()
    inner[...] = convolve(y, weight, padded)


def second_kernel(source, inner, bias, weight_hbm, hidden, normed, weight, padded, sem):
    copy = pltpu.make_async_copy(weight_hbm, weight, sem)
    copy.start()
    y = group_norm_silu(inner[...] + bias[...])
    copy.wait()
    total = source[...].astype(f32).T + convolve(y, weight, padded)
    rounded = total.astype(bf16)
    hidden[...] = rounded
    normed[...] = layer_norm(rounded.astype(f32)).astype(bf16)


def assemble(where, own, received, swapped, whole, first, kinds):
    rows = own.shape[1]
    start = 0 if first == 0 else 2
    for kind in range(kinds):
        whole[kind, pl.ds(pl.multiple_of(where[0] * rows, 16), rows), :] = own[first + kind]
    for k in range(1, len(received) + 1):
        place = pl.ds(pl.multiple_of(where[k] * rows, 16), rows)
        for j in range(2):
            mine = where[len(received) + 1] * 2 + j
            whole[mine, place, :] = received[k - 1][start + j]
            whole[2 - mine + 2 * j, place, :] = swapped[k - 1][start + j]


def query_kernel(count, where, normed, own, *refs):
    received, swapped = refs[:count], refs[count : 2 * count]
    queries, epi, temp = refs[2 * count :]
    assemble(where, own, received, swapped, epi, 0, 4)
    assemble(where, own, received, swapped, temp, 4, 4)
    queries[...] = dot(normed[...], epi[0]).astype(bf16).astype(f32).T


def view_kernel(count, tiles, *refs):
    select, mask, hidden, query_ref, weights = refs[:5]
    maps = refs[5 : 5 + count]
    second, blocks, chosen, totals = refs[5 + count :]
    tokens, channels = hidden.shape
    head = channels // HEADS
    width = tokens // tiles
    scale = LOG2E / math.sqrt(head)
    queries = query_ref[...]
    lane_tile = lax.broadcasted_iota(jnp.int32, (1, tokens), 1) // width
    windows = []
    for h in range(HEADS):
        low = h * head // 128 * 128
        high = min(channels, -(-(h + 1) * head // 128) * 128)
        row = lax.broadcasted_iota(jnp.int32, (high - low, 1), 0) + low
        inside = (row >= h * head) & (row < (h + 1) * head)
        windows.append((low, high, jnp.where(inside, queries[low:high], 0.0).astype(bf16)))
    for matching in range(2):
        for j in range(count):

            @pl.when(select[matching] == j)
            def _():
                chosen[...] = maps[j][...]

        other = chosen[...]
        keys = dot(other, weights[1]).astype(bf16)
        values = dot(other, weights[2]).T
        shifts = []
        for j in range(tiles):
            row = jnp.zeros((1, tokens), f32)
            for i in range(tiles):
                bit = mask[(matching * tiles + i) * tiles + j]
                row = jnp.where(lane_tile == i, jnp.where(bit > 0, 0.0, MASKED), row)
            shifts.append(row)
        for h in range(HEADS):
            low, high, wanted = windows[h]
            scores = dot(keys[:, low:high], wanted) * scale
            scores = jnp.concatenate(
                [scores[j * width : (j + 1) * width] + shifts[j] for j in range(tiles)], axis=0
            )
            powers = jnp.exp2(scores - jnp.max(scores, axis=0, keepdims=True))
            norm = 1.0 / jnp.sum(powers, axis=0, keepdims=True)
            part = dot(values[h * head : (h + 1) * head].astype(bf16), powers.astype(bf16)) * norm
            if matching == 0:
                totals[pl.ds(h * head, head), :] = part
            else:
                totals[pl.ds(h * head, head), :] += part
    mixture = totals[...].T.astype(bf16)
    result = (hidden[...].astype(f32) + dot(mixture, weights[3])).astype(bf16)
    second[...] = result
    blocks[...] = layer_norm(result.astype(f32)).astype(bf16)


def time_kernel(frames, *refs):
    blocks = refs[:frames]
    weights = refs[frames]
    outs = refs[frames + 1 : 2 * frames + 1]
    rows_in, attended = refs[2 * frames + 1 :]
    pixels, channels = blocks[0].shape
    head = channels // HEADS
    for f in range(frames):
        rows_in[pl.ds(f * pixels, pixels), :] = blocks[f][...]
    rows = rows_in[...]
    ones = block_diagonal(channels, head)
    queries = dot(rows, weights[0]).astype(bf16).astype(f32)
    keys = dot(rows, weights[1]).astype(bf16).astype(f32).reshape(frames, pixels, channels)
    values = dot(rows, weights[2]).astype(bf16).astype(f32).reshape(frames, pixels, channels)
    scale = LOG2E / math.sqrt(head)
    for f in range(frames):
        one = queries[f * pixels : (f + 1) * pixels]
        products = (one[None] * keys).reshape(frames * pixels, channels)
        high = products.astype(bf16)
        low = (products - high.astype(f32)).astype(bf16)
        scores = (dot(high, ones) + dot(low, ones)) * scale
        scores = scores.reshape(frames, pixels, channels)
        powers = jnp.exp2(scores - jnp.max(scores, axis=0, keepdims=True))
        norm = 1.0 / jnp.sum(powers, axis=0, keepdims=True)
        probs = (powers * norm).astype(bf16).astype(f32)
        attended[pl.ds(f * pixels, pixels), :] = jnp.sum(probs * values, axis=0).astype(bf16)
    result = dot(attended[...], weights[3]).astype(bf16)
    for f in range(frames):
        outs[f][...] = result[f * pixels : (f + 1) * pixels]


def last_kernel(frames, *refs):
    where = refs[0]
    second = refs[1]
    blocks = refs[2 : 2 + frames]
    out, total = refs[2 + frames :]
    pixels = blocks[0].shape[0]
    for k in range(frames):
        rows = pl.ds(pl.multiple_of(where[k] * pixels, 16), pixels)
        total[rows, :] = second[rows, :].astype(f32) + blocks[k][...].astype(f32)
    out[...] = total[...].T.astype(bf16)


def is_power(n):
    return n & (n - 1) == 0


def partner_permutation(size, k):
    if is_power(size):
        return [(i, i ^ k) for i in range(size)]
    return [(i, (i + k) % size) for i in range(size)]


def partner(me, size, k, sign=1):
    if is_power(size):
        return me ^ k
    return (me + sign * k) % size


def gather_maps(own, axis, size):
    maps = {0: own}
    if is_power(size):
        bit = size // 2
        while bit:
            for k in list(maps):
                maps[k | bit] = lax.ppermute(maps[k], axis, partner_permutation(size, bit))
            bit //= 2
    else:
        for k in range(1, size):
            maps[k] = lax.ppermute(own, axis, partner_permutation(size, k))
    return [maps[k] for k in range(size)]


def sum_over(value, axis, size):
    if not is_power(size):
        return lax.psum(value, axis)
    bit = 1
    while bit < size:
        value = value + lax.ppermute(value, axis, partner_permutation(size, bit))
        bit *= 2
    return value


def gather_weights(parts, frames, videos, video):
    kinds, rows, channels = parts.shape
    halves = parts.reshape(2, 2, 2, rows, channels)
    mine = lax.dynamic_index_in_dim(halves, video % 2, 1, keepdims=False)
    mine = mine.reshape(4, rows, channels)
    received = [
        lax.ppermute(mine, "frame", partner_permutation(frames, k)) for k in range(1, frames)
    ]
    swapped = [lax.ppermute(part, "video", partner_permutation(videos, 1)) for part in received]
    return received, swapped


def per_device(
    latents,
    timesteps,
    matchings,
    tile_mask,
    conv_first,
    conv_second,
    time_proj,
    epi_in,
    epi_out,
    temp_in,
    temp_out,
):
    tokens, channels = latents.shape[2:]
    tiles = tile_mask.shape[2]
    frames = lax.axis_size("frame")
    videos = lax.axis_size("video")
    frame = lax.axis_index("frame")
    video = lax.axis_index("video")
    pixels = tokens // frames
    source = latents.reshape(tokens, channels).T
    where = jnp.stack([partner(frame, frames, k) for k in range(frames)]).astype(jnp.int32)
    parts = jnp.concatenate([epi_in, epi_out[None], temp_in, temp_out[None]], axis=0)
    if is_power(frames) and videos % 2 == 0 and is_power(videos) and parts.shape[1] % 16 == 0:
        received, swapped = gather_weights(parts, frames, videos, video)
        places = jnp.concatenate([where, (video % 2).astype(jnp.int32)[None]])
    else:
        parts = lax.all_gather(parts, "frame", axis=1, tiled=True)
        received, swapped = [], []
        places = jnp.zeros((2,), jnp.int32)

    rows = time_proj.shape[0]
    half = rows * frames // 2
    index = frame * rows + jnp.arange(rows, dtype=jnp.int32)
    exponent = jnp.where(index < half, index, index - half).astype(f32)
    frequency = jnp.exp(-math.log(10000.0) * exponent / half)
    angles = timesteps.astype(f32)[:, None] * frequency[None, :]
    wave = jnp.where(index[None, :] < half, jnp.cos(angles), jnp.sin(angles))
    time_act = jax.nn.silu(wave).astype(bf16)
    bias = sum_over(dot(time_act, time_proj), "frame", frames)

    conv_scratch = [
        pltpu.VMEM((3, 3 * channels, channels), bf16),
        pltpu.VMEM((tokens + 2 * W, 3 * channels), bf16),
        pltpu.SemaphoreType.DMA,
    ]
    conv_cost = pl.CostEstimate(
        flops=2 * 9 * tokens * channels * channels,
        bytes_accessed=2 * 9 * channels * channels + 8 * tokens * channels,
        transcendentals=tokens * channels,
    )
    inner = pl.pallas_call(
        first_kernel,
        out_shape=jax.ShapeDtypeStruct((tokens, channels), f32),
        in_specs=[VMEM, ANY],
        out_specs=VMEM,
        scratch_shapes=conv_scratch,
        compiler_params=params(),
        cost_estimate=conv_cost,
        name="first_conv",
    )(source, conv_first.reshape(3, 3 * channels, channels))
    hidden, normed = pl.pallas_call(
        second_kernel,
        out_shape=[jax.ShapeDtypeStruct((tokens, channels), bf16)] * 2,
        in_specs=[VMEM, VMEM, VMEM, ANY],
        out_specs=[VMEM, VMEM],
        scratch_shapes=conv_scratch,
        compiler_params=params(),
        cost_estimate=conv_cost,
        name="second_conv",
    )(source, inner, bias, conv_second.reshape(3, 3 * channels, channels))

    maps = gather_maps(normed, "video", videos)
    targets = lax.dynamic_index_in_dim(matchings, video, 1, keepdims=False)
    if is_power(videos):
        select = video ^ targets
    else:
        select = (video - targets) % videos
    mask = lax.dynamic_index_in_dim(tile_mask, video, 1, keepdims=False).reshape(-1)
    square = (4, channels, channels)
    queries, epi, temp = pl.pallas_call(
        functools.partial(query_kernel, len(received)),
        out_shape=[
            jax.ShapeDtypeStruct((channels, tokens), f32),
            jax.ShapeDtypeStruct(square, bf16),
            jax.ShapeDtypeStruct(square, bf16),
        ],
        in_specs=[SMEM, VMEM, VMEM] + [VMEM] * (2 * len(received)),
        out_specs=[VMEM] * 3,
        compiler_params=params(),
        name="query",
    )(places, normed, parts, *received, *swapped)
    second, blocks = pl.pallas_call(
        functools.partial(view_kernel, videos, tiles),
        out_shape=[jax.ShapeDtypeStruct((tokens, channels), bf16)] * 2,
        in_specs=[SMEM, SMEM, VMEM, VMEM, VMEM] + [VMEM] * videos,
        out_specs=[VMEM, VMEM],
        scratch_shapes=[
            pltpu.VMEM((tokens, channels), bf16),
            pltpu.VMEM((channels, tokens), f32),
        ],
        compiler_params=params(),
        name="cross_view",
    )(select, mask, hidden, queries, epi, *maps)

    split = blocks.reshape(frames, pixels, channels)
    regrouped = []
    for k in range(frames):
        block = lax.dynamic_index_in_dim(split, partner(frame, frames, k), 0, keepdims=False)
        if k:
            block = lax.ppermute(block, "frame", partner_permutation(frames, k))
        regrouped.append(block)
    outs = pl.pallas_call(
        functools.partial(time_kernel, frames),
        out_shape=[jax.ShapeDtypeStruct((pixels, channels), bf16)] * frames,
        in_specs=[VMEM] * (frames + 1),
        out_specs=[VMEM] * frames,
        scratch_shapes=[
            pltpu.VMEM((tokens, channels), bf16),
            pltpu.VMEM((tokens, channels), bf16),
        ],
        compiler_params=params(),
        name="temporal",
    )(*regrouped, temp)
    returned = [outs[0]]
    for k in range(1, frames):
        back = [(j, i) for i, j in partner_permutation(frames, k)]
        returned.append(lax.ppermute(outs[k], "frame", back))
    denoised = pl.pallas_call(
        functools.partial(last_kernel, frames),
        out_shape=jax.ShapeDtypeStruct((channels, tokens), bf16),
        in_specs=[SMEM] + [VMEM] * (frames + 1),
        out_specs=VMEM,
        scratch_shapes=[pltpu.VMEM((tokens, channels), f32)],
        compiler_params=params(),
        name="last",
    )(where, second, *returned)
    return denoised.T.reshape(1, 1, tokens, channels)


def solution(mesh):
    placed = (
        P(("groups", "video"), "frame", None, None),
        P(("groups", "video")),
        P(None, "groups"),
        P(None, "groups", None, None),
        P(),
        P(),
        P("frame", None),
        P(None, "frame", None),
        P("frame", None),
        P(None, "frame", None),
        P("frame", None),
    )
    return jax.shard_map(
        per_device,
        mesh=mesh,
        in_specs=placed,
        out_specs=P(("groups", "video"), "frame", None, None),
        check_vma=False,
    )
```

```python
import functools
import math

import jax
import jax.numpy as jnp
from jax import lax
from jax.experimental import pallas as pl
from jax.experimental.pallas import tpu as pltpu
from jax.sharding import PartitionSpec as P

HEADS = 8
NORM_GROUPS = 32
TEMB = 1280
H = 8
W = 32

EPSILON = 1e-05
MASKED = -1e30
LOG2E = 1.4426950408889634

VMEM = pl.BlockSpec(memory_space=pltpu.VMEM)
SMEM = pl.BlockSpec(memory_space=pltpu.SMEM)
f32 = jnp.float32
bf16 = jnp.bfloat16


def params():
    return pltpu.CompilerParams(vmem_limit_bytes=16 * 1024 * 1024)


def dot(a, b):
    return jnp.dot(a, b, preferred_element_type=f32)


def block_diagonal(size, width):
    rows = lax.broadcasted_iota(jnp.int32, (size, 1), 0).astype(f32)
    cols = lax.broadcasted_iota(jnp.int32, (1, size), 1).astype(f32)
    rows = jnp.floor((rows + 0.5) * (1.0 / width))
    cols = jnp.floor((cols + 0.5) * (1.0 / width))
    return (rows == cols).astype(f32).astype(bf16)


def group_sum(row, ones):
    first = row.astype(bf16).astype(f32)
    second = (row - first).astype(bf16).astype(f32)
    third = row - first - second
    index = lax.broadcasted_iota(jnp.int32, (16, row.shape[1]), 0)
    stacked = jnp.where(
        index == 0, first, jnp.where(index == 1, second, jnp.where(index == 2, third, 0.0))
    )
    return jnp.sum(dot(stacked.astype(bf16), ones), axis=0, keepdims=True)


def group_norm_silu(x):
    tokens, channels = x.shape
    width = channels // NORM_GROUPS
    ones = block_diagonal(channels, width)
    inverse = 1.0 / (tokens * width)
    average = group_sum(jnp.sum(x, axis=0, keepdims=True), ones) * inverse
    centred = x - average
    spread = group_sum(jnp.sum(centred * centred, axis=0, keepdims=True), ones) * inverse
    y = centred * lax.rsqrt(spread + EPSILON)
    return y / (1.0 + jnp.exp(-y))


def layer_norm(x):
    inverse = 1.0 / x.shape[1]
    average = jnp.sum(x, axis=1, keepdims=True) * inverse
    centred = x - average
    spread = jnp.sum(centred * centred, axis=1, keepdims=True) * inverse
    return centred * lax.rsqrt(spread + EPSILON)


def convolve(y, weight, padded):
    tokens, channels = y.shape
    column = lax.broadcasted_iota(jnp.int32, (tokens, 1), 0) & (W - 1)
    before = jnp.where(column == 0, 0.0, pltpu.roll(y, 1, 0))
    after = jnp.where(column == W - 1, 0.0, pltpu.roll(y, tokens - 1, 0))
    padded[pl.ds(0, W), :] = jnp.zeros((W, 3 * channels), bf16)
    padded[pl.ds(tokens + W, W), :] = jnp.zeros((W, 3 * channels), bf16)
    padded[pl.ds(W, tokens), :] = jnp.concatenate(
        [before.astype(bf16), y.astype(bf16), after.astype(bf16)], axis=1
    )
    total = None
    for k in range(3):
        part = dot(padded[pl.ds(k * W, tokens), :], weight[k])
        total = part if total is None else total + part
    return total


def share_kernel(act, proj, share):
    share[...] = dot(act[...], proj[...])


def first_kernel(source, weight, inner, padded):
    inner[...] = convolve(group_norm_silu(source[...].astype(f32).T), weight, padded)


def second_kernel(source, inner, bias, weight, hidden, normed, padded):
    y = group_norm_silu(inner[...] + bias[...])
    total = source[...].astype(f32).T + convolve(y, weight, padded)
    rounded = total.astype(bf16)
    hidden[...] = rounded
    normed[...] = layer_norm(rounded.astype(f32)).astype(bf16)


def assemble(where, own, received, swapped, whole, first, kinds):
    rows = own.shape[1]
    start = 0 if first == 0 else 2
    for kind in range(kinds):
        whole[kind, pl.ds(pl.multiple_of(where[0] * rows, 16), rows), :] = own[first + kind]
    for k in range(1, len(received) + 1):
        place = pl.ds(pl.multiple_of(where[k] * rows, 16), rows)
        for j in range(2):
            mine = where[len(received) + 1] * 2 + j
            whole[mine, place, :] = received[k - 1][start + j]
            whole[2 - mine + 2 * j, place, :] = swapped[k - 1][start + j]


def query_kernel(count, where, normed, own, *refs):
    received, swapped = refs[:count], refs[count : 2 * count]
    queries, epi, temp = refs[2 * count :]
    assemble(where, own, received, swapped, epi, 0, 4)
    assemble(where, own, received, swapped, temp, 4, 4)
    queries[...] = dot(normed[...], epi[0]).astype(bf16).astype(f32).T


def view_kernel(count, tiles, *refs):
    select, mask, hidden, query_ref, weights = refs[:5]
    maps = refs[5 : 5 + count]
    second, blocks, chosen, totals = refs[5 + count :]
    tokens, channels = hidden.shape
    head = channels // HEADS
    width = tokens // tiles
    scale = LOG2E / math.sqrt(head)
    queries = query_ref[...]
    lane_tile = lax.broadcasted_iota(jnp.int32, (1, tokens), 1) // width
    windows = []
    for h in range(HEADS):
        low = h * head // 128 * 128
        high = min(channels, -(-(h + 1) * head // 128) * 128)
        row = lax.broadcasted_iota(jnp.int32, (high - low, 1), 0) + low
        inside = (row >= h * head) & (row < (h + 1) * head)
        windows.append((low, high, jnp.where(inside, queries[low:high], 0.0).astype(bf16)))
    for matching in range(2):
        for j in range(count):

            @pl.when(select[matching] == j)
            def _():
                chosen[...] = maps[j][...]

        other = chosen[...]
        keys = dot(other, weights[1]).astype(bf16)
        values = dot(other, weights[2]).T
        shifts = []
        for j in range(tiles):
            row = jnp.zeros((1, tokens), f32)
            for i in range(tiles):
                bit = mask[(matching * tiles + i) * tiles + j]
                row = jnp.where(lane_tile == i, jnp.where(bit > 0, 0.0, MASKED), row)
            shifts.append(row)
        for h in range(HEADS):
            low, high, wanted = windows[h]
            scores = dot(keys[:, low:high], wanted) * scale
            scores = jnp.concatenate(
                [scores[j * width : (j + 1) * width] + shifts[j] for j in range(tiles)], axis=0
            )
            powers = jnp.exp2(scores - jnp.max(scores, axis=0, keepdims=True))
            norm = 1.0 / jnp.sum(powers, axis=0, keepdims=True)
            part = dot(values[h * head : (h + 1) * head].astype(bf16), powers.astype(bf16)) * norm
            if matching == 0:
                totals[pl.ds(h * head, head), :] = part
            else:
                totals[pl.ds(h * head, head), :] += part
    mixture = totals[...].T.astype(bf16)
    result = (hidden[...].astype(f32) + dot(mixture, weights[3])).astype(bf16)
    second[...] = result
    blocks[...] = layer_norm(result.astype(f32)).astype(bf16)


def frame_part(queries, rows, weights):
    channels = rows.shape[1]
    head = channels // HEADS
    ones = block_diagonal(channels, head)
    keys = dot(rows, weights[1]).astype(bf16).astype(f32)
    values = dot(rows, weights[2]).astype(bf16)
    products = queries * keys
    high = products.astype(bf16)
    low = (products - high.astype(f32)).astype(bf16)
    return (dot(high, ones) + dot(low, ones)) * (LOG2E / math.sqrt(head)), values


def own_frame_kernel(rows, weights, queries, scores, values):
    queries[...] = dot(rows[...], weights[0]).astype(bf16)
    scores[...], values[...] = frame_part(queries[...].astype(f32), rows[...], weights)


def frame_kernel(queries, rows, weights, scores, values):
    scores[...], values[...] = frame_part(queries[...].astype(f32), rows[...], weights)


def last_kernel(frames, *refs):
    second, queries, rows, weights = refs[:4]
    scores = refs[4 : 3 + frames]
    values = refs[3 + frames : 2 + 2 * frames]
    out = refs[-1]
    last_scores, last_values = frame_part(queries[...].astype(f32), rows[...], weights)
    every = [ref[...] for ref in scores] + [last_scores]
    most = functools.reduce(jnp.maximum, every)
    powers = [jnp.exp2(one - most) for one in every]
    norm = 1.0 / functools.reduce(jnp.add, powers)
    total = (powers[-1] * norm).astype(bf16).astype(f32) * last_values.astype(f32)
    for power, value in zip(powers, values):
        total += (power * norm).astype(bf16).astype(f32) * value[...].astype(f32)
    result = second[...].astype(f32) + dot(total.astype(bf16), weights[3])
    out[...] = result.T.astype(bf16)


def is_power(n):
    return n & (n - 1) == 0


def partner_permutation(size, k):
    if is_power(size):
        return [(i, i ^ k) for i in range(size)]
    return [(i, (i + k) % size) for i in range(size)]


def partner(me, size, k, sign=1):
    if is_power(size):
        return me ^ k
    return (me + sign * k) % size


def gather_maps(own, axis, size):
    maps = {0: own}
    if is_power(size):
        bit = size // 2
        while bit:
            for k in list(maps):
                maps[k | bit] = lax.ppermute(maps[k], axis, partner_permutation(size, bit))
            bit //= 2
    else:
        for k in range(1, size):
            maps[k] = lax.ppermute(own, axis, partner_permutation(size, k))
    return [maps[k] for k in range(size)]


def sum_over(value, beside, later, axis, size):
    if not is_power(size):
        return lax.psum(value, axis), beside, later
    bit = 1
    while bit < size:
        value = value + lax.ppermute(value, axis, partner_permutation(size, bit))
        if bit == 1:
            value, beside = lax.optimization_barrier((value, beside))
        bit *= 2
    value, later = lax.optimization_barrier((value, later))
    return value, beside, later


def gather_weights(parts, frames, videos, video):
    kinds, rows, channels = parts.shape
    halves = parts.reshape(2, 2, 2, rows, channels)
    mine = lax.dynamic_index_in_dim(halves, video % 2, 1, keepdims=False)
    mine = mine.reshape(4, rows, channels)
    received = [
        lax.ppermute(mine, "frame", partner_permutation(frames, k)) for k in range(1, frames)
    ]
    swapped = [lax.ppermute(part, "video", partner_permutation(videos, 1)) for part in received]
    return received, swapped


def per_device(
    latents,
    timesteps,
    matchings,
    tile_mask,
    conv_first,
    conv_second,
    time_proj,
    epi_in,
    epi_out,
    temp_in,
    temp_out,
):
    tokens, channels = latents.shape[2:]
    tiles = tile_mask.shape[2]
    frames = lax.axis_size("frame")
    videos = lax.axis_size("video")
    frame = lax.axis_index("frame")
    video = lax.axis_index("video")
    pixels = tokens // frames
    source = latents.reshape(tokens, channels).T
    where = jnp.stack([partner(frame, frames, k) for k in range(frames)]).astype(jnp.int32)

    rows = time_proj.shape[0]
    half = rows * frames // 2
    index = frame * rows + jnp.arange(rows, dtype=jnp.int32)
    exponent = jnp.where(index < half, index, index - half).astype(f32)
    frequency = jnp.exp(-math.log(10000.0) * exponent / half)
    angles = timesteps.astype(f32)[:, None] * frequency[None, :]
    wave = jnp.where(index[None, :] < half, jnp.cos(angles), jnp.sin(angles))
    time_act = jax.nn.silu(wave).astype(bf16)
    share = pl.pallas_call(
        share_kernel,
        out_shape=jax.ShapeDtypeStruct((1, channels), f32),
        in_specs=[VMEM, VMEM],
        out_specs=VMEM,
        compiler_params=params(),
        cost_estimate=pl.CostEstimate(flops=10**10, bytes_accessed=1 << 20, transcendentals=0),
        name="time_share",
    )(time_act, time_proj)
    parts = jnp.concatenate([epi_in, epi_out[None], temp_in, temp_out[None]], axis=0)
    bias, source, parts = sum_over(share, source, parts, "frame", frames)

    conv_scratch = [
        pltpu.VMEM((tokens + 2 * W, 3 * channels), bf16),
    ]
    conv_cost = pl.CostEstimate(
        flops=2 * 9 * tokens * channels * channels,
        bytes_accessed=2 * 9 * channels * channels + 8 * tokens * channels,
        transcendentals=tokens * channels,
    )
    inner = pl.pallas_call(
        first_kernel,
        out_shape=jax.ShapeDtypeStruct((tokens, channels), f32),
        in_specs=[VMEM, VMEM],
        out_specs=VMEM,
        scratch_shapes=conv_scratch,
        compiler_params=params(),
        cost_estimate=conv_cost,
        name="first_conv",
    )(source, conv_first.reshape(3, 3 * channels, channels))
    if is_power(frames) and videos % 2 == 0 and is_power(videos) and parts.shape[1] % 16 == 0:
        received, swapped = gather_weights(parts, frames, videos, video)
        places = jnp.concatenate([where, (video % 2).astype(jnp.int32)[None]])
    else:
        parts = lax.all_gather(parts, "frame", axis=1, tiled=True)
        received, swapped = [], []
        places = jnp.zeros((2,), jnp.int32)
    hidden, normed = pl.pallas_call(
        second_kernel,
        out_shape=[jax.ShapeDtypeStruct((tokens, channels), bf16)] * 2,
        in_specs=[VMEM, VMEM, VMEM, VMEM],
        out_specs=[VMEM, VMEM],
        scratch_shapes=conv_scratch,
        compiler_params=params(),
        cost_estimate=conv_cost,
        name="second_conv",
    )(source, inner, bias, conv_second.reshape(3, 3 * channels, channels))

    maps = gather_maps(normed, "video", videos)
    targets = lax.dynamic_index_in_dim(matchings, video, 1, keepdims=False)
    if is_power(videos):
        select = video ^ targets
    else:
        select = (video - targets) % videos
    mask = lax.dynamic_index_in_dim(tile_mask, video, 1, keepdims=False).reshape(-1)
    square = (4, channels, channels)
    queries, epi, temp = pl.pallas_call(
        functools.partial(query_kernel, len(received)),
        out_shape=[
            jax.ShapeDtypeStruct((channels, tokens), f32),
            jax.ShapeDtypeStruct(square, bf16),
            jax.ShapeDtypeStruct(square, bf16),
        ],
        in_specs=[SMEM, VMEM, VMEM] + [VMEM] * (2 * len(received)),
        out_specs=[VMEM] * 3,
        compiler_params=params(),
        name="query",
    )(places, normed, parts, *received, *swapped)
    second, blocks = pl.pallas_call(
        functools.partial(view_kernel, videos, tiles),
        out_shape=[jax.ShapeDtypeStruct((tokens, channels), bf16)] * 2,
        in_specs=[SMEM, SMEM, VMEM, VMEM, VMEM] + [VMEM] * videos,
        out_specs=[VMEM, VMEM],
        scratch_shapes=[
            pltpu.VMEM((tokens, channels), bf16),
            pltpu.VMEM((channels, tokens), f32),
        ],
        compiler_params=params(),
        name="cross_view",
    )(select, mask, hidden, queries, epi, *maps)

    arrived = {}
    for k in reversed(range(1, frames)):
        arrived[k] = lax.ppermute(blocks, "frame", partner_permutation(frames, k))
    score_shape = jax.ShapeDtypeStruct((tokens, channels), f32)
    value_shape = jax.ShapeDtypeStruct((tokens, channels), bf16)
    frame_cost = pl.CostEstimate(
        flops=8 * tokens * channels * channels,
        bytes_accessed=8 * channels * channels + 8 * tokens * channels,
        transcendentals=0,
    )
    frame_queries, *first = pl.pallas_call(
        own_frame_kernel,
        out_shape=[value_shape, score_shape, value_shape],
        in_specs=[VMEM] * 2,
        out_specs=[VMEM] * 3,
        compiler_params=params(),
        cost_estimate=frame_cost,
        name="own_frame",
    )(blocks, temp)
    scores, values = [first[0]], [first[1]]
    order = [1] + list(range(frames - 1, 1, -1)) if frames > 1 else []
    for k in order[:-1]:
        one = pl.pallas_call(
            frame_kernel,
            out_shape=[score_shape, value_shape],
            in_specs=[VMEM] * 3,
            out_specs=[VMEM] * 2,
            compiler_params=params(),
            cost_estimate=frame_cost,
            name="other_frame",
        )(frame_queries, arrived[k], temp)
        scores.append(one[0])
        values.append(one[1])
    denoised = pl.pallas_call(
        functools.partial(last_kernel, frames),
        out_shape=jax.ShapeDtypeStruct((channels, tokens), bf16),
        in_specs=[VMEM] * (2 + 2 * frames),
        out_specs=VMEM,
        compiler_params=params(),
        name="last",
    )(second, frame_queries, arrived[order[-1]], temp, *scores, *values)
    return denoised.T.reshape(1, 1, tokens, channels)


def solution(mesh):
    placed = (
        P(("groups", "video"), "frame", None, None),
        P(("groups", "video")),
        P(None, "groups"),
        P(None, "groups", None, None),
        P(),
        P(),
        P("frame", None),
        P(None, "frame", None),
        P("frame", None),
        P(None, "frame", None),
        P("frame", None),
    )
    return jax.shard_map(
        per_device,
        mesh=mesh,
        in_specs=placed,
        out_specs=P(("groups", "video"), "frame", None, None),
        check_vma=False,
    )
```

```python
import functools
import math

import jax
import jax.numpy as jnp
from jax import lax
from jax.experimental import pallas as pl
from jax.experimental.pallas import tpu as pltpu
from jax.sharding import PartitionSpec as P

HEADS = 8
NORM_GROUPS = 32
TEMB = 1280
H = 8
W = 32

EPSILON = 1e-05
MASKED = -1e30
LOG2E = 1.4426950408889634

VMEM = pl.BlockSpec(memory_space=pltpu.VMEM)
SMEM = pl.BlockSpec(memory_space=pltpu.SMEM)
f32 = jnp.float32
bf16 = jnp.bfloat16


def params():
    return pltpu.CompilerParams(vmem_limit_bytes=16 * 1024 * 1024)


def dot(a, b):
    return jnp.dot(a, b, preferred_element_type=f32)


def block_diagonal(size, width):
    rows = lax.broadcasted_iota(jnp.int32, (size, 1), 0).astype(f32)
    cols = lax.broadcasted_iota(jnp.int32, (1, size), 1).astype(f32)
    rows = jnp.floor((rows + 0.5) * (1.0 / width))
    cols = jnp.floor((cols + 0.5) * (1.0 / width))
    return (rows == cols).astype(f32).astype(bf16)


def group_sum(row, ones):
    first = row.astype(bf16).astype(f32)
    second = (row - first).astype(bf16).astype(f32)
    third = row - first - second
    index = lax.broadcasted_iota(jnp.int32, (16, row.shape[1]), 0)
    stacked = jnp.where(
        index == 0, first, jnp.where(index == 1, second, jnp.where(index == 2, third, 0.0))
    )
    return jnp.sum(dot(stacked.astype(bf16), ones), axis=0, keepdims=True)


def group_norm_silu(x):
    tokens, channels = x.shape
    width = channels // NORM_GROUPS
    ones = block_diagonal(channels, width)
    inverse = 1.0 / (tokens * width)
    average = group_sum(jnp.sum(x, axis=0, keepdims=True), ones) * inverse
    centred = x - average
    spread = group_sum(jnp.sum(centred * centred, axis=0, keepdims=True), ones) * inverse
    y = centred * lax.rsqrt(spread + EPSILON)
    return y / (1.0 + jnp.exp(-y))


def layer_norm(x):
    inverse = 1.0 / x.shape[1]
    average = jnp.sum(x, axis=1, keepdims=True) * inverse
    centred = x - average
    spread = jnp.sum(centred * centred, axis=1, keepdims=True) * inverse
    return centred * lax.rsqrt(spread + EPSILON)


def convolve(y, weight, padded):
    tokens, channels = y.shape
    column = lax.broadcasted_iota(jnp.int32, (tokens, 1), 0) & (W - 1)
    before = jnp.where(column == 0, 0.0, pltpu.roll(y, 1, 0))
    after = jnp.where(column == W - 1, 0.0, pltpu.roll(y, tokens - 1, 0))
    padded[pl.ds(0, W), :] = jnp.zeros((W, 3 * channels), bf16)
    padded[pl.ds(tokens + W, W), :] = jnp.zeros((W, 3 * channels), bf16)
    padded[pl.ds(W, tokens), :] = jnp.concatenate(
        [before.astype(bf16), y.astype(bf16), after.astype(bf16)], axis=1
    )
    total = None
    for k in range(3):
        part = dot(padded[pl.ds(k * W, tokens), :], weight[k])
        total = part if total is None else total + part
    return total


def share_kernel(act, proj, share):
    share[...] = dot(act[...], proj[...])


def first_kernel(source, weight, inner, padded):
    inner[...] = convolve(group_norm_silu(source[...].astype(f32).T), weight, padded)


def second_kernel(source, inner, bias, weight, hidden, normed, padded):
    y = group_norm_silu(inner[...] + bias[...])
    total = source[...].astype(f32).T + convolve(y, weight, padded)
    rounded = total.astype(bf16)
    hidden[...] = rounded
    normed[...] = layer_norm(rounded.astype(f32)).astype(bf16)


def assemble(where, parts, whole):
    own, count = parts[0], len(parts) // 2
    rows = own.shape[1]
    for kind in range(4):
        whole[kind, pl.ds(pl.multiple_of(where[0] * rows, 16), rows), :] = own[kind]
    for k in range(1, count + 1):
        place = pl.ds(pl.multiple_of(where[k] * rows, 16), rows)
        for j in range(2):
            mine = where[count + 1] * 2 + j
            whole[mine, place, :] = parts[k][j]
            whole[2 - mine + 2 * j, place, :] = parts[count + k][j]


def query_kernel(where, normed, *refs):
    parts = refs[:-2]
    queries, epi = refs[-2:]
    assemble(where, parts, epi)
    queries[...] = dot(normed[...], epi[0]).astype(bf16).astype(f32).T


def view_kernel(count, tiles, *refs):
    select, mask, hidden, query_ref, weights = refs[:5]
    maps = refs[5 : 5 + count]
    second, blocks, chosen, totals = refs[5 + count :]
    tokens, channels = hidden.shape
    head = channels // HEADS
    width = tokens // tiles
    scale = LOG2E / math.sqrt(head)
    queries = query_ref[...]
    lane_tile = lax.broadcasted_iota(jnp.int32, (1, tokens), 1) // width
    windows = []
    for h in range(HEADS):
        low = h * head // 128 * 128
        high = min(channels, -(-(h + 1) * head // 128) * 128)
        row = lax.broadcasted_iota(jnp.int32, (high - low, 1), 0) + low
        inside = (row >= h * head) & (row < (h + 1) * head)
        windows.append((low, high, jnp.where(inside, queries[low:high], 0.0).astype(bf16)))
    for matching in range(2):
        for j in range(count):

            @pl.when(select[matching] == j)
            def _():
                chosen[...] = maps[j][...]

        other = chosen[...]
        keys = dot(other, weights[1]).astype(bf16)
        values = dot(other, weights[2]).T
        shifts = []
        for j in range(tiles):
            row = jnp.zeros((1, tokens), f32)
            for i in range(tiles):
                bit = mask[(matching * tiles + i) * tiles + j]
                row = jnp.where(lane_tile == i, jnp.where(bit > 0, 0.0, MASKED), row)
            shifts.append(row)
        for h in range(HEADS):
            low, high, wanted = windows[h]
            scores = dot(keys[:, low:high], wanted) * scale
            scores = jnp.concatenate(
                [scores[j * width : (j + 1) * width] + shifts[j] for j in range(tiles)], axis=0
            )
            powers = jnp.exp2(scores - jnp.max(scores, axis=0, keepdims=True))
            norm = 1.0 / jnp.sum(powers, axis=0, keepdims=True)
            part = dot(values[h * head : (h + 1) * head].astype(bf16), powers.astype(bf16)) * norm
            if matching == 0:
                totals[pl.ds(h * head, head), :] = part
            else:
                totals[pl.ds(h * head, head), :] += part
    mixture = totals[...].T.astype(bf16)
    result = (hidden[...].astype(f32) + dot(mixture, weights[3])).astype(bf16)
    second[...] = result
    blocks[...] = layer_norm(result.astype(f32)).astype(bf16)


def frame_part(queries, rows, weights):
    channels = rows.shape[1]
    head = channels // HEADS
    ones = block_diagonal(channels, head)
    keys = dot(rows, weights[1]).astype(bf16).astype(f32)
    values = dot(rows, weights[2]).astype(bf16)
    products = queries * keys
    high = products.astype(bf16)
    low = (products - high.astype(f32)).astype(bf16)
    return (dot(high, ones) + dot(low, ones)) * (LOG2E / math.sqrt(head)), values


def own_frame_kernel(where, rows, *refs):
    parts = refs[:-4]
    weights, queries, scores, values = refs[-4:]
    assemble(where, parts, weights)
    queries[...] = dot(rows[...], weights[0]).astype(bf16)
    scores[...], values[...] = frame_part(queries[...].astype(f32), rows[...], weights)


def frame_kernel(queries, rows, weights, scores, values):
    scores[...], values[...] = frame_part(queries[...].astype(f32), rows[...], weights)


def last_kernel(frames, *refs):
    second, queries, rows, weights = refs[:4]
    scores = refs[4 : 3 + frames]
    values = refs[3 + frames : 2 + 2 * frames]
    out = refs[-1]
    last_scores, last_values = frame_part(queries[...].astype(f32), rows[...], weights)
    every = [ref[...] for ref in scores] + [last_scores]
    most = functools.reduce(jnp.maximum, every)
    powers = [jnp.exp2(one - most) for one in every]
    norm = 1.0 / functools.reduce(jnp.add, powers)
    total = (powers[-1] * norm).astype(bf16).astype(f32) * last_values.astype(f32)
    for power, value in zip(powers, values):
        total += (power * norm).astype(bf16).astype(f32) * value[...].astype(f32)
    result = second[...].astype(f32) + dot(total.astype(bf16), weights[3])
    out[...] = result.T.astype(bf16)


def is_power(n):
    return n & (n - 1) == 0


def partner_permutation(size, k):
    if is_power(size):
        return [(i, i ^ k) for i in range(size)]
    return [(i, (i + k) % size) for i in range(size)]


def partner(me, size, k, sign=1):
    if is_power(size):
        return me ^ k
    return (me + sign * k) % size


def gather_maps(own, axis, size):
    maps = {0: own}
    if is_power(size):
        bit = size // 2
        while bit:
            for k in list(maps):
                maps[k | bit] = lax.ppermute(maps[k], axis, partner_permutation(size, bit))
            bit //= 2
    else:
        for k in range(1, size):
            maps[k] = lax.ppermute(own, axis, partner_permutation(size, k))
    return [maps[k] for k in range(size)]


def sum_over(value, beside, later, axis, size):
    if not is_power(size):
        return lax.psum(value, axis), beside, later
    bit = 1
    while bit < size:
        value = value + lax.ppermute(value, axis, partner_permutation(size, bit))
        if bit == 1:
            value, beside = lax.optimization_barrier((value, beside))
        bit *= 2
    value, later = lax.optimization_barrier((value, later))
    return value, beside, later


def ring_gather(own, axis, size):
    pieces = {0: own}
    right = [(i, (i + 1) % size) for i in range(size)]
    left = [(j, i) for i, j in right]
    for step in range(1, size // 2 + 1):
        pieces[step] = lax.ppermute(pieces[step - 1], axis, right)
        if size - step > step:
            pieces[size - step] = lax.ppermute(pieces[(size - step + 1) % size], axis, left)
    return [pieces[k] for k in range(size)]


def neighbours(pieces):
    return [pieces[1], pieces[-1]] if len(pieces) > 2 else pieces[1:]


def with_neighbours(pieces, near):
    pieces = list(pieces)
    if near:
        pieces[1], pieces[-1] = near[0], near[-1]
    return pieces


def gather_weights(parts, frames, videos, video):
    kinds, rows, channels = parts.shape
    mine = lax.dynamic_index_in_dim(parts.reshape(2, 2, rows, channels), video % 2, 0, keepdims=False)
    return [parts] + ring_gather(mine, "frame", frames)[1:]


def swap_weights(parts, videos):
    return parts + [lax.ppermute(part, "video", partner_permutation(videos, 1)) for part in parts[1:]]


def per_device(
    latents,
    timesteps,
    matchings,
    tile_mask,
    conv_first,
    conv_second,
    time_proj,
    epi_in,
    epi_out,
    temp_in,
    temp_out,
):
    tokens, channels = latents.shape[2:]
    tiles = tile_mask.shape[2]
    frames = lax.axis_size("frame")
    videos = lax.axis_size("video")
    frame = lax.axis_index("frame")
    video = lax.axis_index("video")
    pixels = tokens // frames
    source = latents.reshape(tokens, channels).T

    rows = time_proj.shape[0]
    half = rows * frames // 2
    index = frame * rows + jnp.arange(rows, dtype=jnp.int32)
    exponent = jnp.where(index < half, index, index - half).astype(f32)
    frequency = jnp.exp(-math.log(10000.0) * exponent / half)
    angles = timesteps.astype(f32)[:, None] * frequency[None, :]
    wave = jnp.where(index[None, :] < half, jnp.cos(angles), jnp.sin(angles))
    time_act = jax.nn.silu(wave).astype(bf16)
    share = pl.pallas_call(
        share_kernel,
        out_shape=jax.ShapeDtypeStruct((1, channels), f32),
        in_specs=[VMEM, VMEM],
        out_specs=VMEM,
        compiler_params=params(),
        cost_estimate=pl.CostEstimate(flops=10**10, bytes_accessed=1 << 20, transcendentals=0),
        name="time_share",
    )(time_act, time_proj)
    epi_own = jnp.concatenate([epi_in, epi_out[None]], axis=0)
    temp_own = jnp.concatenate([temp_in, temp_out[None]], axis=0)
    bias, source, epi_own = sum_over(share, source, epi_own, "frame", frames)
    paired = videos % 2 == 0 and is_power(videos) and epi_own.shape[1] % 16 == 0
    if paired:
        places = [(frame - k) % frames for k in range(frames)] + [video % 2]
    else:
        places = [jnp.int32(0)] * 2
    places = jnp.stack(places).astype(jnp.int32)
    if paired:
        epi_parts = gather_weights(epi_own, frames, videos, video)
    else:
        epi_parts = [lax.all_gather(epi_own, "frame", axis=1, tiled=True)]

    conv_scratch = [
        pltpu.VMEM((tokens + 2 * W, 3 * channels), bf16),
    ]
    conv_cost = pl.CostEstimate(
        flops=2 * 9 * tokens * channels * channels,
        bytes_accessed=2 * 9 * channels * channels + 8 * tokens * channels,
        transcendentals=tokens * channels,
    )
    inner = pl.pallas_call(
        first_kernel,
        out_shape=jax.ShapeDtypeStruct((tokens, channels), f32),
        in_specs=[VMEM, VMEM],
        out_specs=VMEM,
        scratch_shapes=conv_scratch,
        compiler_params=params(),
        cost_estimate=conv_cost,
        name="first_conv",
    )(source, conv_first.reshape(3, 3 * channels, channels))
    hidden, normed = pl.pallas_call(
        second_kernel,
        out_shape=[jax.ShapeDtypeStruct((tokens, channels), bf16)] * 2,
        in_specs=[VMEM, VMEM, VMEM, VMEM],
        out_specs=[VMEM, VMEM],
        scratch_shapes=conv_scratch,
        compiler_params=params(),
        cost_estimate=conv_cost,
        name="second_conv",
    )(source, inner, bias, conv_second.reshape(3, 3 * channels, channels))

    if paired:
        normed, hidden, *near = lax.optimization_barrier((normed, hidden, *neighbours(epi_parts)))
        epi_parts = with_neighbours(epi_parts, near)
    maps = gather_maps(normed, "video", videos)
    if paired:
        temp_own, maps[1] = lax.optimization_barrier((temp_own, maps[1]))
        temp_parts = gather_weights(temp_own, frames, videos, video)
        epi_parts = swap_weights(epi_parts, videos)
    else:
        temp_parts = [lax.all_gather(temp_own, "frame", axis=1, tiled=True)]
    targets = lax.dynamic_index_in_dim(matchings, video, 1, keepdims=False)
    if is_power(videos):
        select = video ^ targets
    else:
        select = (video - targets) % videos
    mask = lax.dynamic_index_in_dim(tile_mask, video, 1, keepdims=False).reshape(-1)
    square = (4, channels, channels)
    queries, epi = pl.pallas_call(
        query_kernel,
        out_shape=[
            jax.ShapeDtypeStruct((channels, tokens), f32),
            jax.ShapeDtypeStruct(square, bf16),
        ],
        in_specs=[SMEM, VMEM] + [VMEM] * len(epi_parts),
        out_specs=[VMEM] * 2,
        compiler_params=params(),
        name="query",
    )(places, normed, *epi_parts)
    if paired:
        queries, *near = lax.optimization_barrier((queries, *neighbours(temp_parts)))
        temp_parts = with_neighbours(temp_parts, near)
    second, blocks = pl.pallas_call(
        functools.partial(view_kernel, videos, tiles),
        out_shape=[jax.ShapeDtypeStruct((tokens, channels), bf16)] * 2,
        in_specs=[SMEM, SMEM, VMEM, VMEM, VMEM] + [VMEM] * videos,
        out_specs=[VMEM, VMEM],
        scratch_shapes=[
            pltpu.VMEM((tokens, channels), bf16),
            pltpu.VMEM((channels, tokens), f32),
        ],
        compiler_params=params(),
        name="cross_view",
    )(select, mask, hidden, queries, epi, *maps)

    if paired:
        blocks, *temp_parts = lax.optimization_barrier((blocks, *temp_parts))
        temp_parts = swap_weights(temp_parts, videos)
    arrived = ring_gather(blocks, "frame", frames)
    score_shape = jax.ShapeDtypeStruct((tokens, channels), f32)
    value_shape = jax.ShapeDtypeStruct((tokens, channels), bf16)
    frame_cost = pl.CostEstimate(
        flops=8 * tokens * channels * channels,
        bytes_accessed=8 * channels * channels + 8 * tokens * channels,
        transcendentals=0,
    )
    temp, frame_queries, *first = pl.pallas_call(
        own_frame_kernel,
        out_shape=[jax.ShapeDtypeStruct(square, bf16), value_shape, score_shape, value_shape],
        in_specs=[SMEM, VMEM] + [VMEM] * len(temp_parts),
        out_specs=[VMEM] * 4,
        compiler_params=params(),
        cost_estimate=frame_cost,
        name="own_frame",
    )(places, blocks, *temp_parts)
    scores, values = [first[0]], [first[1]]
    order = sorted(range(1, frames), key=lambda k: min(k, frames - k))
    for k in order[:-1]:
        one = pl.pallas_call(
            frame_kernel,
            out_shape=[score_shape, value_shape],
            in_specs=[VMEM] * 3,
            out_specs=[VMEM] * 2,
            compiler_params=params(),
            cost_estimate=frame_cost,
            name="other_frame",
        )(frame_queries, arrived[k], temp)
        scores.append(one[0])
        values.append(one[1])
    denoised = pl.pallas_call(
        functools.partial(last_kernel, frames),
        out_shape=jax.ShapeDtypeStruct((channels, tokens), bf16),
        in_specs=[VMEM] * (2 + 2 * frames),
        out_specs=VMEM,
        compiler_params=params(),
        name="last",
    )(second, frame_queries, arrived[order[-1]], temp, *scores, *values)
    return denoised.T.reshape(1, 1, tokens, channels)


def solution(mesh):
    placed = (
        P(("groups", "video"), "frame", None, None),
        P(("groups", "video")),
        P(None, "groups"),
        P(None, "groups", None, None),
        P(),
        P(),
        P("frame", None),
        P(None, "frame", None),
        P("frame", None),
        P(None, "frame", None),
        P("frame", None),
    )
    return jax.shard_map(
        per_device,
        mesh=mesh,
        in_specs=placed,
        out_specs=P(("groups", "video"), "frame", None, None),
        check_vma=False,
    )
```

```python
import functools
import math

import jax
import jax.numpy as jnp
from jax import lax
from jax.experimental import pallas as pl
from jax.experimental.pallas import tpu as pltpu
from jax.sharding import PartitionSpec as P

HEADS = 8
NORM_GROUPS = 32
TEMB = 1280
H = 8
W = 32

EPSILON = 1e-05
MASKED = -1e30
LOG2E = 1.4426950408889634
SHARE_ROWS = 16

VMEM = pl.BlockSpec(memory_space=pltpu.VMEM)
SMEM = pl.BlockSpec(memory_space=pltpu.SMEM)
f32 = jnp.float32
bf16 = jnp.bfloat16


def params():
    return pltpu.CompilerParams(vmem_limit_bytes=16 * 1024 * 1024)


def dot(a, b):
    return jnp.dot(a, b, preferred_element_type=f32)


def block_diagonal(size, width):
    rows = lax.broadcasted_iota(jnp.int32, (size, 1), 0).astype(f32)
    cols = lax.broadcasted_iota(jnp.int32, (1, size), 1).astype(f32)
    rows = jnp.floor((rows + 0.5) * (1.0 / width))
    cols = jnp.floor((cols + 0.5) * (1.0 / width))
    return (rows == cols).astype(f32).astype(bf16)


def terms(row):
    first = row.astype(bf16).astype(f32)
    second = (row - first).astype(bf16).astype(f32)
    third = row - first - second
    index = lax.broadcasted_iota(jnp.int32, (SHARE_ROWS, row.shape[1]), 0)
    return jnp.where(
        index == 0, first, jnp.where(index == 1, second, jnp.where(index == 2, third, 0.0))
    )


def group_sum(row, ones):
    return jnp.sum(dot(terms(row).astype(bf16), ones), axis=0, keepdims=True)


def group_norm_silu(x):
    tokens, channels = x.shape
    width = channels // NORM_GROUPS
    ones = block_diagonal(channels, width)
    inverse = 1.0 / (tokens * width)
    average = group_sum(jnp.sum(x, axis=0, keepdims=True), ones) * inverse
    centred = x - average
    spread = group_sum(jnp.sum(centred * centred, axis=0, keepdims=True), ones) * inverse
    y = centred * lax.rsqrt(spread + EPSILON)
    return y / (1.0 + jnp.exp(-y))


def layer_norm(x):
    inverse = 1.0 / x.shape[1]
    average = jnp.sum(x, axis=1, keepdims=True) * inverse
    centred = x - average
    spread = jnp.sum(centred * centred, axis=1, keepdims=True) * inverse
    return centred * lax.rsqrt(spread + EPSILON)


def convolve(y, weight, padded):
    tokens, channels = y.shape
    column = lax.broadcasted_iota(jnp.int32, (tokens, 1), 0) & (W - 1)
    before = jnp.where(column == 0, 0.0, pltpu.roll(y, 1, 0))
    after = jnp.where(column == W - 1, 0.0, pltpu.roll(y, tokens - 1, 0))
    padded[pl.ds(0, W), :] = jnp.zeros((W, 3 * channels), bf16)
    padded[pl.ds(tokens + W, W), :] = jnp.zeros((W, 3 * channels), bf16)
    padded[pl.ds(W, tokens), :] = jnp.concatenate(
        [before.astype(bf16), y.astype(bf16), after.astype(bf16)], axis=1
    )
    total = None
    for k in range(3):
        part = dot(padded[pl.ds(k * W, tokens), :], weight[k])
        total = part if total is None else total + part
    return total


def share_kernel(act, proj, share):
    share[...] = dot(act[...], proj[...])


def payload_kernel(side, act, proj, three, one, payload):
    rows, channels = one.shape
    share = dot(act[...], proj[...])
    payload[pl.ds(2 * rows, SHARE_ROWS), :] = terms(share).astype(bf16)

    @pl.when(side[0] == 0)
    def _():
        payload[pl.ds(0, rows), :] = three[0]
        payload[pl.ds(rows, rows), :] = three[1]

    @pl.when(side[0] != 0)
    def _():
        payload[pl.ds(0, rows), :] = three[2]
        payload[pl.ds(rows, rows), :] = one[...]


def first_kernel(source, weight, inner, padded):
    inner[...] = convolve(group_norm_silu(source[...].astype(f32).T), weight, padded)


def second_kernel(source, inner, weight, *refs):
    shares, (hidden, normed, padded) = refs[:-3], refs[-3:]
    bias = None
    for share in shares:
        rows = min(SHARE_ROWS, share.shape[0])
        part = jnp.sum(share[pl.ds(share.shape[0] - rows, rows), :].astype(f32), axis=0, keepdims=True)
        bias = part if bias is None else bias + part
    y = group_norm_silu(inner[...] + bias)
    total = source[...].astype(f32).T + convolve(y, weight, padded)
    rounded = total.astype(bf16)
    hidden[...] = rounded
    normed[...] = layer_norm(rounded.astype(f32)).astype(bf16)


def assemble(where, own, received, swapped, whole):
    rows = own[0].shape[0]
    for kind in range(4):
        whole[kind, pl.ds(pl.multiple_of(where[0] * rows, 16), rows), :] = own[kind]
    count = len(received)
    for k in range(1, count + 1):
        place = pl.ds(pl.multiple_of(where[k] * rows, 16), rows)
        for j in range(2):
            mine = where[count + 1] * 2 + j
            whole[mine, place, :] = received[k - 1][pl.ds(j * rows, rows), :]
            start = ((k - 1) * 2 + j) * rows
            whole[2 - mine + 2 * j, place, :] = swapped[pl.ds(start, rows), :]


def own_rows(three, one):
    return [three[0], three[1], three[2], one[...]]


def query_kernel(where, normed, three, one, *refs):
    parts, (queries, epi) = refs[:-2], refs[-2:]
    assemble(where, own_rows(three, one), parts[:-1], parts[-1] if parts else None, epi)
    queries[...] = dot(normed[...], epi[0]).astype(bf16).astype(f32).T


def view_kernel(count, tiles, *refs):
    select, mask, hidden, query_ref, weights = refs[:5]
    maps = refs[5 : 5 + count]
    second, blocks, chosen, totals = refs[5 + count :]
    tokens, channels = hidden.shape
    head = channels // HEADS
    width = tokens // tiles
    scale = LOG2E / math.sqrt(head)
    queries = query_ref[...]
    lane_tile = lax.broadcasted_iota(jnp.int32, (1, tokens), 1) // width
    windows = []
    for h in range(HEADS):
        low = h * head // 128 * 128
        high = min(channels, -(-(h + 1) * head // 128) * 128)
        row = lax.broadcasted_iota(jnp.int32, (high - low, 1), 0) + low
        inside = (row >= h * head) & (row < (h + 1) * head)
        windows.append((low, high, jnp.where(inside, queries[low:high], 0.0).astype(bf16)))
    for matching in range(2):
        for j in range(count):

            @pl.when(select[matching] == j)
            def _():
                chosen[...] = maps[j][...]

        other = chosen[...]
        keys = dot(other, weights[1]).astype(bf16)
        values = dot(other, weights[2]).T
        shifts = []
        for j in range(tiles):
            row = jnp.zeros((1, tokens), f32)
            for i in range(tiles):
                bit = mask[(matching * tiles + i) * tiles + j]
                row = jnp.where(lane_tile == i, jnp.where(bit > 0, 0.0, MASKED), row)
            shifts.append(row)
        for h in range(HEADS):
            low, high, wanted = windows[h]
            scores = dot(keys[:, low:high], wanted) * scale
            scores = jnp.concatenate(
                [scores[j * width : (j + 1) * width] + shifts[j] for j in range(tiles)], axis=0
            )
            powers = jnp.exp2(scores - jnp.max(scores, axis=0, keepdims=True))
            norm = 1.0 / jnp.sum(powers, axis=0, keepdims=True)
            part = dot(values[h * head : (h + 1) * head].astype(bf16), powers.astype(bf16)) * norm
            if matching == 0:
                totals[pl.ds(h * head, head), :] = part
            else:
                totals[pl.ds(h * head, head), :] += part
    mixture = totals[...].T.astype(bf16)
    result = (hidden[...].astype(f32) + dot(mixture, weights[3])).astype(bf16)
    second[...] = result
    blocks[...] = layer_norm(result.astype(f32)).astype(bf16)


def frame_part(queries, rows, weights):
    channels = rows.shape[1]
    head = channels // HEADS
    ones = block_diagonal(channels, head)
    keys = dot(rows, weights[1]).astype(bf16).astype(f32)
    values = dot(rows, weights[2]).astype(bf16)
    products = queries * keys
    high = products.astype(bf16)
    low = (products - high.astype(f32)).astype(bf16)
    return (dot(high, ones) + dot(low, ones)) * (LOG2E / math.sqrt(head)), values


def own_frame_kernel(where, rows, three, one, *refs):
    parts, (weights, queries, scores, values) = refs[:-4], refs[-4:]
    assemble(where, own_rows(three, one), parts[:-1], parts[-1] if parts else None, weights)
    queries[...] = dot(rows[...], weights[0]).astype(bf16)
    scores[...], values[...] = frame_part(queries[...].astype(f32), rows[...], weights)


def frame_kernel(queries, rows, weights, scores, values):
    scores[...], values[...] = frame_part(queries[...].astype(f32), rows[...], weights)


def last_kernel(frames, *refs):
    second, queries, rows, weights = refs[:4]
    scores = refs[4 : 3 + frames]
    values = refs[3 + frames : 2 + 2 * frames]
    out = refs[-1]
    last_scores, last_values = frame_part(queries[...].astype(f32), rows[...], weights)
    every = [ref[...] for ref in scores] + [last_scores]
    most = functools.reduce(jnp.maximum, every)
    powers = [jnp.exp2(one - most) for one in every]
    norm = 1.0 / functools.reduce(jnp.add, powers)
    total = (powers[-1] * norm).astype(bf16).astype(f32) * last_values.astype(f32)
    for power, value in zip(powers, values):
        total += (power * norm).astype(bf16).astype(f32) * value[...].astype(f32)
    result = second[...].astype(f32) + dot(total.astype(bf16), weights[3])
    out[...] = result.T.astype(bf16)


def is_power(n):
    return n & (n - 1) == 0


def partner_permutation(size, k):
    if is_power(size):
        return [(i, i ^ k) for i in range(size)]
    return [(i, (i + k) % size) for i in range(size)]


def partner(me, size, k, sign=1):
    if is_power(size):
        return me ^ k
    return (me + sign * k) % size


def gather_maps(own, axis, size):
    maps = {0: own}
    if is_power(size):
        bit = size // 2
        while bit:
            for k in list(maps):
                maps[k | bit] = lax.ppermute(maps[k], axis, partner_permutation(size, bit))
            bit //= 2
    else:
        for k in range(1, size):
            maps[k] = lax.ppermute(own, axis, partner_permutation(size, k))
    return [maps[k] for k in range(size)]


def sum_over(value, beside, later, axis, size):
    if not is_power(size):
        return lax.psum(value, axis), beside, later
    bit = 1
    while bit < size:
        value = value + lax.ppermute(value, axis, partner_permutation(size, bit))
        if bit == 1:
            value, beside = lax.optimization_barrier((value, beside))
        bit *= 2
    value, later = lax.optimization_barrier((value, later))
    return value, beside, later


def ring_gather(own, axis, size, beside=None):
    pieces = {0: own}
    right = [(i, (i + 1) % size) for i in range(size)]
    left = [(j, i) for i, j in right]
    for step in range(1, size // 2 + 1):
        pieces[step] = lax.ppermute(pieces[step - 1], axis, right)
        if size - step > step:
            pieces[size - step] = lax.ppermute(pieces[(size - step + 1) % size], axis, left)
        if step == 1 and beside is not None:
            pieces[1], beside = lax.optimization_barrier((pieces[1], beside))
    pieces = [pieces[k] for k in range(size)]
    return pieces if beside is None else (pieces, beside)


def neighbours(pieces):
    return [pieces[1], pieces[-1]] if len(pieces) > 2 else pieces[1:]


def with_neighbours(pieces, near):
    pieces = list(pieces)
    if near:
        pieces[1], pieces[-1] = near[0], near[-1]
    return pieces


def swap(pieces, rows, videos):
    joined = jnp.concatenate([piece[:rows] for piece in pieces[1:]], axis=0)
    return pieces[1:] + [lax.ppermute(joined, "video", partner_permutation(videos, 1))]


def per_device(
    latents,
    timesteps,
    matchings,
    tile_mask,
    conv_first,
    conv_second,
    time_proj,
    epi_in,
    epi_out,
    temp_in,
    temp_out,
):
    tokens, channels = latents.shape[2:]
    tiles = tile_mask.shape[2]
    frames = lax.axis_size("frame")
    videos = lax.axis_size("video")
    frame = lax.axis_index("frame")
    video = lax.axis_index("video")
    pixels = tokens // frames
    source = latents.reshape(tokens, channels).T

    rows = time_proj.shape[0]
    half = rows * frames // 2
    index = frame * rows + jnp.arange(rows, dtype=jnp.int32)
    exponent = jnp.where(index < half, index, index - half).astype(f32)
    frequency = jnp.exp(-math.log(10000.0) * exponent / half)
    angles = timesteps.astype(f32)[:, None] * frequency[None, :]
    wave = jnp.where(index[None, :] < half, jnp.cos(angles), jnp.sin(angles))
    time_act = jax.nn.silu(wave).astype(bf16)
    height = epi_out.shape[0]
    paired = videos % 2 == 0 and is_power(videos) and height % 16 == 0
    early = pl.CostEstimate(flops=10**10, bytes_accessed=1 << 20, transcendentals=0)
    if paired:
        side = (video % 2).astype(jnp.int32).reshape(1)
        payload = pl.pallas_call(
            payload_kernel,
            out_shape=jax.ShapeDtypeStruct((2 * height + SHARE_ROWS, channels), bf16),
            in_specs=[SMEM, VMEM, VMEM, VMEM, VMEM],
            out_specs=VMEM,
            compiler_params=params(),
            cost_estimate=early,
            name="payload",
        )(side, time_act, time_proj, epi_in, epi_out)
        shares = [payload]
        places = [(frame - k) % frames for k in range(frames)] + [video % 2]
    else:
        share = pl.pallas_call(
            share_kernel,
            out_shape=jax.ShapeDtypeStruct((1, channels), f32),
            in_specs=[VMEM, VMEM],
            out_specs=VMEM,
            compiler_params=params(),
            cost_estimate=early,
            name="time_share",
        )(time_act, time_proj)
        shares = [lax.psum(share, "frame")]
        places = [jnp.int32(0)] * 2
        epi_in = lax.all_gather(epi_in, "frame", axis=1, tiled=True)
        epi_out = lax.all_gather(epi_out, "frame", axis=0, tiled=True)
        temp_in = lax.all_gather(temp_in, "frame", axis=1, tiled=True)
        temp_out = lax.all_gather(temp_out, "frame", axis=0, tiled=True)
    places = jnp.stack(places).astype(jnp.int32)

    conv_scratch = [
        pltpu.VMEM((tokens + 2 * W, 3 * channels), bf16),
    ]
    conv_cost = pl.CostEstimate(
        flops=2 * 9 * tokens * channels * channels,
        bytes_accessed=2 * 9 * channels * channels + 8 * tokens * channels,
        transcendentals=tokens * channels,
    )
    inner = pl.pallas_call(
        first_kernel,
        out_shape=jax.ShapeDtypeStruct((tokens, channels), f32),
        in_specs=[VMEM, VMEM],
        out_specs=VMEM,
        scratch_shapes=conv_scratch,
        compiler_params=params(),
        cost_estimate=conv_cost,
        name="first_conv",
    )(source, conv_first.reshape(3, 3 * channels, channels))
    temp_parts = []
    if paired:
        shares, inner = ring_gather(shares[0], "frame", frames, inner)
        temp_own = jnp.concatenate([temp_in, temp_out[None]], axis=0)
        temp_own = temp_own.reshape(2, 2 * height, channels)
        mine = lax.dynamic_index_in_dim(temp_own, video % 2, 0, keepdims=False)
        mine, *near = lax.optimization_barrier((mine, *neighbours(shares)))
        shares = with_neighbours(shares, near)
        temp_parts = ring_gather(mine, "frame", frames)
    hidden, normed = pl.pallas_call(
        second_kernel,
        out_shape=[
            jax.ShapeDtypeStruct((tokens, channels), bf16),
            jax.ShapeDtypeStruct((tokens, channels), bf16),
        ],
        in_specs=[VMEM] * (3 + len(shares)),
        out_specs=[VMEM] * 2,
        scratch_shapes=conv_scratch,
        compiler_params=params(),
        cost_estimate=conv_cost,
        name="second_conv",
    )(source, inner, conv_second.reshape(3, 3 * channels, channels), *shares)
    if paired:
        normed, hidden, *near = lax.optimization_barrier((normed, hidden, *neighbours(temp_parts)))
        temp_parts = with_neighbours(temp_parts, near)
    maps = gather_maps(normed, "video", videos)
    epi_parts = swap(shares, 2 * height, videos) if paired else []
    targets = lax.dynamic_index_in_dim(matchings, video, 1, keepdims=False)
    if is_power(videos):
        select = video ^ targets
    else:
        select = (video - targets) % videos
    mask = lax.dynamic_index_in_dim(tile_mask, video, 1, keepdims=False).reshape(-1)
    square = (4, channels, channels)
    queries, epi = pl.pallas_call(
        query_kernel,
        out_shape=[
            jax.ShapeDtypeStruct((channels, tokens), f32),
            jax.ShapeDtypeStruct(square, bf16),
        ],
        in_specs=[SMEM, VMEM, VMEM, VMEM] + [VMEM] * len(epi_parts),
        out_specs=[VMEM] * 2,
        compiler_params=params(),
        name="query",
    )(places, normed, epi_in, epi_out, *epi_parts)
    second, blocks = pl.pallas_call(
        functools.partial(view_kernel, videos, tiles),
        out_shape=[jax.ShapeDtypeStruct((tokens, channels), bf16)] * 2,
        in_specs=[SMEM, SMEM, VMEM, VMEM, VMEM] + [VMEM] * videos,
        out_specs=[VMEM, VMEM],
        scratch_shapes=[
            pltpu.VMEM((tokens, channels), bf16),
            pltpu.VMEM((channels, tokens), f32),
        ],
        compiler_params=params(),
        name="cross_view",
    )(select, mask, hidden, queries, epi, *maps)

    if paired:
        blocks, *temp_parts = lax.optimization_barrier((blocks, *temp_parts))
        temp_parts = swap(temp_parts, 2 * height, videos)
    arrived = ring_gather(blocks, "frame", frames)
    score_shape = jax.ShapeDtypeStruct((tokens, channels), f32)
    value_shape = jax.ShapeDtypeStruct((tokens, channels), bf16)
    frame_cost = pl.CostEstimate(
        flops=8 * tokens * channels * channels,
        bytes_accessed=8 * channels * channels + 8 * tokens * channels,
        transcendentals=0,
    )
    temp, frame_queries, *first = pl.pallas_call(
        own_frame_kernel,
        out_shape=[jax.ShapeDtypeStruct(square, bf16), value_shape, score_shape, value_shape],
        in_specs=[SMEM, VMEM, VMEM, VMEM] + [VMEM] * len(temp_parts),
        out_specs=[VMEM] * 4,
        compiler_params=params(),
        cost_estimate=frame_cost,
        name="own_frame",
    )(places, blocks, temp_in, temp_out, *temp_parts)
    scores, values = [first[0]], [first[1]]
    order = sorted(range(1, frames), key=lambda k: min(k, frames - k))
    for k in order[:-1]:
        one = pl.pallas_call(
            frame_kernel,
            out_shape=[score_shape, value_shape],
            in_specs=[VMEM] * 3,
            out_specs=[VMEM] * 2,
            compiler_params=params(),
            cost_estimate=frame_cost,
            name="other_frame",
        )(frame_queries, arrived[k], temp)
        scores.append(one[0])
        values.append(one[1])
    denoised = pl.pallas_call(
        functools.partial(last_kernel, frames),
        out_shape=jax.ShapeDtypeStruct((channels, tokens), bf16),
        in_specs=[VMEM] * (2 + 2 * frames),
        out_specs=VMEM,
        compiler_params=params(),
        name="last",
    )(second, frame_queries, arrived[order[-1]], temp, *scores, *values)
    return denoised.T.reshape(1, 1, tokens, channels)


def solution(mesh):
    placed = (
        P(("groups", "video"), "frame", None, None),
        P(("groups", "video")),
        P(None, "groups"),
        P(None, "groups", None, None),
        P(),
        P(),
        P("frame", None),
        P(None, "frame", None),
        P("frame", None),
        P(None, "frame", None),
        P("frame", None),
    )
    return jax.shard_map(
        per_device,
        mesh=mesh,
        in_specs=placed,
        out_specs=P(("groups", "video"), "frame", None, None),
        check_vma=False,
    )
```

```python
import functools
import math

import jax
import jax.numpy as jnp
from jax import lax
from jax.experimental import pallas as pl
from jax.experimental.pallas import tpu as pltpu
from jax.sharding import PartitionSpec as P

HEADS = 8
NORM_GROUPS = 32
TEMB = 1280
H = 8
W = 32

EPSILON = 1e-05
MASKED = -1e30
LOG2E = 1.4426950408889634
SHARE_ROWS = 16

VMEM = pl.BlockSpec(memory_space=pltpu.VMEM)
SMEM = pl.BlockSpec(memory_space=pltpu.SMEM)
HBM = pl.BlockSpec(memory_space=pl.ANY)
f32 = jnp.float32
bf16 = jnp.bfloat16


def params():
    return pltpu.CompilerParams(vmem_limit_bytes=16 * 1024 * 1024)


def in_hbm(x):
    return pltpu.with_memory_space_constraint(x, pltpu.HBM)


def fetch(source, target, sem):
    copy = pltpu.make_async_copy(source, target, sem)
    copy.start()
    return copy


def dot(a, b):
    return jnp.dot(a, b, preferred_element_type=f32)


def block_diagonal(size, width):
    rows = lax.broadcasted_iota(jnp.int32, (size, 1), 0).astype(f32)
    cols = lax.broadcasted_iota(jnp.int32, (1, size), 1).astype(f32)
    rows = jnp.floor((rows + 0.5) * (1.0 / width))
    cols = jnp.floor((cols + 0.5) * (1.0 / width))
    return (rows == cols).astype(f32).astype(bf16)


def terms(row):
    first = row.astype(bf16).astype(f32)
    second = (row - first).astype(bf16).astype(f32)
    third = row - first - second
    index = lax.broadcasted_iota(jnp.int32, (SHARE_ROWS, row.shape[1]), 0)
    return jnp.where(
        index == 0, first, jnp.where(index == 1, second, jnp.where(index == 2, third, 0.0))
    )


def group_sum(row, ones):
    return jnp.sum(dot(terms(row).astype(bf16), ones), axis=0, keepdims=True)


def group_norm_silu(x):
    tokens, channels = x.shape
    width = channels // NORM_GROUPS
    ones = block_diagonal(channels, width)
    inverse = 1.0 / (tokens * width)
    average = group_sum(jnp.sum(x, axis=0, keepdims=True), ones) * inverse
    centred = x - average
    spread = group_sum(jnp.sum(centred * centred, axis=0, keepdims=True), ones) * inverse
    y = centred * lax.rsqrt(spread + EPSILON)
    return y / (1.0 + jnp.exp(-y))


def layer_norm(x):
    inverse = 1.0 / x.shape[1]
    average = jnp.sum(x, axis=1, keepdims=True) * inverse
    centred = x - average
    spread = jnp.sum(centred * centred, axis=1, keepdims=True) * inverse
    return centred * lax.rsqrt(spread + EPSILON)


def convolve(y, weight, padded, copies):
    tokens, channels = y.shape
    column = lax.broadcasted_iota(jnp.int32, (tokens, 1), 0) & (W - 1)
    before = jnp.where(column == 0, 0.0, pltpu.roll(y, 1, 0))
    after = jnp.where(column == W - 1, 0.0, pltpu.roll(y, tokens - 1, 0))
    padded[pl.ds(0, W), :] = jnp.zeros((W, 3 * channels), bf16)
    padded[pl.ds(tokens + W, W), :] = jnp.zeros((W, 3 * channels), bf16)
    padded[pl.ds(W, tokens), :] = jnp.concatenate(
        [before.astype(bf16), y.astype(bf16), after.astype(bf16)], axis=1
    )
    total = None
    for k in range(3):
        if copies:
            copies[k].wait()
        part = dot(padded[pl.ds(k * W, tokens), :], weight[k])
        total = part if total is None else total + part
    return total


def share_kernel(act, proj, share):
    share[...] = dot(act[...], proj[...])


def payload_kernel(side, act, proj_hbm, three, one, payload, proj, sems):
    rows, channels = one.shape
    copy = fetch(proj_hbm, proj, sems.at[0])
    upper, lower = payload.at[pl.ds(0, rows)], payload.at[pl.ds(rows, rows)]

    @pl.when(side[0] == 0)
    def _():
        fetch(three.at[0], upper, sems.at[1])
        fetch(three.at[1], lower, sems.at[2])

    @pl.when(side[0] != 0)
    def _():
        fetch(three.at[2], upper, sems.at[1])
        fetch(one, lower, sems.at[2])

    copy.wait()
    payload[pl.ds(2 * rows, SHARE_ROWS), :] = terms(dot(act[...], proj[...])).astype(bf16)
    pltpu.make_async_copy(one, upper, sems.at[1]).wait()
    pltpu.make_async_copy(one, lower, sems.at[2]).wait()


def first_kernel(source_hbm, weight_hbm, inner, source, weight, padded, sems):
    copy = fetch(source_hbm, source, sems.at[0])
    copies = [fetch(weight_hbm.at[k], weight.at[k], sems.at[1 + k]) for k in range(3)]
    copy.wait()
    inner[...] = convolve(group_norm_silu(source[...].astype(f32).T), weight, padded, copies)


def second_kernel(source_hbm, inner, weight, *refs):
    shares, (hidden, normed, source, padded, sems) = refs[:-5], refs[-5:]
    copy = fetch(source_hbm, source, sems.at[0])
    bias = None
    for share in shares:
        rows = min(SHARE_ROWS, share.shape[0])
        part = jnp.sum(share[pl.ds(share.shape[0] - rows, rows), :].astype(f32), axis=0, keepdims=True)
        bias = part if bias is None else bias + part
    y = group_norm_silu(inner[...] + bias)
    total = convolve(y, weight, padded, [])
    copy.wait()
    rounded = (source[...].astype(f32).T + total).astype(bf16)
    hidden[...] = rounded
    normed[...] = layer_norm(rounded.astype(f32)).astype(bf16)


def fetch_own(where, three, one, whole, sems):
    rows = one.shape[0]
    place = pl.ds(pl.multiple_of(where[0] * rows, 16), rows)
    copies = [fetch(three.at[k], whole.at[k, place], sems.at[k]) for k in range(3)]
    return copies + [fetch(one, whole.at[3, place], sems.at[3])]


def query_kernel(where, normed, three, one, *refs):
    parts, (queries, epi, sems) = refs[:-3], refs[-3:]
    copies = fetch_own(where, three, one, epi, sems)
    rows = one.shape[0]
    count = len(parts) - 1
    for k in range(1, count + 1):
        place = pl.ds(pl.multiple_of(where[k] * rows, 16), rows)
        for j in range(2):
            mine = where[count + 1] * 2 + j
            epi[mine, place, :] = parts[k - 1][pl.ds(j * rows, rows), :]
            start = ((k - 1) * 2 + j) * rows
            epi[2 - mine + 2 * j, place, :] = parts[-1][pl.ds(start, rows), :]
    for copy in copies:
        copy.wait()
    queries[...] = dot(normed[...], epi[0]).astype(bf16).astype(f32).T


def view_kernel(count, tiles, *refs):
    select, mask, hidden_ref, query_ref, weights = refs[:5]
    maps = refs[5 : 5 + count]
    second, blocks, chosen, totals, hidden, sem = refs[5 + count :]
    copy = fetch(hidden_ref, hidden, sem)
    tokens, channels = hidden.shape
    head = channels // HEADS
    width = tokens // tiles
    scale = LOG2E / math.sqrt(head)
    queries = query_ref[...]
    lane_tile = lax.broadcasted_iota(jnp.int32, (1, tokens), 1) // width
    windows = []
    for h in range(HEADS):
        low = h * head // 128 * 128
        high = min(channels, -(-(h + 1) * head // 128) * 128)
        row = lax.broadcasted_iota(jnp.int32, (high - low, 1), 0) + low
        inside = (row >= h * head) & (row < (h + 1) * head)
        windows.append((low, high, jnp.where(inside, queries[low:high], 0.0).astype(bf16)))
    for matching in range(2):
        for j in range(count):

            @pl.when(select[matching] == j)
            def _():
                chosen[...] = maps[j][...]

        other = chosen[...]
        keys = dot(other, weights[1]).astype(bf16)
        values = dot(other, weights[2]).T
        shifts = []
        for j in range(tiles):
            row = jnp.zeros((1, tokens), f32)
            for i in range(tiles):
                bit = mask[(matching * tiles + i) * tiles + j]
                row = jnp.where(lane_tile == i, jnp.where(bit > 0, 0.0, MASKED), row)
            shifts.append(row)
        for h in range(HEADS):
            low, high, wanted = windows[h]
            scores = dot(keys[:, low:high], wanted) * scale
            scores = jnp.concatenate(
                [scores[j * width : (j + 1) * width] + shifts[j] for j in range(tiles)], axis=0
            )
            powers = jnp.exp2(scores - jnp.max(scores, axis=0, keepdims=True))
            norm = 1.0 / jnp.sum(powers, axis=0, keepdims=True)
            part = dot(values[h * head : (h + 1) * head].astype(bf16), powers.astype(bf16)) * norm
            if matching == 0:
                totals[pl.ds(h * head, head), :] = part
            else:
                totals[pl.ds(h * head, head), :] += part
    mixture = totals[...].T.astype(bf16)
    copy.wait()
    result = (hidden[...].astype(f32) + dot(mixture, weights[3])).astype(bf16)
    second[...] = result
    blocks[...] = layer_norm(result.astype(f32)).astype(bf16)


def frame_part(queries, rows, weights):
    channels = rows.shape[1]
    head = channels // HEADS
    ones = block_diagonal(channels, head)
    keys = dot(rows, weights[1]).astype(bf16).astype(f32)
    values = dot(rows, weights[2]).astype(bf16)
    products = queries * keys
    high = products.astype(bf16)
    low = (products - high.astype(f32)).astype(bf16)
    return (dot(high, ones) + dot(low, ones)) * (LOG2E / math.sqrt(head)), values


def own_frame_kernel(where, rows, three, one, *refs):
    parts, (weights, queries, scores, values, sems) = refs[:-5], refs[-5:]
    copies = fetch_own(where, three, one, weights, sems)
    height = one.shape[0]
    for k, part in enumerate(parts):
        place = pl.ds(pl.multiple_of(where[k + 1] * height, 16), height)
        for kind in range(4):
            weights[kind, place, :] = part[pl.ds(kind * height, height), :]
    for copy in copies:
        copy.wait()
    queries[...] = dot(rows[...], weights[0]).astype(bf16)
    scores[...], values[...] = frame_part(queries[...].astype(f32), rows[...], weights)


def frame_kernel(queries, rows, weights, scores, values):
    scores[...], values[...] = frame_part(queries[...].astype(f32), rows[...], weights)


def last_kernel(frames, *refs):
    second, queries, rows, weights = refs[:4]
    scores = refs[4 : 3 + frames]
    values = refs[3 + frames : 2 + 2 * frames]
    out = refs[-1]
    last_scores, last_values = frame_part(queries[...].astype(f32), rows[...], weights)
    every = [ref[...] for ref in scores] + [last_scores]
    most = functools.reduce(jnp.maximum, every)
    powers = [jnp.exp2(one - most) for one in every]
    norm = 1.0 / functools.reduce(jnp.add, powers)
    total = (powers[-1] * norm).astype(bf16).astype(f32) * last_values.astype(f32)
    for power, value in zip(powers, values):
        total += (power * norm).astype(bf16).astype(f32) * value[...].astype(f32)
    result = second[...].astype(f32) + dot(total.astype(bf16), weights[3])
    out[...] = result.T.astype(bf16)


def is_power(n):
    return n & (n - 1) == 0


def partner_permutation(size, k):
    if is_power(size):
        return [(i, i ^ k) for i in range(size)]
    return [(i, (i + k) % size) for i in range(size)]


def partner(me, size, k, sign=1):
    if is_power(size):
        return me ^ k
    return (me + sign * k) % size


def gather_maps(own, axis, size):
    maps = {0: own}
    if is_power(size):
        bit = size // 2
        while bit:
            for k in list(maps):
                maps[k | bit] = lax.ppermute(maps[k], axis, partner_permutation(size, bit))
            bit //= 2
    else:
        for k in range(1, size):
            maps[k] = lax.ppermute(own, axis, partner_permutation(size, k))
    return [maps[k] for k in range(size)]


def sum_over(value, beside, later, axis, size):
    if not is_power(size):
        return lax.psum(value, axis), beside, later
    bit = 1
    while bit < size:
        value = value + lax.ppermute(value, axis, partner_permutation(size, bit))
        if bit == 1:
            value, beside = lax.optimization_barrier((value, beside))
        bit *= 2
    value, later = lax.optimization_barrier((value, later))
    return value, beside, later


def ring_gather(own, axis, size, beside=None):
    pieces = {0: own}
    right = [(i, (i + 1) % size) for i in range(size)]
    left = [(j, i) for i, j in right]
    for step in range(1, size // 2 + 1):
        pieces[step] = lax.ppermute(pieces[step - 1], axis, right)
        if size - step > step:
            pieces[size - step] = lax.ppermute(pieces[(size - step + 1) % size], axis, left)
        if step == 1 and beside is not None:
            pieces[1], beside = lax.optimization_barrier((pieces[1], beside))
    pieces = [pieces[k] for k in range(size)]
    return pieces if beside is None else (pieces, beside)


def neighbours(pieces):
    return [pieces[1], pieces[-1]] if len(pieces) > 2 else pieces[1:]


def with_neighbours(pieces, near):
    pieces = list(pieces)
    if near:
        pieces[1], pieces[-1] = near[0], near[-1]
    return pieces


def swap(pieces, rows, videos):
    joined = jnp.concatenate([piece[:rows] for piece in pieces[1:]], axis=0)
    return pieces[1:] + [lax.ppermute(joined, "video", partner_permutation(videos, 1))]


def per_device(
    latents,
    timesteps,
    matchings,
    tile_mask,
    conv_first,
    conv_second,
    time_proj,
    epi_in,
    epi_out,
    temp_in,
    temp_out,
):
    tokens, channels = latents.shape[2:]
    tiles = tile_mask.shape[2]
    frames = lax.axis_size("frame")
    videos = lax.axis_size("video")
    frame = lax.axis_index("frame")
    video = lax.axis_index("video")
    pixels = tokens // frames
    source = latents.reshape(tokens, channels).T

    rows = time_proj.shape[0]
    half = rows * frames // 2
    index = frame * rows + jnp.arange(rows, dtype=jnp.int32)
    exponent = jnp.where(index < half, index, index - half).astype(f32)
    frequency = jnp.exp(-math.log(10000.0) * exponent / half)
    angles = timesteps.astype(f32)[:, None] * frequency[None, :]
    wave = jnp.where(index[None, :] < half, jnp.cos(angles), jnp.sin(angles))
    time_act = jax.nn.silu(wave).astype(bf16)
    height = epi_out.shape[0]
    paired = videos % 2 == 0 and is_power(videos) and height % 16 == 0
    early = pl.CostEstimate(flops=10**10, bytes_accessed=1 << 20, transcendentals=0)
    if paired:
        side = (video % 2).astype(jnp.int32).reshape(1)
        payload = pl.pallas_call(
            payload_kernel,
            out_shape=jax.ShapeDtypeStruct((2 * height + SHARE_ROWS, channels), bf16),
            in_specs=[SMEM, VMEM, HBM, HBM, HBM],
            out_specs=VMEM,
            scratch_shapes=[
                pltpu.VMEM(time_proj.shape, bf16),
                pltpu.SemaphoreType.DMA((3,)),
            ],
            compiler_params=params(),
            cost_estimate=early,
            name="payload",
        )(side, time_act, in_hbm(time_proj), in_hbm(epi_in), in_hbm(epi_out))
        shares = [payload]
        places = [(frame - k) % frames for k in range(frames)] + [video % 2]
    else:
        share = pl.pallas_call(
            share_kernel,
            out_shape=jax.ShapeDtypeStruct((1, channels), f32),
            in_specs=[VMEM, VMEM],
            out_specs=VMEM,
            compiler_params=params(),
            cost_estimate=early,
            name="time_share",
        )(time_act, time_proj)
        shares = [lax.psum(share, "frame")]
        places = [jnp.int32(0)] * 2
        epi_in = lax.all_gather(epi_in, "frame", axis=1, tiled=True)
        epi_out = lax.all_gather(epi_out, "frame", axis=0, tiled=True)
        temp_in = lax.all_gather(temp_in, "frame", axis=1, tiled=True)
        temp_out = lax.all_gather(temp_out, "frame", axis=0, tiled=True)
    places = jnp.stack(places).astype(jnp.int32)

    source_scratch = pltpu.VMEM((channels, tokens), bf16)
    padded_scratch = pltpu.VMEM((tokens + 2 * W, 3 * channels), bf16)
    conv_cost = pl.CostEstimate(
        flops=2 * 9 * tokens * channels * channels,
        bytes_accessed=2 * 9 * channels * channels + 8 * tokens * channels,
        transcendentals=tokens * channels,
    )
    inner = pl.pallas_call(
        first_kernel,
        out_shape=jax.ShapeDtypeStruct((tokens, channels), f32),
        in_specs=[HBM, HBM],
        out_specs=VMEM,
        scratch_shapes=[
            source_scratch,
            pltpu.VMEM((3, 3 * channels, channels), bf16),
            padded_scratch,
            pltpu.SemaphoreType.DMA((4,)),
        ],
        compiler_params=params(),
        cost_estimate=conv_cost,
        name="first_conv",
    )(in_hbm(source), in_hbm(conv_first.reshape(3, 3 * channels, channels)))
    temp_parts = []
    if paired:
        shares, inner = ring_gather(shares[0], "frame", frames, inner)
        mine = jnp.concatenate([temp_in, temp_out[None]], axis=0).reshape(4 * height, channels)
        mine, *near = lax.optimization_barrier((mine, *neighbours(shares)))
        shares = with_neighbours(shares, near)
        temp_parts = ring_gather(mine, "frame", frames)
    hidden, normed = pl.pallas_call(
        second_kernel,
        out_shape=[
            jax.ShapeDtypeStruct((tokens, channels), bf16),
            jax.ShapeDtypeStruct((tokens, channels), bf16),
        ],
        in_specs=[HBM] + [VMEM] * (2 + len(shares)),
        out_specs=[VMEM] * 2,
        scratch_shapes=[source_scratch, padded_scratch, pltpu.SemaphoreType.DMA((1,))],
        compiler_params=params(),
        cost_estimate=conv_cost,
        name="second_conv",
    )(in_hbm(source), inner, conv_second.reshape(3, 3 * channels, channels), *shares)
    maps = gather_maps(normed, "video", videos)
    epi_parts = swap(shares, 2 * height, videos) if paired else []
    targets = lax.dynamic_index_in_dim(matchings, video, 1, keepdims=False)
    if is_power(videos):
        select = video ^ targets
    else:
        select = (video - targets) % videos
    mask = lax.dynamic_index_in_dim(tile_mask, video, 1, keepdims=False).reshape(-1)
    square = (4, channels, channels)
    queries, epi = pl.pallas_call(
        query_kernel,
        out_shape=[
            jax.ShapeDtypeStruct((channels, tokens), f32),
            jax.ShapeDtypeStruct(square, bf16),
        ],
        in_specs=[SMEM, VMEM, HBM, HBM] + [VMEM] * len(epi_parts),
        out_specs=[VMEM] * 2,
        scratch_shapes=[pltpu.SemaphoreType.DMA((4,))],
        compiler_params=params(),
        name="query",
    )(places, normed, in_hbm(epi_in), in_hbm(epi_out), *epi_parts)
    if paired:
        queries, *near = lax.optimization_barrier((queries, *neighbours(temp_parts)))
        temp_parts = with_neighbours(temp_parts, near)
    second, blocks = pl.pallas_call(
        functools.partial(view_kernel, videos, tiles),
        out_shape=[jax.ShapeDtypeStruct((tokens, channels), bf16)] * 2,
        in_specs=[SMEM, SMEM, HBM, VMEM, VMEM] + [VMEM] * videos,
        out_specs=[VMEM, VMEM],
        scratch_shapes=[
            pltpu.VMEM((tokens, channels), bf16),
            pltpu.VMEM((channels, tokens), f32),
            pltpu.VMEM((tokens, channels), bf16),
            pltpu.SemaphoreType.DMA,
        ],
        compiler_params=params(),
        name="cross_view",
    )(select, mask, hidden, queries, epi, *maps)

    if paired:
        blocks, *temp_parts = lax.optimization_barrier((blocks, *temp_parts))
        temp_parts = temp_parts[1:]
    arrived = ring_gather(blocks, "frame", frames)
    score_shape = jax.ShapeDtypeStruct((tokens, channels), f32)
    value_shape = jax.ShapeDtypeStruct((tokens, channels), bf16)
    frame_cost = pl.CostEstimate(
        flops=8 * tokens * channels * channels,
        bytes_accessed=8 * channels * channels + 8 * tokens * channels,
        transcendentals=0,
    )
    temp, frame_queries, *first = pl.pallas_call(
        own_frame_kernel,
        out_shape=[jax.ShapeDtypeStruct(square, bf16), value_shape, score_shape, value_shape],
        in_specs=[SMEM, VMEM, HBM, HBM] + [VMEM] * len(temp_parts),
        out_specs=[VMEM] * 4,
        scratch_shapes=[pltpu.SemaphoreType.DMA((4,))],
        compiler_params=params(),
        cost_estimate=frame_cost,
        name="own_frame",
    )(places, blocks, in_hbm(temp_in), in_hbm(temp_out), *temp_parts)
    scores, values = [first[0]], [first[1]]
    order = sorted(range(1, frames), key=lambda k: min(k, frames - k))
    for k in order[:-1]:
        one = pl.pallas_call(
            frame_kernel,
            out_shape=[score_shape, value_shape],
            in_specs=[VMEM] * 3,
            out_specs=[VMEM] * 2,
            compiler_params=params(),
            cost_estimate=frame_cost,
            name="other_frame",
        )(frame_queries, arrived[k], temp)
        scores.append(one[0])
        values.append(one[1])
    denoised = pl.pallas_call(
        functools.partial(last_kernel, frames),
        out_shape=jax.ShapeDtypeStruct((channels, tokens), bf16),
        in_specs=[VMEM] * (2 + 2 * frames),
        out_specs=VMEM,
        compiler_params=params(),
        name="last",
    )(second, frame_queries, arrived[order[-1]], temp, *scores, *values)
    return denoised.T.reshape(1, 1, tokens, channels)


def solution(mesh):
    placed = (
        P(("groups", "video"), "frame", None, None),
        P(("groups", "video")),
        P(None, "groups"),
        P(None, "groups", None, None),
        P(),
        P(),
        P("frame", None),
        P(None, "frame", None),
        P("frame", None),
        P(None, "frame", None),
        P("frame", None),
    )
    return jax.shard_map(
        per_device,
        mesh=mesh,
        in_specs=placed,
        out_specs=P(("groups", "video"), "frame", None, None),
        check_vma=False,
    )
```

```python
import functools
import math

import jax
import jax.numpy as jnp
from jax import lax
from jax.experimental import pallas as pl
from jax.experimental.pallas import tpu as pltpu
from jax.sharding import PartitionSpec as P

HEADS = 8
NORM_GROUPS = 32
TEMB = 1280
H = 8
W = 32

EPSILON = 1e-05
MASKED = -1e30
LOG2E = 1.4426950408889634
SHARE_ROWS = 16

VMEM = pl.BlockSpec(memory_space=pltpu.VMEM)
SMEM = pl.BlockSpec(memory_space=pltpu.SMEM)
HBM = pl.BlockSpec(memory_space=pl.ANY)
f32 = jnp.float32
bf16 = jnp.bfloat16


def params():
    return pltpu.CompilerParams(vmem_limit_bytes=16 * 1024 * 1024)


def in_hbm(x):
    return pltpu.with_memory_space_constraint(x, pltpu.HBM)


def fetch(source, target, sem):
    copy = pltpu.make_async_copy(source, target, sem)
    copy.start()
    return copy


def dot(a, b):
    return jnp.dot(a, b, preferred_element_type=f32)


def block_diagonal(size, width):
    rows = lax.broadcasted_iota(jnp.int32, (size, 1), 0).astype(f32)
    cols = lax.broadcasted_iota(jnp.int32, (1, size), 1).astype(f32)
    rows = jnp.floor((rows + 0.5) * (1.0 / width))
    cols = jnp.floor((cols + 0.5) * (1.0 / width))
    return (rows == cols).astype(f32).astype(bf16)


def terms(row):
    first = row.astype(bf16).astype(f32)
    second = (row - first).astype(bf16).astype(f32)
    third = row - first - second
    index = lax.broadcasted_iota(jnp.int32, (SHARE_ROWS, row.shape[1]), 0)
    return jnp.where(
        index == 0, first, jnp.where(index == 1, second, jnp.where(index == 2, third, 0.0))
    )


def group_sum(row, ones):
    return jnp.sum(dot(terms(row).astype(bf16), ones), axis=0, keepdims=True)


def group_norm_silu(x):
    tokens, channels = x.shape
    width = channels // NORM_GROUPS
    ones = block_diagonal(channels, width)
    inverse = 1.0 / (tokens * width)
    average = group_sum(jnp.sum(x, axis=0, keepdims=True), ones) * inverse
    centred = x - average
    spread = group_sum(jnp.sum(centred * centred, axis=0, keepdims=True), ones) * inverse
    y = centred * lax.rsqrt(spread + EPSILON)
    return y / (1.0 + jnp.exp(-y))


def layer_norm(x):
    inverse = 1.0 / x.shape[1]
    average = jnp.sum(x, axis=1, keepdims=True) * inverse
    centred = x - average
    spread = jnp.sum(centred * centred, axis=1, keepdims=True) * inverse
    return centred * lax.rsqrt(spread + EPSILON)


def convolve(y, weight, padded, copies):
    tokens, channels = y.shape
    column = lax.broadcasted_iota(jnp.int32, (tokens, 1), 0) & (W - 1)
    before = jnp.where(column == 0, 0.0, pltpu.roll(y, 1, 0))
    after = jnp.where(column == W - 1, 0.0, pltpu.roll(y, tokens - 1, 0))
    padded[pl.ds(0, W), :] = jnp.zeros((W, 3 * channels), bf16)
    padded[pl.ds(tokens + W, W), :] = jnp.zeros((W, 3 * channels), bf16)
    padded[pl.ds(W, tokens), :] = jnp.concatenate(
        [before.astype(bf16), y.astype(bf16), after.astype(bf16)], axis=1
    )
    total = None
    for k in range(3):
        if copies:
            copies[k].wait()
        part = dot(padded[pl.ds(k * W, tokens), :], weight[k])
        total = part if total is None else total + part
    return total


def share_kernel(act, proj, share):
    share[...] = dot(act[...], proj[...])


def payload_kernel(side, act, proj_hbm, three, one, payload, proj, sems):
    rows, channels = one.shape
    copy = fetch(proj_hbm, proj, sems.at[0])
    upper, lower = payload.at[pl.ds(0, rows)], payload.at[pl.ds(rows, rows)]

    @pl.when(side[0] == 0)
    def _():
        fetch(three.at[0], upper, sems.at[1])
        fetch(three.at[1], lower, sems.at[2])

    @pl.when(side[0] != 0)
    def _():
        fetch(three.at[2], upper, sems.at[1])
        fetch(one, lower, sems.at[2])

    copy.wait()
    payload[pl.ds(2 * rows, SHARE_ROWS), :] = terms(dot(act[...], proj[...])).astype(bf16)
    pltpu.make_async_copy(one, upper, sems.at[1]).wait()
    pltpu.make_async_copy(one, lower, sems.at[2]).wait()


def first_kernel(source_hbm, weight_hbm, inner, source, weight, padded, sems):
    copy = fetch(source_hbm, source, sems.at[0])
    copies = [fetch(weight_hbm.at[k], weight.at[k], sems.at[1 + k]) for k in range(3)]
    copy.wait()
    inner[...] = convolve(group_norm_silu(source[...].astype(f32).T), weight, padded, copies)


def second_kernel(source_hbm, inner, weight, *refs):
    shares, (hidden, normed, source, padded, sems) = refs[:-5], refs[-5:]
    copy = fetch(source_hbm, source, sems.at[0])
    bias = None
    for share in shares:
        rows = min(SHARE_ROWS, share.shape[0])
        part = jnp.sum(share[pl.ds(share.shape[0] - rows, rows), :].astype(f32), axis=0, keepdims=True)
        bias = part if bias is None else bias + part
    y = group_norm_silu(inner[...] + bias)
    total = convolve(y, weight, padded, [])
    copy.wait()
    rounded = (source[...].astype(f32).T + total).astype(bf16)
    hidden[...] = rounded
    normed[...] = layer_norm(rounded.astype(f32)).astype(bf16)


def fetch_own(where, three, one, whole, sems):
    rows = one.shape[0]
    place = pl.ds(pl.multiple_of(where[0] * rows, 16), rows)
    copies = [fetch(three.at[k], whole.at[k, place], sems.at[k]) for k in range(3)]
    return copies + [fetch(one, whole.at[3, place], sems.at[3])]


def query_kernel(where, normed, three, one, *refs):
    parts, (queries, epi, sems) = refs[:-3], refs[-3:]
    copies = fetch_own(where, three, one, epi, sems)
    rows = one.shape[0]
    count = len(parts) - 1
    for k in range(1, count + 1):
        place = pl.ds(pl.multiple_of(where[k] * rows, 16), rows)
        for j in range(2):
            mine = where[count + 1] * 2 + j
            epi[mine, place, :] = parts[k - 1][pl.ds(j * rows, rows), :]
            start = ((k - 1) * 2 + j) * rows
            epi[2 - mine + 2 * j, place, :] = parts[-1][pl.ds(start, rows), :]
    for copy in copies:
        copy.wait()
    queries[...] = dot(normed[...], epi[0]).astype(bf16).astype(f32).T


def view_kernel(count, tiles, *refs):
    select, mask, hidden_ref, query_ref, weights = refs[:5]
    maps = refs[5 : 5 + count]
    second, blocks, chosen, totals, hidden, sem = refs[5 + count :]
    copy = fetch(hidden_ref, hidden, sem)
    tokens, channels = hidden.shape
    head = channels // HEADS
    width = tokens // tiles
    scale = LOG2E / math.sqrt(head)
    queries = query_ref[...]
    lane_tile = lax.broadcasted_iota(jnp.int32, (1, tokens), 1) // width
    windows = []
    for h in range(HEADS):
        low = h * head // 128 * 128
        high = min(channels, -(-(h + 1) * head // 128) * 128)
        row = lax.broadcasted_iota(jnp.int32, (high - low, 1), 0) + low
        inside = (row >= h * head) & (row < (h + 1) * head)
        windows.append((low, high, jnp.where(inside, queries[low:high], 0.0).astype(bf16)))
    for matching in range(2):
        for j in range(count):

            @pl.when(select[matching] == j)
            def _():
                chosen[...] = maps[j][...]

        other = chosen[...]
        keys = dot(other, weights[1]).astype(bf16)
        values = dot(other, weights[2]).T
        shifts = []
        for j in range(tiles):
            row = jnp.zeros((1, tokens), f32)
            for i in range(tiles):
                bit = mask[(matching * tiles + i) * tiles + j]
                row = jnp.where(lane_tile == i, jnp.where(bit > 0, 0.0, MASKED), row)
            shifts.append(row)
        for h in range(HEADS):
            low, high, wanted = windows[h]
            scores = dot(keys[:, low:high], wanted) * scale
            scores = jnp.concatenate(
                [scores[j * width : (j + 1) * width] + shifts[j] for j in range(tiles)], axis=0
            )
            powers = jnp.exp2(scores - jnp.max(scores, axis=0, keepdims=True))
            norm = 1.0 / jnp.sum(powers, axis=0, keepdims=True)
            part = dot(values[h * head : (h + 1) * head].astype(bf16), powers.astype(bf16)) * norm
            if matching == 0:
                totals[pl.ds(h * head, head), :] = part
            else:
                totals[pl.ds(h * head, head), :] += part
    mixture = totals[...].T.astype(bf16)
    copy.wait()
    result = (hidden[...].astype(f32) + dot(mixture, weights[3])).astype(bf16)
    second[...] = result
    blocks[...] = layer_norm(result.astype(f32)).astype(bf16)


def frame_part(queries, rows, weights):
    channels = rows.shape[1]
    head = channels // HEADS
    ones = block_diagonal(channels, head)
    keys = dot(rows, weights[1]).astype(bf16).astype(f32)
    values = dot(rows, weights[2]).astype(bf16)
    products = queries * keys
    high = products.astype(bf16)
    low = (products - high.astype(f32)).astype(bf16)
    return (dot(high, ones) + dot(low, ones)) * (LOG2E / math.sqrt(head)), values


def own_frame_kernel(where, rows, three, one, *refs):
    parts, (weights, queries, scores, values, sems) = refs[:-5], refs[-5:]
    copies = fetch_own(where, three, one, weights, sems)
    height = one.shape[0]
    for k, part in enumerate(parts):
        place = pl.ds(pl.multiple_of(where[k + 1] * height, 16), height)
        for kind in range(4):
            weights[kind, place, :] = part[pl.ds(kind * height, height), :]
    for copy in copies:
        copy.wait()
    queries[...] = dot(rows[...], weights[0]).astype(bf16)
    scores[...], values[...] = frame_part(queries[...].astype(f32), rows[...], weights)


def frame_kernel(queries, rows, weights, scores, values):
    scores[...], values[...] = frame_part(queries[...].astype(f32), rows[...], weights)


def last_kernel(frames, *refs):
    second, queries, rows, weights = refs[:4]
    scores = refs[4 : 3 + frames]
    values = refs[3 + frames : 2 + 2 * frames]
    out = refs[-1]
    last_scores, last_values = frame_part(queries[...].astype(f32), rows[...], weights)
    every = [ref[...] for ref in scores] + [last_scores]
    most = functools.reduce(jnp.maximum, every)
    powers = [jnp.exp2(one - most) for one in every]
    norm = 1.0 / functools.reduce(jnp.add, powers)
    total = (powers[-1] * norm).astype(bf16).astype(f32) * last_values.astype(f32)
    for power, value in zip(powers, values):
        total += (power * norm).astype(bf16).astype(f32) * value[...].astype(f32)
    result = second[...].astype(f32) + dot(total.astype(bf16), weights[3])
    out[...] = result.T.astype(bf16)


def is_power(n):
    return n & (n - 1) == 0


def partner_permutation(size, k):
    if is_power(size):
        return [(i, i ^ k) for i in range(size)]
    return [(i, (i + k) % size) for i in range(size)]


def partner(me, size, k, sign=1):
    if is_power(size):
        return me ^ k
    return (me + sign * k) % size


def gather_maps(own, axis, size):
    maps = {0: own}
    if is_power(size):
        bit = size // 2
        while bit:
            for k in list(maps):
                maps[k | bit] = lax.ppermute(maps[k], axis, partner_permutation(size, bit))
            bit //= 2
    else:
        for k in range(1, size):
            maps[k] = lax.ppermute(own, axis, partner_permutation(size, k))
    return [maps[k] for k in range(size)]


def sum_over(value, beside, later, axis, size):
    if not is_power(size):
        return lax.psum(value, axis), beside, later
    bit = 1
    while bit < size:
        value = value + lax.ppermute(value, axis, partner_permutation(size, bit))
        if bit == 1:
            value, beside = lax.optimization_barrier((value, beside))
        bit *= 2
    value, later = lax.optimization_barrier((value, later))
    return value, beside, later


def after(x, *others):
    return lax.optimization_barrier((x, *others))[0]


def ring_gather(own, axis, size, beside=None):
    pieces = {0: own}
    right = [(i, (i + 1) % size) for i in range(size)]
    left = [(j, i) for i, j in right]
    for step in range(1, size // 2 + 1):
        pieces[step] = lax.ppermute(pieces[step - 1], axis, right)
        if size - step > step:
            pieces[size - step] = lax.ppermute(pieces[(size - step + 1) % size], axis, left)
        if step == 1 and beside is not None:
            pieces[1] = after(pieces[1], beside)
    return [pieces[k] for k in range(size)]


def swap(pieces, rows, videos):
    joined = jnp.concatenate([piece[:rows] for piece in pieces[1:]], axis=0)
    return pieces[1:] + [lax.ppermute(joined, "video", partner_permutation(videos, 1))]


def per_device(
    latents,
    timesteps,
    matchings,
    tile_mask,
    conv_first,
    conv_second,
    time_proj,
    epi_in,
    epi_out,
    temp_in,
    temp_out,
):
    tokens, channels = latents.shape[2:]
    tiles = tile_mask.shape[2]
    frames = lax.axis_size("frame")
    videos = lax.axis_size("video")
    frame = lax.axis_index("frame")
    video = lax.axis_index("video")
    pixels = tokens // frames
    source = latents.reshape(tokens, channels).T

    rows = time_proj.shape[0]
    half = rows * frames // 2
    index = frame * rows + jnp.arange(rows, dtype=jnp.int32)
    exponent = jnp.where(index < half, index, index - half).astype(f32)
    frequency = jnp.exp(-math.log(10000.0) * exponent / half)
    angles = timesteps.astype(f32)[:, None] * frequency[None, :]
    wave = jnp.where(index[None, :] < half, jnp.cos(angles), jnp.sin(angles))
    time_act = jax.nn.silu(wave).astype(bf16)
    height = epi_out.shape[0]
    paired = videos % 2 == 0 and is_power(videos) and height % 16 == 0
    early = pl.CostEstimate(flops=10**10, bytes_accessed=1 << 20, transcendentals=0)
    if paired:
        side = (video % 2).astype(jnp.int32).reshape(1)
        payload = pl.pallas_call(
            payload_kernel,
            out_shape=jax.ShapeDtypeStruct((2 * height + SHARE_ROWS, channels), bf16),
            in_specs=[SMEM, VMEM, HBM, HBM, HBM],
            out_specs=VMEM,
            scratch_shapes=[
                pltpu.VMEM(time_proj.shape, bf16),
                pltpu.SemaphoreType.DMA((3,)),
            ],
            compiler_params=params(),
            cost_estimate=early,
            name="payload",
        )(side, time_act, in_hbm(time_proj), in_hbm(epi_in), in_hbm(epi_out))
        shares = [payload]
        places = [(frame - k) % frames for k in range(frames)] + [video % 2]
    else:
        share = pl.pallas_call(
            share_kernel,
            out_shape=jax.ShapeDtypeStruct((1, channels), f32),
            in_specs=[VMEM, VMEM],
            out_specs=VMEM,
            compiler_params=params(),
            cost_estimate=early,
            name="time_share",
        )(time_act, time_proj)
        shares = [lax.psum(share, "frame")]
        places = [jnp.int32(0)] * 2
        epi_in = lax.all_gather(epi_in, "frame", axis=1, tiled=True)
        epi_out = lax.all_gather(epi_out, "frame", axis=0, tiled=True)
        temp_in = lax.all_gather(temp_in, "frame", axis=1, tiled=True)
        temp_out = lax.all_gather(temp_out, "frame", axis=0, tiled=True)
    places = jnp.stack(places).astype(jnp.int32)

    source_scratch = pltpu.VMEM((channels, tokens), bf16)
    padded_scratch = pltpu.VMEM((tokens + 2 * W, 3 * channels), bf16)
    conv_cost = pl.CostEstimate(
        flops=2 * 9 * tokens * channels * channels,
        bytes_accessed=2 * 9 * channels * channels + 8 * tokens * channels,
        transcendentals=tokens * channels,
    )
    inner = pl.pallas_call(
        first_kernel,
        out_shape=jax.ShapeDtypeStruct((tokens, channels), f32),
        in_specs=[HBM, HBM],
        out_specs=VMEM,
        scratch_shapes=[
            source_scratch,
            pltpu.VMEM((3, 3 * channels, channels), bf16),
            padded_scratch,
            pltpu.SemaphoreType.DMA((4,)),
        ],
        compiler_params=params(),
        cost_estimate=conv_cost,
        name="first_conv",
    )(in_hbm(source), in_hbm(conv_first.reshape(3, 3 * channels, channels)))
    temp_parts = []
    if paired:
        shares = ring_gather(shares[0], "frame", frames, inner)
    hidden, normed = pl.pallas_call(
        second_kernel,
        out_shape=[
            jax.ShapeDtypeStruct((tokens, channels), bf16),
            jax.ShapeDtypeStruct((tokens, channels), bf16),
        ],
        in_specs=[HBM] + [VMEM] * (2 + len(shares)),
        out_specs=[VMEM] * 2,
        scratch_shapes=[source_scratch, padded_scratch, pltpu.SemaphoreType.DMA((1,))],
        compiler_params=params(),
        cost_estimate=conv_cost,
        name="second_conv",
    )(in_hbm(source), inner, conv_second.reshape(3, 3 * channels, channels), *shares)
    maps = gather_maps(normed, "video", videos)
    epi_parts = swap(shares, 2 * height, videos) if paired else []
    targets = lax.dynamic_index_in_dim(matchings, video, 1, keepdims=False)
    if is_power(videos):
        select = video ^ targets
    else:
        select = (video - targets) % videos
    mask = lax.dynamic_index_in_dim(tile_mask, video, 1, keepdims=False).reshape(-1)
    square = (4, channels, channels)
    queries, epi = pl.pallas_call(
        query_kernel,
        out_shape=[
            jax.ShapeDtypeStruct((channels, tokens), f32),
            jax.ShapeDtypeStruct(square, bf16),
        ],
        in_specs=[SMEM, VMEM, HBM, HBM] + [VMEM] * len(epi_parts),
        out_specs=[VMEM] * 2,
        scratch_shapes=[pltpu.SemaphoreType.DMA((4,))],
        compiler_params=params(),
        name="query",
    )(places, normed, in_hbm(epi_in), in_hbm(epi_out), *epi_parts)
    second, blocks = pl.pallas_call(
        functools.partial(view_kernel, videos, tiles),
        out_shape=[jax.ShapeDtypeStruct((tokens, channels), bf16)] * 2,
        in_specs=[SMEM, SMEM, HBM, VMEM, VMEM] + [VMEM] * videos,
        out_specs=[VMEM, VMEM],
        scratch_shapes=[
            pltpu.VMEM((tokens, channels), bf16),
            pltpu.VMEM((channels, tokens), f32),
            pltpu.VMEM((tokens, channels), bf16),
            pltpu.SemaphoreType.DMA,
        ],
        compiler_params=params(),
        name="cross_view",
    )(select, mask, hidden, queries, epi, *maps)

    if paired:
        mine = jnp.concatenate([temp_in, temp_out[None]], axis=0).reshape(4 * height, channels)
        temp_parts = ring_gather(after(mine, maps[videos // 2]), "frame", frames, blocks)[1:]
        blocks = after(blocks, temp_parts[-1])
    arrived = ring_gather(blocks, "frame", frames)
    score_shape = jax.ShapeDtypeStruct((tokens, channels), f32)
    value_shape = jax.ShapeDtypeStruct((tokens, channels), bf16)
    frame_cost = pl.CostEstimate(
        flops=8 * tokens * channels * channels,
        bytes_accessed=8 * channels * channels + 8 * tokens * channels,
        transcendentals=0,
    )
    temp, frame_queries, *first = pl.pallas_call(
        own_frame_kernel,
        out_shape=[jax.ShapeDtypeStruct(square, bf16), value_shape, score_shape, value_shape],
        in_specs=[SMEM, VMEM, HBM, HBM] + [VMEM] * len(temp_parts),
        out_specs=[VMEM] * 4,
        scratch_shapes=[pltpu.SemaphoreType.DMA((4,))],
        compiler_params=params(),
        cost_estimate=frame_cost,
        name="own_frame",
    )(places, blocks, in_hbm(temp_in), in_hbm(temp_out), *temp_parts)
    scores, values = [first[0]], [first[1]]
    order = sorted(range(1, frames), key=lambda k: min(k, frames - k))
    for k in order[:-1]:
        one = pl.pallas_call(
            frame_kernel,
            out_shape=[score_shape, value_shape],
            in_specs=[VMEM] * 3,
            out_specs=[VMEM] * 2,
            compiler_params=params(),
            cost_estimate=frame_cost,
            name="other_frame",
        )(frame_queries, arrived[k], temp)
        scores.append(one[0])
        values.append(one[1])
    denoised = pl.pallas_call(
        functools.partial(last_kernel, frames),
        out_shape=jax.ShapeDtypeStruct((channels, tokens), bf16),
        in_specs=[VMEM] * (2 + 2 * frames),
        out_specs=VMEM,
        compiler_params=params(),
        name="last",
    )(second, frame_queries, arrived[order[-1]], temp, *scores, *values)
    return denoised.T.reshape(1, 1, tokens, channels)


def solution(mesh):
    placed = (
        P(("groups", "video"), "frame", None, None),
        P(("groups", "video")),
        P(None, "groups"),
        P(None, "groups", None, None),
        P(),
        P(),
        P("frame", None),
        P(None, "frame", None),
        P("frame", None),
        P(None, "frame", None),
        P("frame", None),
    )
    return jax.shard_map(
        per_device,
        mesh=mesh,
        in_specs=placed,
        out_specs=P(("groups", "video"), "frame", None, None),
        check_vma=False,
    )
```

```python
import functools
import math

import jax
import jax.numpy as jnp
from jax import lax
from jax.experimental import pallas as pl
from jax.experimental.pallas import tpu as pltpu
from jax.sharding import PartitionSpec as P

HEADS = 8
NORM_GROUPS = 32
TEMB = 1280
H = 8
W = 32

EPSILON = 1e-05
MASKED = -1e30
LOG2E = 1.4426950408889634
SHARE_ROWS = 16

VMEM = pl.BlockSpec(memory_space=pltpu.VMEM)
SMEM = pl.BlockSpec(memory_space=pltpu.SMEM)
HBM = pl.BlockSpec(memory_space=pl.ANY)
f32 = jnp.float32
bf16 = jnp.bfloat16


def params():
    return pltpu.CompilerParams(vmem_limit_bytes=16 * 1024 * 1024)


def in_hbm(x):
    return pltpu.with_memory_space_constraint(x, pltpu.HBM)


def fetch(source, target, sem):
    copy = pltpu.make_async_copy(source, target, sem)
    copy.start()
    return copy


def dot(a, b):
    return jnp.dot(a, b, preferred_element_type=f32)


def block_diagonal(size, width):
    rows = lax.broadcasted_iota(jnp.int32, (size, 1), 0).astype(f32)
    cols = lax.broadcasted_iota(jnp.int32, (1, size), 1).astype(f32)
    rows = jnp.floor((rows + 0.5) * (1.0 / width))
    cols = jnp.floor((cols + 0.5) * (1.0 / width))
    return (rows == cols).astype(f32).astype(bf16)


def terms(row):
    first = row.astype(bf16).astype(f32)
    second = (row - first).astype(bf16).astype(f32)
    third = row - first - second
    index = lax.broadcasted_iota(jnp.int32, (SHARE_ROWS, row.shape[1]), 0)
    return jnp.where(
        index == 0, first, jnp.where(index == 1, second, jnp.where(index == 2, third, 0.0))
    )


def group_sum(row, ones):
    return jnp.sum(dot(terms(row).astype(bf16), ones), axis=0, keepdims=True)


def group_norm_silu(x):
    tokens, channels = x.shape
    width = channels // NORM_GROUPS
    ones = block_diagonal(channels, width)
    inverse = 1.0 / (tokens * width)
    average = group_sum(jnp.sum(x, axis=0, keepdims=True), ones) * inverse
    centred = x - average
    spread = group_sum(jnp.sum(centred * centred, axis=0, keepdims=True), ones) * inverse
    y = centred * lax.rsqrt(spread + EPSILON)
    return y / (1.0 + jnp.exp(-y))


def layer_norm(x):
    inverse = 1.0 / x.shape[1]
    average = jnp.sum(x, axis=1, keepdims=True) * inverse
    centred = x - average
    spread = jnp.sum(centred * centred, axis=1, keepdims=True) * inverse
    return centred * lax.rsqrt(spread + EPSILON)


def convolve(y, weight, padded, copies):
    tokens, channels = y.shape
    column = lax.broadcasted_iota(jnp.int32, (tokens, 1), 0) & (W - 1)
    before = jnp.where(column == 0, 0.0, pltpu.roll(y, 1, 0))
    after = jnp.where(column == W - 1, 0.0, pltpu.roll(y, tokens - 1, 0))
    padded[pl.ds(0, W), :] = jnp.zeros((W, 3 * channels), bf16)
    padded[pl.ds(tokens + W, W), :] = jnp.zeros((W, 3 * channels), bf16)
    padded[pl.ds(W, tokens), :] = jnp.concatenate(
        [before.astype(bf16), y.astype(bf16), after.astype(bf16)], axis=1
    )
    total = None
    for k in range(3):
        if copies:
            copies[k].wait()
        part = dot(padded[pl.ds(k * W, tokens), :], weight[k])
        total = part if total is None else total + part
    return total


def share_kernel(act, proj_hbm, share, proj, sem):
    fetch(proj_hbm, proj, sem).wait()
    share[...] = dot(act[...], proj[...])


def first_kernel(source_hbm, weight_hbm, inner, turned, source, weight, padded, sems):
    copy = fetch(source_hbm, source, sems.at[0])
    copies = [fetch(weight_hbm.at[k], weight.at[k], sems.at[1 + k]) for k in range(3)]
    copy.wait()
    rows = source[...].astype(f32).T
    turned[...] = rows.astype(bf16)
    inner[...] = convolve(group_norm_silu(rows), weight, padded, copies)


def second_kernel(source, inner, bias, weight, hidden, normed, padded):
    y = group_norm_silu(inner[...] + bias[...])
    total = convolve(y, weight, padded, [])
    rounded = (source[...].astype(f32) + total).astype(bf16)
    hidden[...] = rounded
    normed[...] = layer_norm(rounded.astype(f32)).astype(bf16)


def fetch_own(where, three, one, whole, sems):
    rows = one.shape[0]
    place = pl.ds(pl.multiple_of(where[0] * rows, 16), rows)
    copies = [fetch(three.at[k], whole.at[k, place], sems.at[k]) for k in range(3)]
    return copies + [fetch(one, whole.at[3, place], sems.at[3])]


def assemble(where, side, parts, whole, rows):
    for k, part in enumerate(parts[:-1]):
        place = pl.ds(pl.multiple_of(where[k + 1] * rows, 16), rows)
        for j in range(2):
            mine = side * 2 + j
            whole[mine, place, :] = part[pl.ds(j * rows, rows), :]
            whole[2 - mine + 2 * j, place, :] = parts[-1][pl.ds((2 * k + j) * rows, rows), :]


def query_kernel(where, normed, three, one, *refs):
    parts, (queries, epi, sems) = refs[:-3], refs[-3:]
    copies = fetch_own(where, three, one, epi, sems)
    assemble(where, where[max(1, len(parts))], parts, epi, one.shape[0])
    for copy in copies:
        copy.wait()
    queries[...] = dot(normed[...], epi[0]).astype(bf16).astype(f32).T


def view_kernel(count, tiles, *refs):
    select, mask, hidden_ref, query_ref, weights = refs[:5]
    maps = refs[5 : 5 + count]
    second, blocks, chosen, totals, hidden, sem = refs[5 + count :]
    copy = fetch(hidden_ref, hidden, sem)
    tokens, channels = hidden.shape
    head = channels // HEADS
    width = tokens // tiles
    scale = LOG2E / math.sqrt(head)
    queries = query_ref[...]
    lane_tile = lax.broadcasted_iota(jnp.int32, (1, tokens), 1) // width
    windows = []
    for h in range(HEADS):
        low = h * head // 128 * 128
        high = min(channels, -(-(h + 1) * head // 128) * 128)
        row = lax.broadcasted_iota(jnp.int32, (high - low, 1), 0) + low
        inside = (row >= h * head) & (row < (h + 1) * head)
        windows.append((low, high, jnp.where(inside, queries[low:high], 0.0).astype(bf16)))
    for matching in range(2):
        for j in range(count):

            @pl.when(select[matching] == j)
            def _():
                chosen[...] = maps[j][...]

        other = chosen[...]
        keys = dot(other, weights[1]).astype(bf16)
        values = dot(other, weights[2]).T
        shifts = []
        for j in range(tiles):
            row = jnp.zeros((1, tokens), f32)
            for i in range(tiles):
                bit = mask[(matching * tiles + i) * tiles + j]
                row = jnp.where(lane_tile == i, jnp.where(bit > 0, 0.0, MASKED), row)
            shifts.append(row)
        for h in range(HEADS):
            low, high, wanted = windows[h]
            scores = dot(keys[:, low:high], wanted) * scale
            scores = jnp.concatenate(
                [scores[j * width : (j + 1) * width] + shifts[j] for j in range(tiles)], axis=0
            )
            powers = jnp.exp2(scores - jnp.max(scores, axis=0, keepdims=True))
            norm = 1.0 / jnp.sum(powers, axis=0, keepdims=True)
            part = dot(values[h * head : (h + 1) * head].astype(bf16), powers.astype(bf16)) * norm
            if matching == 0:
                totals[pl.ds(h * head, head), :] = part
            else:
                totals[pl.ds(h * head, head), :] += part
    mixture = totals[...].T.astype(bf16)
    copy.wait()
    result = (hidden[...].astype(f32) + dot(mixture, weights[3])).astype(bf16)
    second[...] = result
    blocks[...] = layer_norm(result.astype(f32)).astype(bf16)


def frame_part(queries, rows, weights):
    channels = rows.shape[1]
    head = channels // HEADS
    ones = block_diagonal(channels, head)
    keys = dot(rows, weights[1]).astype(bf16).astype(f32)
    values = dot(rows, weights[2]).astype(bf16)
    products = queries * keys
    high = products.astype(bf16)
    low = (products - high.astype(f32)).astype(bf16)
    return (dot(high, ones) + dot(low, ones)) * (LOG2E / math.sqrt(head)), values


def own_frame_kernel(where, rows, three, one, *refs):
    parts, (weights, queries, scores, values, sems) = refs[:-5], refs[-5:]
    copies = fetch_own(where, three, one, weights, sems)
    assemble(where, where[max(1, len(parts))], parts, weights, one.shape[0])
    for copy in copies:
        copy.wait()
    queries[...] = dot(rows[...], weights[0]).astype(bf16)
    scores[...], values[...] = frame_part(queries[...].astype(f32), rows[...], weights)


def frame_kernel(queries, rows, weights, scores, values):
    scores[...], values[...] = frame_part(queries[...].astype(f32), rows[...], weights)


def last_kernel(frames, *refs):
    second, queries, rows, weights = refs[:4]
    scores = refs[4 : 3 + frames]
    values = refs[3 + frames : 2 + 2 * frames]
    out = refs[-1]
    last_scores, last_values = frame_part(queries[...].astype(f32), rows[...], weights)
    every = [ref[...] for ref in scores] + [last_scores]
    most = functools.reduce(jnp.maximum, every)
    powers = [jnp.exp2(one - most) for one in every]
    norm = 1.0 / functools.reduce(jnp.add, powers)
    total = (powers[-1] * norm).astype(bf16).astype(f32) * last_values.astype(f32)
    for power, value in zip(powers, values):
        total += (power * norm).astype(bf16).astype(f32) * value[...].astype(f32)
    result = second[...].astype(f32) + dot(total.astype(bf16), weights[3])
    out[...] = result.T.astype(bf16)


def is_power(n):
    return n & (n - 1) == 0


def partner_permutation(size, k):
    if is_power(size):
        return [(i, i ^ k) for i in range(size)]
    return [(i, (i + k) % size) for i in range(size)]


def partner(me, size, k, sign=1):
    if is_power(size):
        return me ^ k
    return (me + sign * k) % size


def gather_maps(own, axis, size):
    maps = {0: own}
    if is_power(size):
        bit = size // 2
        while bit:
            for k in list(maps):
                maps[k | bit] = lax.ppermute(maps[k], axis, partner_permutation(size, bit))
            bit //= 2
    else:
        for k in range(1, size):
            maps[k] = lax.ppermute(own, axis, partner_permutation(size, k))
    return [maps[k] for k in range(size)]


def sum_over(value, axis, size):
    if not is_power(size):
        return lax.psum(value, axis)
    bit = 1
    while bit < size:
        value = value + lax.ppermute(value, axis, partner_permutation(size, bit))
        bit *= 2
    return value


def after(x, *others):
    return lax.optimization_barrier((x, *others))[0]


def ring_gather(own, axis, size, beside=None):
    pieces = {0: own}
    right = [(i, (i + 1) % size) for i in range(size)]
    left = [(j, i) for i, j in right]
    for step in range(1, size // 2 + 1):
        pieces[step] = lax.ppermute(pieces[step - 1], axis, right)
        if size - step > step:
            pieces[size - step] = lax.ppermute(pieces[(size - step + 1) % size], axis, left)
        if step == 1 and beside is not None:
            pieces[1] = after(pieces[1], beside)
    return [pieces[k] for k in range(size)]


def half_of(three, one, side):
    whole = jnp.concatenate([three, one[None]], axis=0)
    whole = whole.reshape(2, 2 * one.shape[0], one.shape[1])
    return lax.dynamic_index_in_dim(whole, side, 0, keepdims=False)


def swap(pieces, videos):
    joined = jnp.concatenate(pieces[1:], axis=0)
    return pieces[1:] + [lax.ppermute(joined, "video", partner_permutation(videos, 1))]


def per_device(
    latents,
    timesteps,
    matchings,
    tile_mask,
    conv_first,
    conv_second,
    time_proj,
    epi_in,
    epi_out,
    temp_in,
    temp_out,
):
    tokens, channels = latents.shape[2:]
    tiles = tile_mask.shape[2]
    frames = lax.axis_size("frame")
    videos = lax.axis_size("video")
    frame = lax.axis_index("frame")
    video = lax.axis_index("video")
    pixels = tokens // frames
    source = latents.reshape(tokens, channels).T

    rows = time_proj.shape[0]
    half = rows * frames // 2
    index = frame * rows + jnp.arange(rows, dtype=jnp.int32)
    exponent = jnp.where(index < half, index, index - half).astype(f32)
    frequency = jnp.exp(-math.log(10000.0) * exponent / half)
    angles = timesteps.astype(f32)[:, None] * frequency[None, :]
    wave = jnp.where(index[None, :] < half, jnp.cos(angles), jnp.sin(angles))
    time_act = jax.nn.silu(wave).astype(bf16)
    height = epi_out.shape[0]
    paired = videos % 2 == 0 and is_power(videos) and height % 16 == 0
    early = pl.CostEstimate(flops=10**10, bytes_accessed=1 << 20, transcendentals=0)
    share = pl.pallas_call(
        share_kernel,
        out_shape=jax.ShapeDtypeStruct((1, channels), f32),
        in_specs=[VMEM, HBM],
        out_specs=VMEM,
        scratch_shapes=[pltpu.VMEM(time_proj.shape, bf16), pltpu.SemaphoreType.DMA],
        compiler_params=params(),
        cost_estimate=early,
        name="time_share",
    )(time_act, in_hbm(time_proj))
    bias = sum_over(share, "frame", frames)
    if paired:
        steps = [frame - k for k in range(frames)]
        places = [step % frames for step in steps] + [video % 2]
    else:
        places = [jnp.int32(0)] * 2
        epi_in = lax.all_gather(epi_in, "frame", axis=1, tiled=True)
        epi_out = lax.all_gather(epi_out, "frame", axis=0, tiled=True)
        temp_in = lax.all_gather(temp_in, "frame", axis=1, tiled=True)
        temp_out = lax.all_gather(temp_out, "frame", axis=0, tiled=True)
    places = jnp.stack(places).astype(jnp.int32)
    temp_places = places
    if paired:
        temp_places = [partner(frame, frames, k, -1) for k in range(frames)] + [video % 2]
        temp_places = jnp.stack(temp_places).astype(jnp.int32)

    source_scratch = pltpu.VMEM((channels, tokens), bf16)
    padded_scratch = pltpu.VMEM((tokens + 2 * W, 3 * channels), bf16)
    conv_cost = pl.CostEstimate(
        flops=2 * 9 * tokens * channels * channels,
        bytes_accessed=2 * 9 * channels * channels + 8 * tokens * channels,
        transcendentals=tokens * channels,
    )
    inner, turned = pl.pallas_call(
        first_kernel,
        out_shape=[
            jax.ShapeDtypeStruct((tokens, channels), f32),
            jax.ShapeDtypeStruct((tokens, channels), bf16),
        ],
        in_specs=[HBM, HBM],
        out_specs=[VMEM, VMEM],
        scratch_shapes=[
            source_scratch,
            pltpu.VMEM((3, 3 * channels, channels), bf16),
            padded_scratch,
            pltpu.SemaphoreType.DMA((4,)),
        ],
        compiler_params=params(),
        cost_estimate=conv_cost,
        name="first_conv",
    )(in_hbm(source), in_hbm(conv_first.reshape(3, 3 * channels, channels)))
    hidden, normed = pl.pallas_call(
        second_kernel,
        out_shape=[
            jax.ShapeDtypeStruct((tokens, channels), bf16),
            jax.ShapeDtypeStruct((tokens, channels), bf16),
        ],
        in_specs=[VMEM] * 4,
        out_specs=[VMEM] * 2,
        scratch_shapes=[padded_scratch],
        compiler_params=params(),
        cost_estimate=conv_cost,
        name="second_conv",
    )(turned, inner, bias, conv_second.reshape(3, 3 * channels, channels))
    if paired:
        mine = half_of(epi_in, epi_out, video % 2)
        epi_parts = ring_gather(after(mine, bias), "frame", frames, normed)
        normed = after(normed, epi_parts[-1])
    maps = gather_maps(normed, "video", videos)
    epi_parts = swap(epi_parts, videos) if paired else []
    temp_parts = []
    if paired:
        mine = after(half_of(temp_in, temp_out, video % 2), maps[1])
        temp_parts = [mine] + [
            lax.ppermute(mine, "frame", partner_permutation(frames, k)) for k in range(1, frames)
        ]
    targets = lax.dynamic_index_in_dim(matchings, video, 1, keepdims=False)
    if is_power(videos):
        select = video ^ targets
    else:
        select = (video - targets) % videos
    mask = lax.dynamic_index_in_dim(tile_mask, video, 1, keepdims=False).reshape(-1)
    square = (4, channels, channels)
    queries, epi = pl.pallas_call(
        query_kernel,
        out_shape=[
            jax.ShapeDtypeStruct((channels, tokens), f32),
            jax.ShapeDtypeStruct(square, bf16),
        ],
        in_specs=[SMEM, VMEM, HBM, HBM] + [VMEM] * len(epi_parts),
        out_specs=[VMEM] * 2,
        scratch_shapes=[pltpu.SemaphoreType.DMA((4,))],
        compiler_params=params(),
        name="query",
    )(places, normed, in_hbm(epi_in), in_hbm(epi_out), *epi_parts)
    second, blocks = pl.pallas_call(
        functools.partial(view_kernel, videos, tiles),
        out_shape=[jax.ShapeDtypeStruct((tokens, channels), bf16)] * 2,
        in_specs=[SMEM, SMEM, HBM, VMEM, VMEM] + [VMEM] * videos,
        out_specs=[VMEM, VMEM],
        scratch_shapes=[
            pltpu.VMEM((tokens, channels), bf16),
            pltpu.VMEM((channels, tokens), f32),
            pltpu.VMEM((tokens, channels), bf16),
            pltpu.SemaphoreType.DMA,
        ],
        compiler_params=params(),
        name="cross_view",
    )(select, mask, hidden, queries, epi, *maps)

    if paired:
        held = [after(part, blocks) for part in temp_parts]
        blocks = after(blocks, *temp_parts)
        temp_parts = swap(held, videos)
    arrived = ring_gather(blocks, "frame", frames)
    score_shape = jax.ShapeDtypeStruct((tokens, channels), f32)
    value_shape = jax.ShapeDtypeStruct((tokens, channels), bf16)
    frame_cost = pl.CostEstimate(
        flops=8 * tokens * channels * channels,
        bytes_accessed=8 * channels * channels + 8 * tokens * channels,
        transcendentals=0,
    )
    temp, frame_queries, *first = pl.pallas_call(
        own_frame_kernel,
        out_shape=[jax.ShapeDtypeStruct(square, bf16), value_shape, score_shape, value_shape],
        in_specs=[SMEM, VMEM, HBM, HBM] + [VMEM] * len(temp_parts),
        out_specs=[VMEM] * 4,
        scratch_shapes=[pltpu.SemaphoreType.DMA((4,))],
        compiler_params=params(),
        cost_estimate=frame_cost,
        name="own_frame",
    )(temp_places, blocks, in_hbm(temp_in), in_hbm(temp_out), *temp_parts)
    scores, values = [first[0]], [first[1]]
    order = sorted(range(1, frames), key=lambda k: min(k, frames - k))
    for k in order[:-1]:
        one = pl.pallas_call(
            frame_kernel,
            out_shape=[score_shape, value_shape],
            in_specs=[VMEM] * 3,
            out_specs=[VMEM] * 2,
            compiler_params=params(),
            cost_estimate=frame_cost,
            name="other_frame",
        )(frame_queries, arrived[k], temp)
        scores.append(one[0])
        values.append(one[1])
    denoised = pl.pallas_call(
        functools.partial(last_kernel, frames),
        out_shape=jax.ShapeDtypeStruct((channels, tokens), bf16),
        in_specs=[VMEM] * (2 + 2 * frames),
        out_specs=VMEM,
        compiler_params=params(),
        name="last",
    )(second, frame_queries, arrived[order[-1]], temp, *scores, *values)
    return denoised.T.reshape(1, 1, tokens, channels)


def solution(mesh):
    placed = (
        P(("groups", "video"), "frame", None, None),
        P(("groups", "video")),
        P(None, "groups"),
        P(None, "groups", None, None),
        P(),
        P(),
        P("frame", None),
        P(None, "frame", None),
        P("frame", None),
        P(None, "frame", None),
        P("frame", None),
    )
    return jax.shard_map(
        per_device,
        mesh=mesh,
        in_specs=placed,
        out_specs=P(("groups", "video"), "frame", None, None),
        check_vma=False,
    )
```

```python
import functools
import math

import jax
import jax.numpy as jnp
from jax import lax
from jax.experimental import pallas as pl
from jax.experimental.pallas import tpu as pltpu
from jax.sharding import PartitionSpec as P

HEADS = 8
NORM_GROUPS = 32
TEMB = 1280
H = 8
W = 32

EPSILON = 1e-05
MASKED = -1e30
LOG2E = 1.4426950408889634
SHARE_ROWS = 16

VMEM = pl.BlockSpec(memory_space=pltpu.VMEM)
SMEM = pl.BlockSpec(memory_space=pltpu.SMEM)
HBM = pl.BlockSpec(memory_space=pl.ANY)
f32 = jnp.float32
bf16 = jnp.bfloat16


def params():
    return pltpu.CompilerParams(vmem_limit_bytes=16 * 1024 * 1024)


def in_hbm(x):
    return pltpu.with_memory_space_constraint(x, pltpu.HBM)


def fetch(source, target, sem):
    copy = pltpu.make_async_copy(source, target, sem)
    copy.start()
    return copy


def dot(a, b):
    return jnp.dot(a, b, preferred_element_type=f32)


def block_diagonal(size, width):
    rows = lax.broadcasted_iota(jnp.int32, (size, 1), 0).astype(f32)
    cols = lax.broadcasted_iota(jnp.int32, (1, size), 1).astype(f32)
    rows = jnp.floor((rows + 0.5) * (1.0 / width))
    cols = jnp.floor((cols + 0.5) * (1.0 / width))
    return (rows == cols).astype(f32).astype(bf16)


def terms(row):
    first = row.astype(bf16).astype(f32)
    second = (row - first).astype(bf16).astype(f32)
    third = row - first - second
    index = lax.broadcasted_iota(jnp.int32, (SHARE_ROWS, row.shape[1]), 0)
    return jnp.where(
        index == 0, first, jnp.where(index == 1, second, jnp.where(index == 2, third, 0.0))
    )


def group_sum(row, ones):
    return jnp.sum(dot(terms(row).astype(bf16), ones), axis=0, keepdims=True)


def group_norm_silu(x):
    tokens, channels = x.shape
    width = channels // NORM_GROUPS
    ones = block_diagonal(channels, width)
    inverse = 1.0 / (tokens * width)
    average = group_sum(jnp.sum(x, axis=0, keepdims=True), ones) * inverse
    centred = x - average
    spread = group_sum(jnp.sum(centred * centred, axis=0, keepdims=True), ones) * inverse
    y = centred * lax.rsqrt(spread + EPSILON)
    return y / (1.0 + jnp.exp(-y))


def layer_norm(x):
    inverse = 1.0 / x.shape[1]
    average = jnp.sum(x, axis=1, keepdims=True) * inverse
    centred = x - average
    spread = jnp.sum(centred * centred, axis=1, keepdims=True) * inverse
    return centred * lax.rsqrt(spread + EPSILON)


def convolve(y, weight, padded, copies):
    tokens, channels = y.shape
    column = lax.broadcasted_iota(jnp.int32, (tokens, 1), 0) & (W - 1)
    before = jnp.where(column == 0, 0.0, pltpu.roll(y, 1, 0))
    after = jnp.where(column == W - 1, 0.0, pltpu.roll(y, tokens - 1, 0))
    padded[pl.ds(0, W), :] = jnp.zeros((W, 3 * channels), bf16)
    padded[pl.ds(tokens + W, W), :] = jnp.zeros((W, 3 * channels), bf16)
    padded[pl.ds(W, tokens), :] = jnp.concatenate(
        [before.astype(bf16), y.astype(bf16), after.astype(bf16)], axis=1
    )
    total = None
    for k in range(3):
        if copies:
            copies[k].wait()
        part = dot(padded[pl.ds(k * W, tokens), :], weight[k])
        total = part if total is None else total + part
    return total


def share_kernel(act, proj_hbm, share, proj, sem):
    fetch(proj_hbm, proj, sem).wait()
    share[...] = dot(act[...], proj[...])


def first_kernel(source_hbm, weight_hbm, inner, turned, source, weight, padded, sems):
    copy = fetch(source_hbm, source, sems.at[0])
    copies = [fetch(weight_hbm.at[k], weight.at[k], sems.at[1 + k]) for k in range(3)]
    copy.wait()
    rows = source[...].astype(f32).T
    turned[...] = rows.astype(bf16)
    inner[...] = convolve(group_norm_silu(rows), weight, padded, copies)


def second_kernel(source, inner, bias, weight, hidden, normed, padded):
    y = group_norm_silu(inner[...] + bias[...])
    total = convolve(y, weight, padded, [])
    rounded = (source[...].astype(f32) + total).astype(bf16)
    hidden[...] = rounded
    normed[...] = layer_norm(rounded.astype(f32)).astype(bf16)


def fetch_own(where, three, one, whole, sems):
    rows = one.shape[0]
    place = pl.ds(pl.multiple_of(where[0] * rows, 16), rows)
    copies = [fetch(three.at[k], whole.at[k, place], sems.at[k]) for k in range(3)]
    return copies + [fetch(one, whole.at[3, place], sems.at[3])]


def assemble(where, side, parts, whole, rows, first):
    for k, part in enumerate(parts[:-1]):
        place = pl.ds(pl.multiple_of(where[k + 1] * rows, 16), rows)
        for j in range(2):
            mine = side * 2 + j
            whole[mine, place, :] = part[pl.ds((first + j) * rows, rows), :]
            start = (2 * k + j) * rows
            whole[2 - mine + 2 * j, place, :] = parts[-1][pl.ds(start, rows), :]


def query_kernel(where, normed, three, one, *refs):
    parts, (queries, epi, sems) = refs[:-3], refs[-3:]
    copies = fetch_own(where, three, one, epi, sems)
    assemble(where, where[max(1, len(parts))], parts, epi, one.shape[0], 0)
    for copy in copies:
        copy.wait()
    queries[...] = dot(normed[...], epi[0]).astype(bf16).astype(f32).T


def view_kernel(count, tiles, *refs):
    select, mask, hidden_ref, query_ref, weights = refs[:5]
    maps = refs[5 : 5 + count]
    second, blocks, chosen, totals, hidden, sem = refs[5 + count :]
    copy = fetch(hidden_ref, hidden, sem)
    tokens, channels = hidden.shape
    head = channels // HEADS
    width = tokens // tiles
    scale = LOG2E / math.sqrt(head)
    queries = query_ref[...]
    lane_tile = lax.broadcasted_iota(jnp.int32, (1, tokens), 1) // width
    windows = []
    for h in range(HEADS):
        low = h * head // 128 * 128
        high = min(channels, -(-(h + 1) * head // 128) * 128)
        row = lax.broadcasted_iota(jnp.int32, (high - low, 1), 0) + low
        inside = (row >= h * head) & (row < (h + 1) * head)
        windows.append((low, high, jnp.where(inside, queries[low:high], 0.0).astype(bf16)))
    for matching in range(2):
        for j in range(count):

            @pl.when(select[matching] == j)
            def _():
                chosen[...] = maps[j][...]

        other = chosen[...]
        keys = dot(other, weights[1]).astype(bf16)
        values = dot(other, weights[2]).T
        shifts = []
        for j in range(tiles):
            row = jnp.zeros((1, tokens), f32)
            for i in range(tiles):
                bit = mask[(matching * tiles + i) * tiles + j]
                row = jnp.where(lane_tile == i, jnp.where(bit > 0, 0.0, MASKED), row)
            shifts.append(row)
        for h in range(HEADS):
            low, high, wanted = windows[h]
            scores = dot(keys[:, low:high], wanted) * scale
            scores = jnp.concatenate(
                [scores[j * width : (j + 1) * width] + shifts[j] for j in range(tiles)], axis=0
            )
            powers = jnp.exp2(scores - jnp.max(scores, axis=0, keepdims=True))
            norm = 1.0 / jnp.sum(powers, axis=0, keepdims=True)
            part = dot(values[h * head : (h + 1) * head].astype(bf16), powers.astype(bf16)) * norm
            if matching == 0:
                totals[pl.ds(h * head, head), :] = part
            else:
                totals[pl.ds(h * head, head), :] += part
    mixture = totals[...].T.astype(bf16)
    copy.wait()
    result = (hidden[...].astype(f32) + dot(mixture, weights[3])).astype(bf16)
    second[...] = result
    blocks[...] = layer_norm(result.astype(f32)).astype(bf16)


def frame_part(queries, rows, weights):
    channels = rows.shape[1]
    head = channels // HEADS
    ones = block_diagonal(channels, head)
    keys = dot(rows, weights[1]).astype(bf16).astype(f32)
    values = dot(rows, weights[2]).astype(bf16)
    products = queries * keys
    high = products.astype(bf16)
    low = (products - high.astype(f32)).astype(bf16)
    return (dot(high, ones) + dot(low, ones)) * (LOG2E / math.sqrt(head)), values


def own_frame_kernel(where, rows, three, one, *refs):
    parts, (weights, queries, scores, values, sems) = refs[:-5], refs[-5:]
    copies = fetch_own(where, three, one, weights, sems)
    assemble(where, where[max(1, len(parts))], parts, weights, one.shape[0], 2)
    for copy in copies:
        copy.wait()
    queries[...] = dot(rows[...], weights[0]).astype(bf16)
    scores[...], values[...] = frame_part(queries[...].astype(f32), rows[...], weights)


def frame_kernel(queries, rows, weights, scores, values):
    scores[...], values[...] = frame_part(queries[...].astype(f32), rows[...], weights)


def last_kernel(frames, *refs):
    second, queries, rows, weights = refs[:4]
    scores = refs[4 : 3 + frames]
    values = refs[3 + frames : 2 + 2 * frames]
    out = refs[-1]
    last_scores, last_values = frame_part(queries[...].astype(f32), rows[...], weights)
    every = [ref[...] for ref in scores] + [last_scores]
    most = functools.reduce(jnp.maximum, every)
    powers = [jnp.exp2(one - most) for one in every]
    norm = 1.0 / functools.reduce(jnp.add, powers)
    total = (powers[-1] * norm).astype(bf16).astype(f32) * last_values.astype(f32)
    for power, value in zip(powers, values):
        total += (power * norm).astype(bf16).astype(f32) * value[...].astype(f32)
    result = second[...].astype(f32) + dot(total.astype(bf16), weights[3])
    out[...] = result.T.astype(bf16)


def is_power(n):
    return n & (n - 1) == 0


def partner_permutation(size, k):
    if is_power(size):
        return [(i, i ^ k) for i in range(size)]
    return [(i, (i + k) % size) for i in range(size)]


def partner(me, size, k, sign=1):
    if is_power(size):
        return me ^ k
    return (me + sign * k) % size


def gather_maps(own, axis, size, beside=None):
    maps = {0: own}
    if is_power(size):
        bit = size // 2
        while bit:
            for k in list(maps):
                sent = maps[k] if k == 0 or beside is None else after(maps[k], beside)
                maps[k | bit] = lax.ppermute(sent, axis, partner_permutation(size, bit))
            bit //= 2
    else:
        for k in range(1, size):
            maps[k] = lax.ppermute(own, axis, partner_permutation(size, k))
    return [maps[k] for k in range(size)]


def sum_over(value, axis, size):
    if not is_power(size):
        return lax.psum(value, axis)
    bit = 1
    while bit < size:
        value = value + lax.ppermute(value, axis, partner_permutation(size, bit))
        bit *= 2
    return value


def after(x, *others):
    return lax.optimization_barrier((x, *others))[0]


def ring_gather(own, axis, size, beside=None):
    pieces = {0: own}
    right = [(i, (i + 1) % size) for i in range(size)]
    left = [(j, i) for i, j in right]
    for step in range(1, size // 2 + 1):
        pieces[step] = lax.ppermute(pieces[step - 1], axis, right)
        if size - step > step:
            pieces[size - step] = lax.ppermute(pieces[(size - step + 1) % size], axis, left)
        if step == 1 and beside is not None:
            pieces[1] = after(pieces[1], beside)
    return [pieces[k] for k in range(size)]


def half_of(three, one, side):
    whole = jnp.concatenate([three, one[None]], axis=0)
    whole = whole.reshape(2, 2 * one.shape[0], one.shape[1])
    return lax.dynamic_index_in_dim(whole, side, 0, keepdims=False)


def swap(pieces, first, rows, videos):
    joined = jnp.concatenate([piece[first : first + rows] for piece in pieces], axis=0)
    return lax.ppermute(joined, "video", partner_permutation(videos, 1))


def per_device(
    latents,
    timesteps,
    matchings,
    tile_mask,
    conv_first,
    conv_second,
    time_proj,
    epi_in,
    epi_out,
    temp_in,
    temp_out,
):
    tokens, channels = latents.shape[2:]
    tiles = tile_mask.shape[2]
    frames = lax.axis_size("frame")
    videos = lax.axis_size("video")
    frame = lax.axis_index("frame")
    video = lax.axis_index("video")
    pixels = tokens // frames
    source = latents.reshape(tokens, channels).T

    rows = time_proj.shape[0]
    half = rows * frames // 2
    index = frame * rows + jnp.arange(rows, dtype=jnp.int32)
    exponent = jnp.where(index < half, index, index - half).astype(f32)
    frequency = jnp.exp(-math.log(10000.0) * exponent / half)
    angles = timesteps.astype(f32)[:, None] * frequency[None, :]
    wave = jnp.where(index[None, :] < half, jnp.cos(angles), jnp.sin(angles))
    time_act = jax.nn.silu(wave).astype(bf16)
    height = epi_out.shape[0]
    paired = videos % 2 == 0 and is_power(videos) and height % 16 == 0
    early = pl.CostEstimate(flops=10**10, bytes_accessed=1 << 20, transcendentals=0)
    share = pl.pallas_call(
        share_kernel,
        out_shape=jax.ShapeDtypeStruct((1, channels), f32),
        in_specs=[VMEM, HBM],
        out_specs=VMEM,
        scratch_shapes=[pltpu.VMEM(time_proj.shape, bf16), pltpu.SemaphoreType.DMA],
        compiler_params=params(),
        cost_estimate=early,
        name="time_share",
    )(time_act, in_hbm(time_proj))
    bias = sum_over(share, "frame", frames)
    if paired:
        steps = [frame - k for k in range(frames)]
        places = [step % frames for step in steps] + [video % 2]
    else:
        places = [jnp.int32(0)] * 2
        epi_in = lax.all_gather(epi_in, "frame", axis=1, tiled=True)
        epi_out = lax.all_gather(epi_out, "frame", axis=0, tiled=True)
        temp_in = lax.all_gather(temp_in, "frame", axis=1, tiled=True)
        temp_out = lax.all_gather(temp_out, "frame", axis=0, tiled=True)
    places = jnp.stack(places).astype(jnp.int32)

    source_scratch = pltpu.VMEM((channels, tokens), bf16)
    padded_scratch = pltpu.VMEM((tokens + 2 * W, 3 * channels), bf16)
    conv_cost = pl.CostEstimate(
        flops=2 * 9 * tokens * channels * channels,
        bytes_accessed=2 * 9 * channels * channels + 8 * tokens * channels,
        transcendentals=tokens * channels,
    )
    inner, turned = pl.pallas_call(
        first_kernel,
        out_shape=[
            jax.ShapeDtypeStruct((tokens, channels), f32),
            jax.ShapeDtypeStruct((tokens, channels), bf16),
        ],
        in_specs=[HBM, HBM],
        out_specs=[VMEM, VMEM],
        scratch_shapes=[
            source_scratch,
            pltpu.VMEM((3, 3 * channels, channels), bf16),
            padded_scratch,
            pltpu.SemaphoreType.DMA((4,)),
        ],
        compiler_params=params(),
        cost_estimate=conv_cost,
        name="first_conv",
    )(in_hbm(source), in_hbm(conv_first.reshape(3, 3 * channels, channels)))
    hidden, normed = pl.pallas_call(
        second_kernel,
        out_shape=[
            jax.ShapeDtypeStruct((tokens, channels), bf16),
            jax.ShapeDtypeStruct((tokens, channels), bf16),
        ],
        in_specs=[VMEM] * 4,
        out_specs=[VMEM] * 2,
        scratch_shapes=[padded_scratch],
        compiler_params=params(),
        cost_estimate=conv_cost,
        name="second_conv",
    )(turned, inner, bias, conv_second.reshape(3, 3 * channels, channels))
    parts = []
    last_part = None
    if paired:
        mine = jnp.concatenate(
            [half_of(epi_in, epi_out, video % 2), half_of(temp_in, temp_out, video % 2)], axis=0
        )
        parts = ring_gather(after(mine, bias), "frame", frames, normed)
        normed = after(normed, parts[1 % frames], parts[-1])
        last_part = parts[frames // 2]
    maps = gather_maps(normed, "video", videos, last_part)
    epi_parts = temp_parts = []
    if paired:
        parts = parts[1:]
        epi_parts = parts + [swap(parts, 0, 2 * height, videos)]
        temp_parts = parts + [swap(parts, 2 * height, 2 * height, videos)]
    targets = lax.dynamic_index_in_dim(matchings, video, 1, keepdims=False)
    if is_power(videos):
        select = video ^ targets
    else:
        select = (video - targets) % videos
    mask = lax.dynamic_index_in_dim(tile_mask, video, 1, keepdims=False).reshape(-1)
    square = (4, channels, channels)
    queries, epi = pl.pallas_call(
        query_kernel,
        out_shape=[
            jax.ShapeDtypeStruct((channels, tokens), f32),
            jax.ShapeDtypeStruct(square, bf16),
        ],
        in_specs=[SMEM, VMEM, HBM, HBM] + [VMEM] * len(epi_parts),
        out_specs=[VMEM] * 2,
        scratch_shapes=[pltpu.SemaphoreType.DMA((4,))],
        compiler_params=params(),
        name="query",
    )(places, normed, in_hbm(epi_in), in_hbm(epi_out), *epi_parts)
    second, blocks = pl.pallas_call(
        functools.partial(view_kernel, videos, tiles),
        out_shape=[jax.ShapeDtypeStruct((tokens, channels), bf16)] * 2,
        in_specs=[SMEM, SMEM, HBM, VMEM, VMEM] + [VMEM] * videos,
        out_specs=[VMEM, VMEM],
        scratch_shapes=[
            pltpu.VMEM((tokens, channels), bf16),
            pltpu.VMEM((channels, tokens), f32),
            pltpu.VMEM((tokens, channels), bf16),
            pltpu.SemaphoreType.DMA,
        ],
        compiler_params=params(),
        name="cross_view",
    )(select, mask, hidden, queries, epi, *maps)

    arrived = ring_gather(blocks, "frame", frames)
    score_shape = jax.ShapeDtypeStruct((tokens, channels), f32)
    value_shape = jax.ShapeDtypeStruct((tokens, channels), bf16)
    frame_cost = pl.CostEstimate(
        flops=8 * tokens * channels * channels,
        bytes_accessed=8 * channels * channels + 8 * tokens * channels,
        transcendentals=0,
    )
    temp, frame_queries, *first = pl.pallas_call(
        own_frame_kernel,
        out_shape=[jax.ShapeDtypeStruct(square, bf16), value_shape, score_shape, value_shape],
        in_specs=[SMEM, VMEM, HBM, HBM] + [VMEM] * len(epi_parts),
        out_specs=[VMEM] * 4,
        scratch_shapes=[pltpu.SemaphoreType.DMA((4,))],
        compiler_params=params(),
        cost_estimate=frame_cost,
        name="own_frame",
    )(places, blocks, in_hbm(temp_in), in_hbm(temp_out), *temp_parts)
    scores, values = [first[0]], [first[1]]
    order = sorted(range(1, frames), key=lambda k: min(k, frames - k))
    for k in order[:-1]:
        one = pl.pallas_call(
            frame_kernel,
            out_shape=[score_shape, value_shape],
            in_specs=[VMEM] * 3,
            out_specs=[VMEM] * 2,
            compiler_params=params(),
            cost_estimate=frame_cost,
            name="other_frame",
        )(frame_queries, arrived[k], temp)
        scores.append(one[0])
        values.append(one[1])
    denoised = pl.pallas_call(
        functools.partial(last_kernel, frames),
        out_shape=jax.ShapeDtypeStruct((channels, tokens), bf16),
        in_specs=[VMEM] * (2 + 2 * frames),
        out_specs=VMEM,
        compiler_params=params(),
        name="last",
    )(second, frame_queries, arrived[order[-1]], temp, *scores, *values)
    return denoised.T.reshape(1, 1, tokens, channels)


def solution(mesh):
    placed = (
        P(("groups", "video"), "frame", None, None),
        P(("groups", "video")),
        P(None, "groups"),
        P(None, "groups", None, None),
        P(),
        P(),
        P("frame", None),
        P(None, "frame", None),
        P("frame", None),
        P(None, "frame", None),
        P("frame", None),
    )
    return jax.shard_map(
        per_device,
        mesh=mesh,
        in_specs=placed,
        out_specs=P(("groups", "video"), "frame", None, None),
        check_vma=False,
    )
```

```python
import functools
import math

import jax
import jax.numpy as jnp
from jax import lax
from jax.experimental import pallas as pl
from jax.experimental.pallas import tpu as pltpu
from jax.sharding import PartitionSpec as P

HEADS = 8
NORM_GROUPS = 32
TEMB = 1280
H = 8
W = 32

EPSILON = 1e-05
MASKED = -1e30
LOG2E = 1.4426950408889634
SHARE_ROWS = 16

VMEM = pl.BlockSpec(memory_space=pltpu.VMEM)
SMEM = pl.BlockSpec(memory_space=pltpu.SMEM)
HBM = pl.BlockSpec(memory_space=pl.ANY)
f32 = jnp.float32
bf16 = jnp.bfloat16


def params():
    return pltpu.CompilerParams(vmem_limit_bytes=16 * 1024 * 1024)


def in_hbm(x):
    return pltpu.with_memory_space_constraint(x, pltpu.HBM)


def fetch(source, target, sem):
    copy = pltpu.make_async_copy(source, target, sem)
    copy.start()
    return copy


def dot(a, b):
    return jnp.dot(a, b, preferred_element_type=f32)


def block_diagonal(size, width):
    rows = lax.broadcasted_iota(jnp.int32, (size, 1), 0).astype(f32)
    cols = lax.broadcasted_iota(jnp.int32, (1, size), 1).astype(f32)
    rows = jnp.floor((rows + 0.5) * (1.0 / width))
    cols = jnp.floor((cols + 0.5) * (1.0 / width))
    return (rows == cols).astype(f32).astype(bf16)


def terms(row):
    first = row.astype(bf16).astype(f32)
    second = (row - first).astype(bf16).astype(f32)
    third = row - first - second
    index = lax.broadcasted_iota(jnp.int32, (SHARE_ROWS, row.shape[1]), 0)
    return jnp.where(
        index == 0, first, jnp.where(index == 1, second, jnp.where(index == 2, third, 0.0))
    )


def group_sum(row, ones):
    return jnp.sum(dot(terms(row).astype(bf16), ones), axis=0, keepdims=True)


def group_norm_silu(x):
    tokens, channels = x.shape
    width = channels // NORM_GROUPS
    ones = block_diagonal(channels, width)
    inverse = 1.0 / (tokens * width)
    average = group_sum(jnp.sum(x, axis=0, keepdims=True), ones) * inverse
    centred = x - average
    spread = group_sum(jnp.sum(centred * centred, axis=0, keepdims=True), ones) * inverse
    y = centred * lax.rsqrt(spread + EPSILON)
    return y / (1.0 + jnp.exp(-y))


def layer_norm(x):
    inverse = 1.0 / x.shape[1]
    average = jnp.sum(x, axis=1, keepdims=True) * inverse
    centred = x - average
    spread = jnp.sum(centred * centred, axis=1, keepdims=True) * inverse
    return centred * lax.rsqrt(spread + EPSILON)


def convolve(y, weight, padded, copies):
    tokens, channels = y.shape
    column = lax.broadcasted_iota(jnp.int32, (tokens, 1), 0) & (W - 1)
    before = jnp.where(column == 0, 0.0, pltpu.roll(y, 1, 0))
    after = jnp.where(column == W - 1, 0.0, pltpu.roll(y, tokens - 1, 0))
    padded[pl.ds(0, W), :] = jnp.zeros((W, 3 * channels), bf16)
    padded[pl.ds(tokens + W, W), :] = jnp.zeros((W, 3 * channels), bf16)
    padded[pl.ds(W, tokens), :] = jnp.concatenate(
        [before.astype(bf16), y.astype(bf16), after.astype(bf16)], axis=1
    )
    total = None
    for k in range(3):
        if copies:
            copies[k].wait()
        part = dot(padded[pl.ds(k * W, tokens), :], weight[k])
        total = part if total is None else total + part
    return total


def share_kernel(act, proj_hbm, share, proj, sem):
    fetch(proj_hbm, proj, sem).wait()
    share[...] = dot(act[...], proj[...])


def first_kernel(source_hbm, weight_hbm, inner, turned, source, weight, padded, sems):
    copy = fetch(source_hbm, source, sems.at[0])
    copies = [fetch(weight_hbm.at[k], weight.at[k], sems.at[1 + k]) for k in range(3)]
    copy.wait()
    rows = source[...].astype(f32).T
    turned[...] = rows.astype(bf16)
    inner[...] = convolve(group_norm_silu(rows), weight, padded, copies)


def second_kernel(source, inner, bias, weight, hidden, normed, padded):
    y = group_norm_silu(inner[...] + bias[...])
    total = convolve(y, weight, padded, [])
    rounded = (source[...].astype(f32) + total).astype(bf16)
    hidden[...] = rounded
    normed[...] = layer_norm(rounded.astype(f32)).astype(bf16)


def fetch_own(where, three, one, whole, sems):
    rows = one.shape[0]
    place = pl.ds(pl.multiple_of(where[0] * rows, 16), rows)
    copies = [fetch(three.at[k], whole.at[k, place], sems.at[k]) for k in range(3)]
    return copies + [fetch(one, whole.at[3, place], sems.at[3])]


def assemble(where, side, parts, whole, rows):
    for k, part in enumerate(parts[:-1]):
        place = pl.ds(pl.multiple_of(where[k + 1] * rows, 16), rows)
        for j in range(2):
            mine = side * 2 + j
            whole[mine, place, :] = part[pl.ds(j * rows, rows), :]
            whole[2 - mine + 2 * j, place, :] = parts[-1][pl.ds((2 * k + j) * rows, rows), :]


def query_kernel(where, normed, three, one, *refs):
    parts, (queries, epi, sems) = refs[:-3], refs[-3:]
    copies = fetch_own(where, three, one, epi, sems)
    assemble(where, where[max(1, len(parts))], parts, epi, one.shape[0])
    for copy in copies:
        copy.wait()
    queries[...] = dot(normed[...], epi[0]).astype(bf16).astype(f32).T


def view_kernel(count, tiles, *refs):
    select, mask, hidden_ref, query_ref, weights = refs[:5]
    maps = refs[5 : 5 + count]
    second, blocks, chosen, totals, hidden, sem = refs[5 + count :]
    copy = fetch(hidden_ref, hidden, sem)
    tokens, channels = hidden.shape
    head = channels // HEADS
    width = tokens // tiles
    scale = LOG2E / math.sqrt(head)
    queries = query_ref[...]
    lane_tile = lax.broadcasted_iota(jnp.int32, (1, tokens), 1) // width
    windows = []
    for h in range(HEADS):
        low = h * head // 128 * 128
        high = min(channels, -(-(h + 1) * head // 128) * 128)
        row = lax.broadcasted_iota(jnp.int32, (high - low, 1), 0) + low
        inside = (row >= h * head) & (row < (h + 1) * head)
        windows.append((low, high, jnp.where(inside, queries[low:high], 0.0).astype(bf16)))
    for matching in range(2):
        for j in range(count):

            @pl.when(select[matching] == j)
            def _():
                chosen[...] = maps[j][...]

        other = chosen[...]
        keys = dot(other, weights[1]).astype(bf16)
        values = dot(other, weights[2]).T
        shifts = []
        for j in range(tiles):
            row = jnp.zeros((1, tokens), f32)
            for i in range(tiles):
                bit = mask[(matching * tiles + i) * tiles + j]
                row = jnp.where(lane_tile == i, jnp.where(bit > 0, 0.0, MASKED), row)
            shifts.append(row)
        for h in range(HEADS):
            low, high, wanted = windows[h]
            scores = dot(keys[:, low:high], wanted) * scale
            scores = jnp.concatenate(
                [scores[j * width : (j + 1) * width] + shifts[j] for j in range(tiles)], axis=0
            )
            powers = jnp.exp2(scores - jnp.max(scores, axis=0, keepdims=True))
            norm = 1.0 / jnp.sum(powers, axis=0, keepdims=True)
            part = dot(values[h * head : (h + 1) * head].astype(bf16), powers.astype(bf16)) * norm
            if matching == 0:
                totals[pl.ds(h * head, head), :] = part
            else:
                totals[pl.ds(h * head, head), :] += part
    mixture = totals[...].T.astype(bf16)
    copy.wait()
    result = (hidden[...].astype(f32) + dot(mixture, weights[3])).astype(bf16)
    second[...] = result
    blocks[...] = layer_norm(result.astype(f32)).astype(bf16)


def frame_part(queries, rows, weights):
    channels = rows.shape[1]
    head = channels // HEADS
    ones = block_diagonal(channels, head)
    keys = dot(rows, weights[1]).astype(bf16).astype(f32)
    values = dot(rows, weights[2]).astype(bf16)
    products = queries * keys
    high = products.astype(bf16)
    low = (products - high.astype(f32)).astype(bf16)
    return (dot(high, ones) + dot(low, ones)) * (LOG2E / math.sqrt(head)), values


def own_frame_kernel(where, rows, three, one, *refs):
    parts, (weights, queries, scores, values, sems) = refs[:-5], refs[-5:]
    copies = fetch_own(where, three, one, weights, sems)
    assemble(where, where[max(1, len(parts))], parts, weights, one.shape[0])
    for copy in copies:
        copy.wait()
    queries[...] = dot(rows[...], weights[0]).astype(bf16)
    scores[...], values[...] = frame_part(queries[...].astype(f32), rows[...], weights)


def frame_kernel(queries, rows, weights, scores, values):
    scores[...], values[...] = frame_part(queries[...].astype(f32), rows[...], weights)


def last_kernel(frames, *refs):
    second, queries, rows, weights = refs[:4]
    scores = refs[4 : 3 + frames]
    values = refs[3 + frames : 2 + 2 * frames]
    out = refs[-1]
    last_scores, last_values = frame_part(queries[...].astype(f32), rows[...], weights)
    every = [ref[...] for ref in scores] + [last_scores]
    most = functools.reduce(jnp.maximum, every)
    powers = [jnp.exp2(one - most) for one in every]
    norm = 1.0 / functools.reduce(jnp.add, powers)
    total = (powers[-1] * norm).astype(bf16).astype(f32) * last_values.astype(f32)
    for power, value in zip(powers, values):
        total += (power * norm).astype(bf16).astype(f32) * value[...].astype(f32)
    result = second[...].astype(f32) + dot(total.astype(bf16), weights[3])
    out[...] = result.T.astype(bf16)


def is_power(n):
    return n & (n - 1) == 0


def partner_permutation(size, k):
    if is_power(size):
        return [(i, i ^ k) for i in range(size)]
    return [(i, (i + k) % size) for i in range(size)]


def partner(me, size, k, sign=1):
    if is_power(size):
        return me ^ k
    return (me + sign * k) % size


def gather_maps(own, axis, size, beside=None):
    maps = {0: own}
    if is_power(size):
        bit = size // 2
        while bit:
            for k in list(maps):
                sent = maps[k] if k == 0 or beside is None else after(maps[k], beside)
                maps[k | bit] = lax.ppermute(sent, axis, partner_permutation(size, bit))
            bit //= 2
    else:
        for k in range(1, size):
            maps[k] = lax.ppermute(own, axis, partner_permutation(size, k))
    return [maps[k] for k in range(size)]


def sum_over(value, axis, size, bit=1):
    if not is_power(size):
        return lax.psum(value, axis)
    while bit < size:
        value = value + lax.ppermute(value, axis, partner_permutation(size, bit))
        bit *= 2
    return value


def after(x, *others):
    return lax.optimization_barrier((x, *others))[0]


def ring_gather(own, axis, size, beside=None, steps=0, pieces=None):
    pieces = dict(pieces or {0: own})
    right = [(i, (i + 1) % size) for i in range(size)]
    left = [(j, i) for i, j in right]
    for step in range(1, (steps or size // 2) + 1):
        if step not in pieces:
            sent = pieces[step - 1]
            if beside is not None:
                sent = after(sent, beside)
            pieces[step] = lax.ppermute(sent, axis, right)
        if size - step > step and size - step not in pieces:
            pieces[size - step] = lax.ppermute(pieces[(size - step + 1) % size], axis, left)
    return pieces if steps else [pieces[k] for k in range(size)]


def half_of(three, one, side):
    whole = jnp.concatenate([three, one[None]], axis=0)
    whole = whole.reshape(2, 2 * one.shape[0], one.shape[1])
    return lax.dynamic_index_in_dim(whole, side, 0, keepdims=False)


def swap(pieces, videos):
    joined = jnp.concatenate(pieces[1:], axis=0)
    return pieces[1:] + [lax.ppermute(joined, "video", partner_permutation(videos, 1))]


def per_device(
    latents,
    timesteps,
    matchings,
    tile_mask,
    conv_first,
    conv_second,
    time_proj,
    epi_in,
    epi_out,
    temp_in,
    temp_out,
):
    tokens, channels = latents.shape[2:]
    tiles = tile_mask.shape[2]
    frames = lax.axis_size("frame")
    videos = lax.axis_size("video")
    frame = lax.axis_index("frame")
    video = lax.axis_index("video")
    pixels = tokens // frames
    source = latents.reshape(tokens, channels).T

    rows = time_proj.shape[0]
    half = rows * frames // 2
    index = frame * rows + jnp.arange(rows, dtype=jnp.int32)
    exponent = jnp.where(index < half, index, index - half).astype(f32)
    frequency = jnp.exp(-math.log(10000.0) * exponent / half)
    angles = timesteps.astype(f32)[:, None] * frequency[None, :]
    wave = jnp.where(index[None, :] < half, jnp.cos(angles), jnp.sin(angles))
    time_act = jax.nn.silu(wave).astype(bf16)
    height = epi_out.shape[0]
    paired = videos % 2 == 0 and is_power(videos) and height % 16 == 0
    early = pl.CostEstimate(flops=10**10, bytes_accessed=1 << 20, transcendentals=0)
    share = pl.pallas_call(
        share_kernel,
        out_shape=jax.ShapeDtypeStruct((1, channels), f32),
        in_specs=[VMEM, HBM],
        out_specs=VMEM,
        scratch_shapes=[pltpu.VMEM(time_proj.shape, bf16), pltpu.SemaphoreType.DMA],
        compiler_params=params(),
        cost_estimate=early,
        name="time_share",
    )(time_act, in_hbm(time_proj))
    if paired:
        steps = [frame - k for k in range(frames)]
        places = [step % frames for step in steps] + [video % 2]
    else:
        places = [jnp.int32(0)] * 2
        epi_in = lax.all_gather(epi_in, "frame", axis=1, tiled=True)
        epi_out = lax.all_gather(epi_out, "frame", axis=0, tiled=True)
        temp_in = lax.all_gather(temp_in, "frame", axis=1, tiled=True)
        temp_out = lax.all_gather(temp_out, "frame", axis=0, tiled=True)
    places = jnp.stack(places).astype(jnp.int32)
    temp_places = places
    if paired:
        temp_places = [partner(frame, frames, k, -1) for k in range(frames)] + [video % 2]
        temp_places = jnp.stack(temp_places).astype(jnp.int32)

    source_scratch = pltpu.VMEM((channels, tokens), bf16)
    padded_scratch = pltpu.VMEM((tokens + 2 * W, 3 * channels), bf16)
    conv_cost = pl.CostEstimate(
        flops=2 * 9 * tokens * channels * channels,
        bytes_accessed=2 * 9 * channels * channels + 8 * tokens * channels,
        transcendentals=tokens * channels,
    )
    inner, turned = pl.pallas_call(
        first_kernel,
        out_shape=[
            jax.ShapeDtypeStruct((tokens, channels), f32),
            jax.ShapeDtypeStruct((tokens, channels), bf16),
        ],
        in_specs=[HBM, HBM],
        out_specs=[VMEM, VMEM],
        scratch_shapes=[
            source_scratch,
            pltpu.VMEM((3, 3 * channels, channels), bf16),
            padded_scratch,
            pltpu.SemaphoreType.DMA((4,)),
        ],
        compiler_params=params(),
        cost_estimate=conv_cost,
        name="first_conv",
    )(in_hbm(after(source, share)), in_hbm(conv_first.reshape(3, 3 * channels, channels)))
    if paired:
        mine = half_of(epi_in, epi_out, video % 2)
        near = ring_gather(mine, "frame", frames, None, 1)
        bias = share
        if frames > 1 and is_power(frames):
            bias = share + lax.ppermute(share, "frame", partner_permutation(frames, 1))
            bias = after(bias, near[1], near[frames - 1], inner)
        bias = sum_over(bias, "frame", frames, 2)
        epi_parts = ring_gather(mine, "frame", frames, bias, 0, near)
    else:
        bias = sum_over(share, "frame", frames)
    hidden, normed = pl.pallas_call(
        second_kernel,
        out_shape=[
            jax.ShapeDtypeStruct((tokens, channels), bf16),
            jax.ShapeDtypeStruct((tokens, channels), bf16),
        ],
        in_specs=[VMEM] * 4,
        out_specs=[VMEM] * 2,
        scratch_shapes=[padded_scratch],
        compiler_params=params(),
        cost_estimate=conv_cost,
        name="second_conv",
    )(turned, inner, bias, conv_second.reshape(3, 3 * channels, channels))
    last_part, epi_parts = None, list(epi_parts) if paired else []
    temp_parts = []
    if paired:
        mine = after(half_of(temp_in, temp_out, video % 2), normed)
        temp_parts = [mine] + [
            lax.ppermute(mine, "frame", partner_permutation(frames, k)) for k in range(1, frames)
        ]
        last_part = temp_parts[1 % frames]
        epi_parts = swap([after(part, normed) for part in epi_parts], videos)
    maps = gather_maps(normed, "video", videos, last_part)
    targets = lax.dynamic_index_in_dim(matchings, video, 1, keepdims=False)
    if is_power(videos):
        select = video ^ targets
    else:
        select = (video - targets) % videos
    mask = lax.dynamic_index_in_dim(tile_mask, video, 1, keepdims=False).reshape(-1)
    square = (4, channels, channels)
    small = pl.CostEstimate(flops=1, bytes_accessed=1, transcendentals=0)
    queries, epi = pl.pallas_call(
        query_kernel,
        out_shape=[
            jax.ShapeDtypeStruct((channels, tokens), f32),
            jax.ShapeDtypeStruct(square, bf16),
        ],
        in_specs=[SMEM, VMEM, HBM, HBM] + [VMEM] * len(epi_parts),
        out_specs=[VMEM] * 2,
        scratch_shapes=[pltpu.SemaphoreType.DMA((4,))],
        compiler_params=params(),
        cost_estimate=small,
        name="query",
    )(places, normed, in_hbm(epi_in), in_hbm(epi_out), *epi_parts)
    second, blocks = pl.pallas_call(
        functools.partial(view_kernel, videos, tiles),
        out_shape=[jax.ShapeDtypeStruct((tokens, channels), bf16)] * 2,
        in_specs=[SMEM, SMEM, HBM, VMEM, VMEM] + [VMEM] * videos,
        out_specs=[VMEM, VMEM],
        scratch_shapes=[
            pltpu.VMEM((tokens, channels), bf16),
            pltpu.VMEM((channels, tokens), f32),
            pltpu.VMEM((tokens, channels), bf16),
            pltpu.SemaphoreType.DMA,
        ],
        compiler_params=params(),
        cost_estimate=small,
        name="cross_view",
    )(select, mask, hidden, queries, epi, *maps)

    if paired:
        held = [after(part, blocks) for part in temp_parts]
        blocks = after(blocks, *temp_parts)
        temp_parts = swap(held, videos)
    arrived = ring_gather(blocks, "frame", frames)
    score_shape = jax.ShapeDtypeStruct((tokens, channels), f32)
    value_shape = jax.ShapeDtypeStruct((tokens, channels), bf16)
    frame_cost = pl.CostEstimate(
        flops=8 * tokens * channels * channels,
        bytes_accessed=8 * channels * channels + 8 * tokens * channels,
        transcendentals=0,
    )
    temp, frame_queries, *first = pl.pallas_call(
        own_frame_kernel,
        out_shape=[jax.ShapeDtypeStruct(square, bf16), value_shape, score_shape, value_shape],
        in_specs=[SMEM, VMEM, HBM, HBM] + [VMEM] * len(temp_parts),
        out_specs=[VMEM] * 4,
        scratch_shapes=[pltpu.SemaphoreType.DMA((4,))],
        compiler_params=params(),
        cost_estimate=frame_cost,
        name="own_frame",
    )(temp_places, blocks, in_hbm(temp_in), in_hbm(temp_out), *temp_parts)
    scores, values = [first[0]], [first[1]]
    order = sorted(range(1, frames), key=lambda k: min(k, frames - k))
    for k in order[:-1]:
        one = pl.pallas_call(
            frame_kernel,
            out_shape=[score_shape, value_shape],
            in_specs=[VMEM] * 3,
            out_specs=[VMEM] * 2,
            compiler_params=params(),
            cost_estimate=frame_cost,
            name="other_frame",
        )(frame_queries, arrived[k], temp)
        scores.append(one[0])
        values.append(one[1])
    denoised = pl.pallas_call(
        functools.partial(last_kernel, frames),
        out_shape=jax.ShapeDtypeStruct((channels, tokens), bf16),
        in_specs=[VMEM] * (2 + 2 * frames),
        out_specs=VMEM,
        compiler_params=params(),
        name="last",
    )(second, frame_queries, arrived[order[-1]], temp, *scores, *values)
    return denoised.T.reshape(1, 1, tokens, channels)


def solution(mesh):
    placed = (
        P(("groups", "video"), "frame", None, None),
        P(("groups", "video")),
        P(None, "groups"),
        P(None, "groups", None, None),
        P(),
        P(),
        P("frame", None),
        P(None, "frame", None),
        P("frame", None),
        P(None, "frame", None),
        P("frame", None),
    )
    return jax.shard_map(
        per_device,
        mesh=mesh,
        in_specs=placed,
        out_specs=P(("groups", "video"), "frame", None, None),
        check_vma=False,
    )
```

```python
import functools
import math

import jax
import jax.numpy as jnp
from jax import lax
from jax.experimental import pallas as pl
from jax.experimental.pallas import tpu as pltpu
from jax.sharding import PartitionSpec as P

HEADS = 8
NORM_GROUPS = 32
TEMB = 1280
H = 8
W = 32

EPSILON = 1e-05
MASKED = -1e30
LOG2E = 1.4426950408889634
SHARE_ROWS = 16

VMEM = pl.BlockSpec(memory_space=pltpu.VMEM)
SMEM = pl.BlockSpec(memory_space=pltpu.SMEM)
HBM = pl.BlockSpec(memory_space=pl.ANY)
f32 = jnp.float32
bf16 = jnp.bfloat16


def params():
    return pltpu.CompilerParams(vmem_limit_bytes=16 * 1024 * 1024)


def in_hbm(x):
    return pltpu.with_memory_space_constraint(x, pltpu.HBM)


def fetch(source, target, sem):
    copy = pltpu.make_async_copy(source, target, sem)
    copy.start()
    return copy


def dot(a, b):
    return jnp.dot(a, b, preferred_element_type=f32)


def block_diagonal(size, width):
    rows = lax.broadcasted_iota(jnp.int32, (size, 1), 0).astype(f32)
    cols = lax.broadcasted_iota(jnp.int32, (1, size), 1).astype(f32)
    rows = jnp.floor((rows + 0.5) * (1.0 / width))
    cols = jnp.floor((cols + 0.5) * (1.0 / width))
    return (rows == cols).astype(f32).astype(bf16)


def terms(row):
    first = row.astype(bf16).astype(f32)
    second = (row - first).astype(bf16).astype(f32)
    third = row - first - second
    index = lax.broadcasted_iota(jnp.int32, (SHARE_ROWS, row.shape[1]), 0)
    return jnp.where(
        index == 0, first, jnp.where(index == 1, second, jnp.where(index == 2, third, 0.0))
    )


def group_sum(row, ones):
    return jnp.sum(dot(terms(row).astype(bf16), ones), axis=0, keepdims=True)


def group_norm_silu(x):
    tokens, channels = x.shape
    width = channels // NORM_GROUPS
    ones = block_diagonal(channels, width)
    inverse = 1.0 / (tokens * width)
    average = group_sum(jnp.sum(x, axis=0, keepdims=True), ones) * inverse
    centred = x - average
    spread = group_sum(jnp.sum(centred * centred, axis=0, keepdims=True), ones) * inverse
    y = centred * lax.rsqrt(spread + EPSILON)
    return y / (1.0 + jnp.exp(-y))


def layer_norm(x):
    inverse = 1.0 / x.shape[1]
    average = jnp.sum(x, axis=1, keepdims=True) * inverse
    centred = x - average
    spread = jnp.sum(centred * centred, axis=1, keepdims=True) * inverse
    return centred * lax.rsqrt(spread + EPSILON)


def convolve(y, weight, padded, copies):
    tokens, channels = y.shape
    column = lax.broadcasted_iota(jnp.int32, (tokens, 1), 0) & (W - 1)
    before = jnp.where(column == 0, 0.0, pltpu.roll(y, 1, 0))
    after = jnp.where(column == W - 1, 0.0, pltpu.roll(y, tokens - 1, 0))
    padded[pl.ds(0, W), :] = jnp.zeros((W, 3 * channels), bf16)
    padded[pl.ds(tokens + W, W), :] = jnp.zeros((W, 3 * channels), bf16)
    padded[pl.ds(W, tokens), :] = jnp.concatenate(
        [before.astype(bf16), y.astype(bf16), after.astype(bf16)], axis=1
    )
    total = None
    for k in range(3):
        if copies:
            copies[k].wait()
        part = dot(padded[pl.ds(k * W, tokens), :], weight[k])
        total = part if total is None else total + part
    return total


def share_kernel(act, proj_hbm, share, proj, sem):
    fetch(proj_hbm, proj, sem).wait()
    share[...] = dot(act[...], proj[...])


def first_kernel(source_hbm, weight_hbm, inner, turned, source, weight, padded, sems):
    copy = fetch(source_hbm, source, sems.at[0])
    copies = [fetch(weight_hbm.at[k], weight.at[k], sems.at[1 + k]) for k in range(3)]
    copy.wait()
    rows = source[...].astype(f32).T
    turned[...] = rows.astype(bf16)
    inner[...] = convolve(group_norm_silu(rows), weight, padded, copies)


def second_kernel(source, inner, bias, weight, hidden, normed, padded):
    y = group_norm_silu(inner[...] + bias[...])
    total = convolve(y, weight, padded, [])
    rounded = (source[...].astype(f32) + total).astype(bf16)
    hidden[...] = rounded
    normed[...] = layer_norm(rounded.astype(f32)).astype(bf16)


def fetch_own(where, three, one, whole, sems):
    rows = one.shape[0]
    place = pl.ds(pl.multiple_of(where[0] * rows, 16), rows)
    copies = [fetch(three.at[k], whole.at[k, place], sems.at[k]) for k in range(3)]
    return copies + [fetch(one, whole.at[3, place], sems.at[3])]


def assemble(where, side, parts, whole, rows):
    for k, part in enumerate(parts[:-1]):
        place = pl.ds(pl.multiple_of(where[k + 1] * rows, 16), rows)
        for j in range(2):
            mine = side * 2 + j
            whole[mine, place, :] = part[pl.ds(j * rows, rows), :]
            whole[2 - mine + 2 * j, place, :] = parts[-1][pl.ds((2 * k + j) * rows, rows), :]


def query_kernel(where, normed, three, one, *refs):
    parts, (queries, epi, sems) = refs[:-3], refs[-3:]
    copies = fetch_own(where, three, one, epi, sems)
    assemble(where, where[max(1, len(parts))], parts, epi, one.shape[0])
    for copy in copies:
        copy.wait()
    queries[...] = dot(normed[...], epi[0]).astype(bf16).astype(f32).T


def view_kernel(count, tiles, *refs):
    select, mask, hidden_ref, query_ref, weights = refs[:5]
    maps = refs[5 : 5 + count]
    second, blocks, chosen, totals, hidden, sem = refs[5 + count :]
    copy = fetch(hidden_ref, hidden, sem)
    tokens, channels = hidden.shape
    head = channels // HEADS
    width = tokens // tiles
    scale = LOG2E / math.sqrt(head)
    queries = query_ref[...]
    lane_tile = lax.broadcasted_iota(jnp.int32, (1, tokens), 1) // width
    windows = []
    for h in range(HEADS):
        low = h * head // 128 * 128
        high = min(channels, -(-(h + 1) * head // 128) * 128)
        row = lax.broadcasted_iota(jnp.int32, (high - low, 1), 0) + low
        inside = (row >= h * head) & (row < (h + 1) * head)
        windows.append((low, high, jnp.where(inside, queries[low:high], 0.0).astype(bf16)))
    for matching in range(2):
        for j in range(count):

            @pl.when(select[matching] == j)
            def _():
                chosen[...] = maps[j][...]

        other = chosen[...]
        keys = dot(other, weights[1]).astype(bf16)
        values = dot(other, weights[2]).T
        shifts = []
        for j in range(tiles):
            row = jnp.zeros((1, tokens), f32)
            for i in range(tiles):
                bit = mask[(matching * tiles + i) * tiles + j]
                row = jnp.where(lane_tile == i, jnp.where(bit > 0, 0.0, MASKED), row)
            shifts.append(row)
        for h in range(HEADS):
            low, high, wanted = windows[h]
            scores = dot(keys[:, low:high], wanted) * scale
            scores = jnp.concatenate(
                [scores[j * width : (j + 1) * width] + shifts[j] for j in range(tiles)], axis=0
            )
            powers = jnp.exp2(scores - jnp.max(scores, axis=0, keepdims=True))
            norm = 1.0 / jnp.sum(powers, axis=0, keepdims=True)
            part = dot(values[h * head : (h + 1) * head].astype(bf16), powers.astype(bf16)) * norm
            if matching == 0:
                totals[pl.ds(h * head, head), :] = part
            else:
                totals[pl.ds(h * head, head), :] += part
    mixture = totals[...].T.astype(bf16)
    copy.wait()
    result = (hidden[...].astype(f32) + dot(mixture, weights[3])).astype(bf16)
    second[...] = result
    blocks[...] = layer_norm(result.astype(f32)).astype(bf16)


def frame_part(queries, rows, weights):
    channels = rows.shape[1]
    head = channels // HEADS
    ones = block_diagonal(channels, head)
    keys = dot(rows, weights[1]).astype(bf16).astype(f32)
    values = dot(rows, weights[2]).astype(bf16)
    products = queries * keys
    high = products.astype(bf16)
    low = (products - high.astype(f32)).astype(bf16)
    return (dot(high, ones) + dot(low, ones)) * (LOG2E / math.sqrt(head)), values


def own_frame_kernel(where, rows, three, one, *refs):
    parts, (weights, queries, scores, values, sems) = refs[:-5], refs[-5:]
    copies = fetch_own(where, three, one, weights, sems)
    assemble(where, where[max(1, len(parts))], parts, weights, one.shape[0])
    for copy in copies:
        copy.wait()
    queries[...] = dot(rows[...], weights[0]).astype(bf16)
    scores[...], values[...] = frame_part(queries[...].astype(f32), rows[...], weights)


def frame_kernel(queries, rows, weights, scores, values):
    scores[...], values[...] = frame_part(queries[...].astype(f32), rows[...], weights)


def last_kernel(frames, *refs):
    second, queries, rows, weights = refs[:4]
    scores = refs[4 : 3 + frames]
    values = refs[3 + frames : 2 + 2 * frames]
    out = refs[-1]
    last_scores, last_values = frame_part(queries[...].astype(f32), rows[...], weights)
    every = [ref[...] for ref in scores] + [last_scores]
    most = functools.reduce(jnp.maximum, every)
    powers = [jnp.exp2(one - most) for one in every]
    norm = 1.0 / functools.reduce(jnp.add, powers)
    total = (powers[-1] * norm).astype(bf16).astype(f32) * last_values.astype(f32)
    for power, value in zip(powers, values):
        total += (power * norm).astype(bf16).astype(f32) * value[...].astype(f32)
    result = second[...].astype(f32) + dot(total.astype(bf16), weights[3])
    out[...] = result.T.astype(bf16)


def is_power(n):
    return n & (n - 1) == 0


def partner_permutation(size, k):
    if is_power(size):
        return [(i, i ^ k) for i in range(size)]
    return [(i, (i + k) % size) for i in range(size)]


def partner(me, size, k, sign=1):
    if is_power(size):
        return me ^ k
    return (me + sign * k) % size


def gather_maps(own, axis, size):
    maps = {0: own}
    if is_power(size):
        bit = size // 2
        while bit:
            for k in list(maps):
                maps[k | bit] = lax.ppermute(maps[k], axis, partner_permutation(size, bit))
            bit //= 2
    else:
        for k in range(1, size):
            maps[k] = lax.ppermute(own, axis, partner_permutation(size, k))
    return [maps[k] for k in range(size)]


def sum_over(value, axis, size):
    if not is_power(size):
        return lax.psum(value, axis)
    bit = 1
    while bit < size:
        value = value + lax.ppermute(value, axis, partner_permutation(size, bit))
        bit *= 2
    return value


def after(x, *others):
    return lax.optimization_barrier((x, *others))[0]


def ring_gather(own, axis, size, beside=None):
    pieces = {0: own}
    right = [(i, (i + 1) % size) for i in range(size)]
    left = [(j, i) for i, j in right]
    for step in range(1, size // 2 + 1):
        pieces[step] = lax.ppermute(pieces[step - 1], axis, right)
        if size - step > step:
            pieces[size - step] = lax.ppermute(pieces[(size - step + 1) % size], axis, left)
        if step == 1 and beside is not None:
            pieces[1] = after(pieces[1], beside)
    return [pieces[k] for k in range(size)]


def half_of(three, one, side):
    whole = jnp.concatenate([three, one[None]], axis=0)
    whole = whole.reshape(2, 2 * one.shape[0], one.shape[1])
    return lax.dynamic_index_in_dim(whole, side, 0, keepdims=False)


def swap(pieces, videos):
    joined = jnp.concatenate(pieces[1:], axis=0)
    return pieces[1:] + [lax.ppermute(joined, "video", partner_permutation(videos, 1))]


def per_device(
    latents,
    timesteps,
    matchings,
    tile_mask,
    conv_first,
    conv_second,
    time_proj,
    epi_in,
    epi_out,
    temp_in,
    temp_out,
):
    tokens, channels = latents.shape[2:]
    tiles = tile_mask.shape[2]
    frames = lax.axis_size("frame")
    videos = lax.axis_size("video")
    frame = lax.axis_index("frame")
    video = lax.axis_index("video")
    pixels = tokens // frames
    source = latents.reshape(tokens, channels).T

    rows = time_proj.shape[0]
    half = rows * frames // 2
    index = frame * rows + jnp.arange(rows, dtype=jnp.int32)
    exponent = jnp.where(index < half, index, index - half).astype(f32)
    frequency = jnp.exp(-math.log(10000.0) * exponent / half)
    angles = timesteps.astype(f32)[:, None] * frequency[None, :]
    wave = jnp.where(index[None, :] < half, jnp.cos(angles), jnp.sin(angles))
    time_act = jax.nn.silu(wave).astype(bf16)
    height = epi_out.shape[0]
    paired = videos % 2 == 0 and is_power(videos) and height % 16 == 0
    early = pl.CostEstimate(flops=10**10, bytes_accessed=1 << 20, transcendentals=0)
    share = pl.pallas_call(
        share_kernel,
        out_shape=jax.ShapeDtypeStruct((1, channels), f32),
        in_specs=[VMEM, HBM],
        out_specs=VMEM,
        scratch_shapes=[pltpu.VMEM(time_proj.shape, bf16), pltpu.SemaphoreType.DMA],
        compiler_params=params(),
        cost_estimate=early,
        name="time_share",
    )(time_act, in_hbm(time_proj))
    bias = sum_over(share, "frame", frames)
    if paired:
        steps = [frame - k for k in range(frames)]
        places = [step % frames for step in steps] + [video % 2]
    else:
        places = [jnp.int32(0)] * 2
        epi_in = lax.all_gather(epi_in, "frame", axis=1, tiled=True)
        epi_out = lax.all_gather(epi_out, "frame", axis=0, tiled=True)
        temp_in = lax.all_gather(temp_in, "frame", axis=1, tiled=True)
        temp_out = lax.all_gather(temp_out, "frame", axis=0, tiled=True)
    places = jnp.stack(places).astype(jnp.int32)

    source_scratch = pltpu.VMEM((channels, tokens), bf16)
    padded_scratch = pltpu.VMEM((tokens + 2 * W, 3 * channels), bf16)
    conv_cost = pl.CostEstimate(
        flops=2 * 9 * tokens * channels * channels,
        bytes_accessed=2 * 9 * channels * channels + 8 * tokens * channels,
        transcendentals=tokens * channels,
    )
    inner, turned = pl.pallas_call(
        first_kernel,
        out_shape=[
            jax.ShapeDtypeStruct((tokens, channels), f32),
            jax.ShapeDtypeStruct((tokens, channels), bf16),
        ],
        in_specs=[HBM, HBM],
        out_specs=[VMEM, VMEM],
        scratch_shapes=[
            source_scratch,
            pltpu.VMEM((3, 3 * channels, channels), bf16),
            padded_scratch,
            pltpu.SemaphoreType.DMA((4,)),
        ],
        compiler_params=params(),
        cost_estimate=conv_cost,
        name="first_conv",
    )(in_hbm(source), in_hbm(conv_first.reshape(3, 3 * channels, channels)))
    hidden, normed = pl.pallas_call(
        second_kernel,
        out_shape=[
            jax.ShapeDtypeStruct((tokens, channels), bf16),
            jax.ShapeDtypeStruct((tokens, channels), bf16),
        ],
        in_specs=[VMEM] * 4,
        out_specs=[VMEM] * 2,
        scratch_shapes=[padded_scratch],
        compiler_params=params(),
        cost_estimate=conv_cost,
        name="second_conv",
    )(turned, inner, bias, conv_second.reshape(3, 3 * channels, channels))
    if paired:
        mine = half_of(epi_in, epi_out, video % 2)
        epi_parts = ring_gather(after(mine, bias), "frame", frames, normed)
        normed = after(normed, epi_parts[-1])
    maps = gather_maps(normed, "video", videos)
    epi_parts = swap(epi_parts, videos) if paired else []
    targets = lax.dynamic_index_in_dim(matchings, video, 1, keepdims=False)
    if is_power(videos):
        select = video ^ targets
    else:
        select = (video - targets) % videos
    mask = lax.dynamic_index_in_dim(tile_mask, video, 1, keepdims=False).reshape(-1)
    square = (4, channels, channels)
    queries, epi = pl.pallas_call(
        query_kernel,
        out_shape=[
            jax.ShapeDtypeStruct((channels, tokens), f32),
            jax.ShapeDtypeStruct(square, bf16),
        ],
        in_specs=[SMEM, VMEM, HBM, HBM] + [VMEM] * len(epi_parts),
        out_specs=[VMEM] * 2,
        scratch_shapes=[pltpu.SemaphoreType.DMA((4,))],
        compiler_params=params(),
        name="query",
    )(places, normed, in_hbm(epi_in), in_hbm(epi_out), *epi_parts)
    temp_parts = []
    if paired:
        mine = after(half_of(temp_in, temp_out, video % 2), maps[1])
        temp_parts = ring_gather(mine, "frame", frames, queries)
    if paired:
        queries = after(queries, temp_parts[1 % frames], temp_parts[-1])
    second, blocks = pl.pallas_call(
        functools.partial(view_kernel, videos, tiles),
        out_shape=[jax.ShapeDtypeStruct((tokens, channels), bf16)] * 2,
        in_specs=[SMEM, SMEM, HBM, VMEM, VMEM] + [VMEM] * videos,
        out_specs=[VMEM, VMEM],
        scratch_shapes=[
            pltpu.VMEM((tokens, channels), bf16),
            pltpu.VMEM((channels, tokens), f32),
            pltpu.VMEM((tokens, channels), bf16),
            pltpu.SemaphoreType.DMA,
        ],
        compiler_params=params(),
        name="cross_view",
    )(select, mask, hidden, queries, epi, *maps)

    if paired:
        held = [after(part, blocks) for part in temp_parts]
        blocks = after(blocks, *temp_parts)
        temp_parts = swap(held, videos)
    arrived = ring_gather(blocks, "frame", frames)
    score_shape = jax.ShapeDtypeStruct((tokens, channels), f32)
    value_shape = jax.ShapeDtypeStruct((tokens, channels), bf16)
    frame_cost = pl.CostEstimate(
        flops=8 * tokens * channels * channels,
        bytes_accessed=8 * channels * channels + 8 * tokens * channels,
        transcendentals=0,
    )
    temp, frame_queries, *first = pl.pallas_call(
        own_frame_kernel,
        out_shape=[jax.ShapeDtypeStruct(square, bf16), value_shape, score_shape, value_shape],
        in_specs=[SMEM, VMEM, HBM, HBM] + [VMEM] * len(temp_parts),
        out_specs=[VMEM] * 4,
        scratch_shapes=[pltpu.SemaphoreType.DMA((4,))],
        compiler_params=params(),
        cost_estimate=frame_cost,
        name="own_frame",
    )(places, blocks, in_hbm(temp_in), in_hbm(temp_out), *temp_parts)
    scores, values = [first[0]], [first[1]]
    order = sorted(range(1, frames), key=lambda k: min(k, frames - k))
    for k in order[:-1]:
        one = pl.pallas_call(
            frame_kernel,
            out_shape=[score_shape, value_shape],
            in_specs=[VMEM] * 3,
            out_specs=[VMEM] * 2,
            compiler_params=params(),
            cost_estimate=frame_cost,
            name="other_frame",
        )(frame_queries, arrived[k], temp)
        scores.append(one[0])
        values.append(one[1])
    denoised = pl.pallas_call(
        functools.partial(last_kernel, frames),
        out_shape=jax.ShapeDtypeStruct((channels, tokens), bf16),
        in_specs=[VMEM] * (2 + 2 * frames),
        out_specs=VMEM,
        compiler_params=params(),
        name="last",
    )(second, frame_queries, arrived[order[-1]], temp, *scores, *values)
    return denoised.T.reshape(1, 1, tokens, channels)


def solution(mesh):
    placed = (
        P(("groups", "video"), "frame", None, None),
        P(("groups", "video")),
        P(None, "groups"),
        P(None, "groups", None, None),
        P(),
        P(),
        P("frame", None),
        P(None, "frame", None),
        P("frame", None),
        P(None, "frame", None),
        P("frame", None),
    )
    return jax.shard_map(
        per_device,
        mesh=mesh,
        in_specs=placed,
        out_specs=P(("groups", "video"), "frame", None, None),
        check_vma=False,
    )
```

```python
import functools
import math

import jax
import jax.numpy as jnp
from jax import lax
from jax.experimental import pallas as pl
from jax.experimental.pallas import tpu as pltpu
from jax.sharding import PartitionSpec as P

HEADS = 8
NORM_GROUPS = 32
TEMB = 1280
H = 8
W = 32

EPSILON = 1e-05
MASKED = -1e30
LOG2E = 1.4426950408889634

VMEM = pl.BlockSpec(memory_space=pltpu.VMEM)
SMEM = pl.BlockSpec(memory_space=pltpu.SMEM)
f32 = jnp.float32
bf16 = jnp.bfloat16


def params():
    return pltpu.CompilerParams(vmem_limit_bytes=16 * 1024 * 1024)


def dot(a, b):
    return jnp.dot(a, b, preferred_element_type=f32)


def block_diagonal(size, width):
    rows = lax.broadcasted_iota(jnp.int32, (size, 1), 0).astype(f32)
    cols = lax.broadcasted_iota(jnp.int32, (1, size), 1).astype(f32)
    rows = jnp.floor((rows + 0.5) * (1.0 / width))
    cols = jnp.floor((cols + 0.5) * (1.0 / width))
    return (rows == cols).astype(f32).astype(bf16)


def group_sum(row, ones):
    first = row.astype(bf16).astype(f32)
    second = (row - first).astype(bf16).astype(f32)
    third = row - first - second
    index = lax.broadcasted_iota(jnp.int32, (16, row.shape[1]), 0)
    stacked = jnp.where(
        index == 0, first, jnp.where(index == 1, second, jnp.where(index == 2, third, 0.0))
    )
    return jnp.sum(dot(stacked.astype(bf16), ones), axis=0, keepdims=True)


def group_norm_silu(x):
    tokens, channels = x.shape
    width = channels // NORM_GROUPS
    ones = block_diagonal(channels, width)
    inverse = 1.0 / (tokens * width)
    average = group_sum(jnp.sum(x, axis=0, keepdims=True), ones) * inverse
    centred = x - average
    spread = group_sum(jnp.sum(centred * centred, axis=0, keepdims=True), ones) * inverse
    y = centred * lax.rsqrt(spread + EPSILON)
    return y / (1.0 + jnp.exp(-y))


def layer_norm(x):
    inverse = 1.0 / x.shape[1]
    average = jnp.sum(x, axis=1, keepdims=True) * inverse
    centred = x - average
    spread = jnp.sum(centred * centred, axis=1, keepdims=True) * inverse
    return centred * lax.rsqrt(spread + EPSILON)


def convolve(y, weight, padded):
    tokens, channels = y.shape
    column = lax.broadcasted_iota(jnp.int32, (tokens, 1), 0) & (W - 1)
    before = jnp.where(column == 0, 0.0, pltpu.roll(y, 1, 0))
    after = jnp.where(column == W - 1, 0.0, pltpu.roll(y, tokens - 1, 0))
    padded[pl.ds(0, W), :] = jnp.zeros((W, 3 * channels), bf16)
    padded[pl.ds(tokens + W, W), :] = jnp.zeros((W, 3 * channels), bf16)
    padded[pl.ds(W, tokens), :] = jnp.concatenate(
        [before.astype(bf16), y.astype(bf16), after.astype(bf16)], axis=1
    )
    total = None
    for k in range(3):
        part = dot(padded[pl.ds(k * W, tokens), :], weight[k])
        total = part if total is None else total + part
    return total


def share_kernel(act, proj, share):
    share[...] = dot(act[...], proj[...])


def first_kernel(source, weight, inner, padded):
    inner[...] = convolve(group_norm_silu(source[...].astype(f32).T), weight, padded)


def second_kernel(source, inner, bias, weight, hidden, normed, padded):
    y = group_norm_silu(inner[...] + bias[...])
    total = source[...].astype(f32).T + convolve(y, weight, padded)
    rounded = total.astype(bf16)
    hidden[...] = rounded
    normed[...] = layer_norm(rounded.astype(f32)).astype(bf16)


def assemble(where, parts, whole):
    own, count = parts[0], len(parts) // 2
    rows = own.shape[1]
    for kind in range(4):
        whole[kind, pl.ds(pl.multiple_of(where[0] * rows, 16), rows), :] = own[kind]
    for k in range(1, count + 1):
        place = pl.ds(pl.multiple_of(where[k] * rows, 16), rows)
        for j in range(2):
            mine = where[count + 1] * 2 + j
            whole[mine, place, :] = parts[k][j]
            whole[2 - mine + 2 * j, place, :] = parts[count + k][j]


def query_kernel(where, normed, *refs):
    parts = refs[:-2]
    queries, epi = refs[-2:]
    assemble(where, parts, epi)
    queries[...] = dot(normed[...], epi[0]).astype(bf16).astype(f32).T


def view_kernel(count, tiles, *refs):
    select, mask, hidden, query_ref, weights = refs[:5]
    maps = refs[5 : 5 + count]
    second, blocks, chosen, totals = refs[5 + count :]
    tokens, channels = hidden.shape
    head = channels // HEADS
    width = tokens // tiles
    scale = LOG2E / math.sqrt(head)
    queries = query_ref[...]
    lane_tile = lax.broadcasted_iota(jnp.int32, (1, tokens), 1) // width
    windows = []
    for h in range(HEADS):
        low = h * head // 128 * 128
        high = min(channels, -(-(h + 1) * head // 128) * 128)
        row = lax.broadcasted_iota(jnp.int32, (high - low, 1), 0) + low
        inside = (row >= h * head) & (row < (h + 1) * head)
        windows.append((low, high, jnp.where(inside, queries[low:high], 0.0).astype(bf16)))
    for matching in range(2):
        for j in range(count):

            @pl.when(select[matching] == j)
            def _():
                chosen[pl.ds(matching * tokens, tokens), :] = maps[j][...]

    keys = dot(chosen[...], weights[1]).astype(bf16)
    values = dot(chosen[...], weights[2]).T
    shifts = []
    for block in range(2 * tiles):
        matching, j = divmod(block, tiles)
        row = jnp.zeros((1, tokens), f32)
        for i in range(tiles):
            bit = mask[(matching * tiles + i) * tiles + j]
            row = jnp.where(lane_tile == i, jnp.where(bit > 0, 0.0, MASKED), row)
        shifts.append(row)
    for h in range(HEADS):
        low, high, wanted = windows[h]
        both = dot(keys[:, low:high], wanted)
        total = None
        for matching in range(2):
            first = matching * tiles
            scores = jnp.concatenate(
                [
                    both[k * width : (k + 1) * width] * scale + shifts[k]
                    for k in range(first, first + tiles)
                ],
                axis=0,
            )
            powers = jnp.exp2(scores - jnp.max(scores, axis=0, keepdims=True))
            norm = 1.0 / jnp.sum(powers, axis=0, keepdims=True)
            rows = values[h * head : (h + 1) * head, matching * tokens : (matching + 1) * tokens]
            part = dot(rows.astype(bf16), powers.astype(bf16)) * norm
            total = part if total is None else total + part
        totals[pl.ds(h * head, head), :] = total
    mixture = totals[...].T.astype(bf16)
    result = (hidden[...].astype(f32) + dot(mixture, weights[3])).astype(bf16)
    second[...] = result
    blocks[...] = layer_norm(result.astype(f32)).astype(bf16)


def frame_part(queries, rows, weights):
    channels = rows.shape[1]
    head = channels // HEADS
    ones = block_diagonal(channels, head)
    keys = dot(rows, weights[1]).astype(bf16).astype(f32)
    values = dot(rows, weights[2]).astype(bf16)
    products = (queries * keys).astype(bf16)
    return dot(products, ones) * (LOG2E / math.sqrt(head)), values


def own_frame_kernel(where, rows, *refs):
    parts = refs[:-4]
    weights, queries, scores, values = refs[-4:]
    assemble(where, parts, weights)
    queries[...] = dot(rows[...], weights[0]).astype(bf16)
    scores[...], values[...] = frame_part(queries[...].astype(f32), rows[...], weights)


def frame_kernel(queries, rows, weights, scores, values):
    scores[...], values[...] = frame_part(queries[...].astype(f32), rows[...], weights)


def last_kernel(frames, *refs):
    second, queries, rows, weights = refs[:4]
    scores = refs[4 : 3 + frames]
    values = refs[3 + frames : 2 + 2 * frames]
    out = refs[-1]
    last_scores, last_values = frame_part(queries[...].astype(f32), rows[...], weights)
    every = [ref[...] for ref in scores] + [last_scores]
    most = functools.reduce(jnp.maximum, every)
    powers = [jnp.exp2(one - most) for one in every]
    norm = 1.0 / functools.reduce(jnp.add, powers)
    total = (powers[-1] * norm).astype(bf16).astype(f32) * last_values.astype(f32)
    for power, value in zip(powers, values):
        total += (power * norm).astype(bf16).astype(f32) * value[...].astype(f32)
    result = second[...].astype(f32) + dot(total.astype(bf16), weights[3])
    out[...] = result.T.astype(bf16)


def is_power(n):
    return n & (n - 1) == 0


def partner_permutation(size, k):
    if is_power(size):
        return [(i, i ^ k) for i in range(size)]
    return [(i, (i + k) % size) for i in range(size)]


def partner(me, size, k, sign=1):
    if is_power(size):
        return me ^ k
    return (me + sign * k) % size


def gather_maps(own, axis, size):
    maps = {0: own}
    if is_power(size):
        bit = size // 2
        while bit:
            for k in list(maps):
                maps[k | bit] = lax.ppermute(maps[k], axis, partner_permutation(size, bit))
            bit //= 2
    else:
        for k in range(1, size):
            maps[k] = lax.ppermute(own, axis, partner_permutation(size, k))
    return [maps[k] for k in range(size)]


def sum_over(value, beside, later, axis, size):
    if not is_power(size):
        return lax.psum(value, axis), beside, later
    bit = 1
    while bit < size:
        value = value + lax.ppermute(value, axis, partner_permutation(size, bit))
        if bit == 1:
            value, beside = lax.optimization_barrier((value, beside))
        bit *= 2
    value, later = lax.optimization_barrier((value, later))
    return value, beside, later


def ring_gather(own, axis, size):
    pieces = {0: own}
    right = [(i, (i + 1) % size) for i in range(size)]
    left = [(j, i) for i, j in right]
    for step in range(1, size // 2 + 1):
        pieces[step] = lax.ppermute(pieces[step - 1], axis, right)
        if size - step > step:
            pieces[size - step] = lax.ppermute(pieces[(size - step + 1) % size], axis, left)
    return [pieces[k] for k in range(size)]


def neighbours(pieces):
    return [pieces[1], pieces[-1]] if len(pieces) > 2 else pieces[1:]


def with_neighbours(pieces, near):
    pieces = list(pieces)
    if near:
        pieces[1], pieces[-1] = near[0], near[-1]
    return pieces


def gather_weights(parts, frames, videos, video):
    kinds, rows, channels = parts.shape
    mine = lax.dynamic_index_in_dim(parts.reshape(2, 2, rows, channels), video % 2, 0, keepdims=False)
    return [parts] + ring_gather(mine, "frame", frames)[1:]


def swap_weights(parts, videos):
    return parts + [lax.ppermute(part, "video", partner_permutation(videos, 1)) for part in parts[1:]]


def per_device(
    latents,
    timesteps,
    matchings,
    tile_mask,
    conv_first,
    conv_second,
    time_proj,
    epi_in,
    epi_out,
    temp_in,
    temp_out,
):
    tokens, channels = latents.shape[2:]
    tiles = tile_mask.shape[2]
    frames = lax.axis_size("frame")
    videos = lax.axis_size("video")
    frame = lax.axis_index("frame")
    video = lax.axis_index("video")
    pixels = tokens // frames
    source = latents.reshape(tokens, channels).T

    rows = time_proj.shape[0]
    half = rows * frames // 2
    index = frame * rows + jnp.arange(rows, dtype=jnp.int32)
    exponent = jnp.where(index < half, index, index - half).astype(f32)
    frequency = jnp.exp(-math.log(10000.0) * exponent / half)
    angles = timesteps.astype(f32)[:, None] * frequency[None, :]
    wave = jnp.where(index[None, :] < half, jnp.cos(angles), jnp.sin(angles))
    time_act = jax.nn.silu(wave).astype(bf16)
    share = pl.pallas_call(
        share_kernel,
        out_shape=jax.ShapeDtypeStruct((1, channels), f32),
        in_specs=[VMEM, VMEM],
        out_specs=VMEM,
        compiler_params=params(),
        cost_estimate=pl.CostEstimate(flops=10**10, bytes_accessed=1 << 20, transcendentals=0),
        name="time_share",
    )(time_act, time_proj)
    epi_own = jnp.concatenate([epi_in, epi_out[None]], axis=0)
    temp_own = jnp.concatenate([temp_in, temp_out[None]], axis=0)
    bias, source, epi_own = sum_over(share, source, epi_own, "frame", frames)
    paired = videos % 2 == 0 and is_power(videos) and epi_own.shape[1] % 16 == 0
    if paired:
        places = [(frame - k) % frames for k in range(frames)] + [video % 2]
    else:
        places = [jnp.int32(0)] * 2
    places = jnp.stack(places).astype(jnp.int32)
    if paired:
        epi_parts = gather_weights(epi_own, frames, videos, video)
    else:
        epi_parts = [lax.all_gather(epi_own, "frame", axis=1, tiled=True)]

    conv_scratch = [
        pltpu.VMEM((tokens + 2 * W, 3 * channels), bf16),
    ]
    conv_cost = pl.CostEstimate(
        flops=2 * 9 * tokens * channels * channels,
        bytes_accessed=2 * 9 * channels * channels + 8 * tokens * channels,
        transcendentals=tokens * channels,
    )
    inner = pl.pallas_call(
        first_kernel,
        out_shape=jax.ShapeDtypeStruct((tokens, channels), f32),
        in_specs=[VMEM, VMEM],
        out_specs=VMEM,
        scratch_shapes=conv_scratch,
        compiler_params=params(),
        cost_estimate=conv_cost,
        name="first_conv",
    )(source, conv_first.reshape(3, 3 * channels, channels))
    hidden, normed = pl.pallas_call(
        second_kernel,
        out_shape=[jax.ShapeDtypeStruct((tokens, channels), bf16)] * 2,
        in_specs=[VMEM, VMEM, VMEM, VMEM],
        out_specs=[VMEM, VMEM],
        scratch_shapes=conv_scratch,
        compiler_params=params(),
        cost_estimate=conv_cost,
        name="second_conv",
    )(source, inner, bias, conv_second.reshape(3, 3 * channels, channels))

    if paired:
        normed, hidden, *near = lax.optimization_barrier((normed, hidden, *neighbours(epi_parts)))
        epi_parts = with_neighbours(epi_parts, near)
    maps = gather_maps(normed, "video", videos)
    if paired:
        temp_own, maps[1] = lax.optimization_barrier((temp_own, maps[1]))
        temp_parts = gather_weights(temp_own, frames, videos, video)
        epi_parts = swap_weights(epi_parts, videos)
    else:
        temp_parts = [lax.all_gather(temp_own, "frame", axis=1, tiled=True)]
    targets = lax.dynamic_index_in_dim(matchings, video, 1, keepdims=False)
    if is_power(videos):
        select = video ^ targets
    else:
        select = (video - targets) % videos
    mask = lax.dynamic_index_in_dim(tile_mask, video, 1, keepdims=False).reshape(-1)
    square = (4, channels, channels)
    queries, epi = pl.pallas_call(
        query_kernel,
        out_shape=[
            jax.ShapeDtypeStruct((channels, tokens), f32),
            jax.ShapeDtypeStruct(square, bf16),
        ],
        in_specs=[SMEM, VMEM] + [VMEM] * len(epi_parts),
        out_specs=[VMEM] * 2,
        compiler_params=params(),
        name="query",
    )(places, normed, *epi_parts)
    if paired:
        queries, *near = lax.optimization_barrier((queries, *neighbours(temp_parts)))
        temp_parts = with_neighbours(temp_parts, near)
    second, blocks = pl.pallas_call(
        functools.partial(view_kernel, videos, tiles),
        out_shape=[jax.ShapeDtypeStruct((tokens, channels), bf16)] * 2,
        in_specs=[SMEM, SMEM, VMEM, VMEM, VMEM] + [VMEM] * videos,
        out_specs=[VMEM, VMEM],
        scratch_shapes=[
            pltpu.VMEM((2 * tokens, channels), bf16),
            pltpu.VMEM((channels, tokens), f32),
        ],
        compiler_params=params(),
        name="cross_view",
    )(select, mask, hidden, queries, epi, *maps)

    if paired:
        blocks, *temp_parts = lax.optimization_barrier((blocks, *temp_parts))
        temp_parts = swap_weights(temp_parts, videos)
    arrived = ring_gather(blocks, "frame", frames)
    score_shape = jax.ShapeDtypeStruct((tokens, channels), f32)
    value_shape = jax.ShapeDtypeStruct((tokens, channels), bf16)
    frame_cost = pl.CostEstimate(
        flops=8 * tokens * channels * channels,
        bytes_accessed=8 * channels * channels + 8 * tokens * channels,
        transcendentals=0,
    )
    temp, frame_queries, *first = pl.pallas_call(
        own_frame_kernel,
        out_shape=[jax.ShapeDtypeStruct(square, bf16), value_shape, score_shape, value_shape],
        in_specs=[SMEM, VMEM] + [VMEM] * len(temp_parts),
        out_specs=[VMEM] * 4,
        compiler_params=params(),
        cost_estimate=frame_cost,
        name="own_frame",
    )(places, blocks, *temp_parts)
    scores, values = [first[0]], [first[1]]
    order = sorted(range(1, frames), key=lambda k: min(k, frames - k))
    for k in order[:-1]:
        one = pl.pallas_call(
            frame_kernel,
            out_shape=[score_shape, value_shape],
            in_specs=[VMEM] * 3,
            out_specs=[VMEM] * 2,
            compiler_params=params(),
            cost_estimate=frame_cost,
            name="other_frame",
        )(frame_queries, arrived[k], temp)
        scores.append(one[0])
        values.append(one[1])
    denoised = pl.pallas_call(
        functools.partial(last_kernel, frames),
        out_shape=jax.ShapeDtypeStruct((channels, tokens), bf16),
        in_specs=[VMEM] * (2 + 2 * frames),
        out_specs=VMEM,
        compiler_params=params(),
        name="last",
    )(second, frame_queries, arrived[order[-1]], temp, *scores, *values)
    return denoised.T.reshape(1, 1, tokens, channels)


def solution(mesh):
    placed = (
        P(("groups", "video"), "frame", None, None),
        P(("groups", "video")),
        P(None, "groups"),
        P(None, "groups", None, None),
        P(),
        P(),
        P("frame", None),
        P(None, "frame", None),
        P("frame", None),
        P(None, "frame", None),
        P("frame", None),
    )
    return jax.shard_map(
        per_device,
        mesh=mesh,
        in_specs=placed,
        out_specs=P(("groups", "video"), "frame", None, None),
        check_vma=False,
    )
```

```python
import functools
import math

import jax
import jax.numpy as jnp
from jax import lax
from jax.experimental import pallas as pl
from jax.experimental.pallas import tpu as pltpu
from jax.sharding import PartitionSpec as P

HEADS = 8
NORM_GROUPS = 32
TEMB = 1280
H = 8
W = 32

EPSILON = 1e-05
MASKED = -1e30
LOG2E = 1.4426950408889634
SHARE_ROWS = 16

VMEM = pl.BlockSpec(memory_space=pltpu.VMEM)
SMEM = pl.BlockSpec(memory_space=pltpu.SMEM)
HBM = pl.BlockSpec(memory_space=pl.ANY)
f32 = jnp.float32
bf16 = jnp.bfloat16


def params():
    return pltpu.CompilerParams(vmem_limit_bytes=16 * 1024 * 1024)


def in_hbm(x):
    return pltpu.with_memory_space_constraint(x, pltpu.HBM)


def fetch(source, target, sem):
    copy = pltpu.make_async_copy(source, target, sem)
    copy.start()
    return copy


def dot(a, b):
    return jnp.dot(a, b, preferred_element_type=f32)


def block_diagonal(size, width):
    rows = lax.broadcasted_iota(jnp.int32, (size, 1), 0).astype(f32)
    cols = lax.broadcasted_iota(jnp.int32, (1, size), 1).astype(f32)
    rows = jnp.floor((rows + 0.5) * (1.0 / width))
    cols = jnp.floor((cols + 0.5) * (1.0 / width))
    return (rows == cols).astype(f32).astype(bf16)


def terms(row):
    first = row.astype(bf16).astype(f32)
    second = (row - first).astype(bf16).astype(f32)
    third = row - first - second
    index = lax.broadcasted_iota(jnp.int32, (SHARE_ROWS, row.shape[1]), 0)
    return jnp.where(
        index == 0, first, jnp.where(index == 1, second, jnp.where(index == 2, third, 0.0))
    )


def group_sum(row, ones):
    return jnp.sum(dot(terms(row).astype(bf16), ones), axis=0, keepdims=True)


def group_norm_silu(x):
    tokens, channels = x.shape
    width = channels // NORM_GROUPS
    ones = block_diagonal(channels, width)
    inverse = 1.0 / (tokens * width)
    average = group_sum(jnp.sum(x, axis=0, keepdims=True), ones) * inverse
    centred = x - average
    spread = group_sum(jnp.sum(centred * centred, axis=0, keepdims=True), ones) * inverse
    y = centred * lax.rsqrt(spread + EPSILON)
    return y / (1.0 + jnp.exp(-y))


def layer_norm(x):
    inverse = 1.0 / x.shape[1]
    average = jnp.sum(x, axis=1, keepdims=True) * inverse
    centred = x - average
    spread = jnp.sum(centred * centred, axis=1, keepdims=True) * inverse
    return centred * lax.rsqrt(spread + EPSILON)


def convolve(y, weight, padded, copies):
    tokens, channels = y.shape
    column = lax.broadcasted_iota(jnp.int32, (tokens, 1), 0) & (W - 1)
    before = jnp.where(column == 0, 0.0, pltpu.roll(y, 1, 0))
    after = jnp.where(column == W - 1, 0.0, pltpu.roll(y, tokens - 1, 0))
    padded[pl.ds(0, W), :] = jnp.zeros((W, 3 * channels), bf16)
    padded[pl.ds(tokens + W, W), :] = jnp.zeros((W, 3 * channels), bf16)
    padded[pl.ds(W, tokens), :] = jnp.concatenate(
        [before.astype(bf16), y.astype(bf16), after.astype(bf16)], axis=1
    )
    total = None
    for k in range(3):
        if copies:
            copies[k].wait()
        part = dot(padded[pl.ds(k * W, tokens), :], weight[k])
        total = part if total is None else total + part
    return total


def share_kernel(act, proj_hbm, share, proj, sem):
    fetch(proj_hbm, proj, sem).wait()
    share[...] = dot(act[...], proj[...])


def first_kernel(source_hbm, weight_hbm, inner, turned, source, weight, padded, sems):
    copy = fetch(source_hbm, source, sems.at[0])
    copies = [fetch(weight_hbm.at[k], weight.at[k], sems.at[1 + k]) for k in range(3)]
    copy.wait()
    rows = source[...].astype(f32).T
    turned[...] = rows.astype(bf16)
    inner[...] = convolve(group_norm_silu(rows), weight, padded, copies)


def second_kernel(source, inner, bias, weight, hidden, normed, padded):
    y = group_norm_silu(inner[...] + bias[...])
    total = convolve(y, weight, padded, [])
    rounded = (source[...].astype(f32) + total).astype(bf16)
    hidden[...] = rounded
    normed[...] = layer_norm(rounded.astype(f32)).astype(bf16)


def fetch_own(where, three, one, whole, sems):
    rows = one.shape[0]
    place = pl.ds(pl.multiple_of(where[0] * rows, 16), rows)
    copies = [fetch(three.at[k], whole.at[k, place], sems.at[k]) for k in range(3)]
    return copies + [fetch(one, whole.at[3, place], sems.at[3])]


def assemble(where, side, parts, whole, rows, first):
    count = len(parts) // 2
    for k in range(count):
        place = pl.ds(pl.multiple_of(where[k + 1] * rows, 16), rows)
        for j in range(2):
            block = pl.ds((first + j) * rows, rows)
            mine = side * 2 + j
            whole[mine, place, :] = parts[k][block, :]
            whole[2 - mine + 2 * j, place, :] = parts[count + k][block, :]


def query_kernel(where, normed, three, one, *refs):
    parts, (queries, epi, sems) = refs[:-3], refs[-3:]
    copies = fetch_own(where, three, one, epi, sems)
    assemble(where, where[len(parts) // 2 + 1], parts, epi, one.shape[0], 0)
    for copy in copies:
        copy.wait()
    queries[...] = dot(normed[...], epi[0]).astype(bf16).astype(f32).T


def view_kernel(count, tiles, *refs):
    select, mask, hidden_ref, query_ref, weights = refs[:5]
    maps = refs[5 : 5 + count]
    second, blocks, chosen, totals, hidden, sem = refs[5 + count :]
    copy = fetch(hidden_ref, hidden, sem)
    tokens, channels = hidden.shape
    head = channels // HEADS
    width = tokens // tiles
    scale = LOG2E / math.sqrt(head)
    queries = query_ref[...]
    lane_tile = lax.broadcasted_iota(jnp.int32, (1, tokens), 1) // width
    windows = []
    for h in range(HEADS):
        low = h * head // 128 * 128
        high = min(channels, -(-(h + 1) * head // 128) * 128)
        row = lax.broadcasted_iota(jnp.int32, (high - low, 1), 0) + low
        inside = (row >= h * head) & (row < (h + 1) * head)
        windows.append((low, high, jnp.where(inside, queries[low:high], 0.0).astype(bf16)))
    for matching in range(2):
        for j in range(count):

            @pl.when(select[matching] == j)
            def _():
                chosen[pl.ds(matching * tokens, tokens), :] = maps[j][...]

    keys = dot(chosen[...], weights[1]).astype(bf16)
    values = dot(chosen[...], weights[2]).T
    shifts = []
    for block in range(2 * tiles):
        matching, j = divmod(block, tiles)
        row = jnp.zeros((1, tokens), f32)
        for i in range(tiles):
            bit = mask[(matching * tiles + i) * tiles + j]
            row = jnp.where(lane_tile == i, jnp.where(bit > 0, 0.0, MASKED), row)
        shifts.append(row)
    for h in range(HEADS):
        low, high, wanted = windows[h]
        both = dot(keys[:, low:high], wanted)
        total = None
        for matching in range(2):
            first = matching * tiles
            scores = jnp.concatenate(
                [
                    both[k * width : (k + 1) * width] * scale + shifts[k]
                    for k in range(first, first + tiles)
                ],
                axis=0,
            )
            powers = jnp.exp2(scores - jnp.max(scores, axis=0, keepdims=True))
            norm = 1.0 / jnp.sum(powers, axis=0, keepdims=True)
            rows = values[h * head : (h + 1) * head, matching * tokens : (matching + 1) * tokens]
            part = dot(rows.astype(bf16), powers.astype(bf16)) * norm
            total = part if total is None else total + part
        totals[pl.ds(h * head, head), :] = total
    mixture = totals[...].T.astype(bf16)
    copy.wait()
    result = (hidden[...].astype(f32) + dot(mixture, weights[3])).astype(bf16)
    second[...] = result
    blocks[...] = layer_norm(result.astype(f32)).astype(bf16)


def frame_part(queries, rows, weights):
    channels = rows.shape[1]
    head = channels // HEADS
    ones = block_diagonal(channels, head)
    keys = dot(rows, weights[1]).astype(bf16).astype(f32)
    values = dot(rows, weights[2]).astype(bf16)
    products = (queries * keys).astype(bf16)
    return dot(products, ones) * (LOG2E / math.sqrt(head)), values


def own_frame_kernel(where, rows, three, one, *refs):
    parts, (weights, queries, scores, values, sems) = refs[:-5], refs[-5:]
    copies = fetch_own(where, three, one, weights, sems)
    assemble(where, where[len(parts) // 2 + 1], parts, weights, one.shape[0], 2)
    for copy in copies:
        copy.wait()
    queries[...] = dot(rows[...], weights[0]).astype(bf16)
    scores[...], values[...] = frame_part(queries[...].astype(f32), rows[...], weights)


def frame_kernel(queries, rows, weights, scores, values):
    scores[...], values[...] = frame_part(queries[...].astype(f32), rows[...], weights)


def last_kernel(frames, *refs):
    second, queries, rows, weights = refs[:4]
    scores = refs[4 : 3 + frames]
    values = refs[3 + frames : 2 + 2 * frames]
    out = refs[-1]
    last_scores, last_values = frame_part(queries[...].astype(f32), rows[...], weights)
    every = [ref[...] for ref in scores] + [last_scores]
    most = functools.reduce(jnp.maximum, every)
    powers = [jnp.exp2(one - most) for one in every]
    norm = 1.0 / functools.reduce(jnp.add, powers)
    total = (powers[-1] * norm).astype(bf16).astype(f32) * last_values.astype(f32)
    for power, value in zip(powers, values):
        total += (power * norm).astype(bf16).astype(f32) * value[...].astype(f32)
    result = second[...].astype(f32) + dot(total.astype(bf16), weights[3])
    out[...] = result.T.astype(bf16)


def is_power(n):
    return n & (n - 1) == 0


def partner_permutation(size, k):
    if is_power(size):
        return [(i, i ^ k) for i in range(size)]
    return [(i, (i + k) % size) for i in range(size)]


def partner(me, size, k, sign=1):
    if is_power(size):
        return me ^ k
    return (me + sign * k) % size


def gather_maps(own, axis, size, beside=None):
    maps = {0: own}
    if is_power(size):
        bit = size // 2
        while bit:
            for k in list(maps):
                sent = maps[k] if k == 0 or beside is None else after(maps[k], beside)
                maps[k | bit] = lax.ppermute(sent, axis, partner_permutation(size, bit))
            bit //= 2
    else:
        for k in range(1, size):
            maps[k] = lax.ppermute(own, axis, partner_permutation(size, k))
    return [maps[k] for k in range(size)]


def sum_over(value, axis, size):
    if not is_power(size):
        return lax.psum(value, axis)
    bit = 1
    while bit < size:
        value = value + lax.ppermute(value, axis, partner_permutation(size, bit))
        bit *= 2
    return value


def after(x, *others):
    return lax.optimization_barrier((x, *others))[0]


def ring_gather(own, axis, size, beside=None):
    pieces = {0: own}
    right = [(i, (i + 1) % size) for i in range(size)]
    left = [(j, i) for i, j in right]
    for step in range(1, size // 2 + 1):
        pieces[step] = lax.ppermute(pieces[step - 1], axis, right)
        if size - step > step:
            pieces[size - step] = lax.ppermute(pieces[(size - step + 1) % size], axis, left)
        if step == 1 and beside is not None:
            pieces[1] = after(pieces[1], beside)
    return [pieces[k] for k in range(size)]


def half_of(three, one, side):
    whole = jnp.concatenate([three, one[None]], axis=0)
    whole = whole.reshape(2, 2 * one.shape[0], one.shape[1])
    return lax.dynamic_index_in_dim(whole, side, 0, keepdims=False)


def swap(pieces, videos):
    return [lax.ppermute(piece, "video", partner_permutation(videos, 1)) for piece in pieces]


def per_device(
    latents,
    timesteps,
    matchings,
    tile_mask,
    conv_first,
    conv_second,
    time_proj,
    epi_in,
    epi_out,
    temp_in,
    temp_out,
):
    tokens, channels = latents.shape[2:]
    tiles = tile_mask.shape[2]
    frames = lax.axis_size("frame")
    videos = lax.axis_size("video")
    frame = lax.axis_index("frame")
    video = lax.axis_index("video")
    pixels = tokens // frames
    source = latents.reshape(tokens, channels).T

    rows = time_proj.shape[0]
    half = rows * frames // 2
    index = frame * rows + jnp.arange(rows, dtype=jnp.int32)
    exponent = jnp.where(index < half, index, index - half).astype(f32)
    frequency = jnp.exp(-math.log(10000.0) * exponent / half)
    angles = timesteps.astype(f32)[:, None] * frequency[None, :]
    wave = jnp.where(index[None, :] < half, jnp.cos(angles), jnp.sin(angles))
    time_act = jax.nn.silu(wave).astype(bf16)
    height = epi_out.shape[0]
    paired = videos % 2 == 0 and is_power(videos) and height % 16 == 0
    early = pl.CostEstimate(flops=10**10, bytes_accessed=1 << 20, transcendentals=0)
    share = pl.pallas_call(
        share_kernel,
        out_shape=jax.ShapeDtypeStruct((1, channels), f32),
        in_specs=[VMEM, HBM],
        out_specs=VMEM,
        scratch_shapes=[pltpu.VMEM(time_proj.shape, bf16), pltpu.SemaphoreType.DMA],
        compiler_params=params(),
        cost_estimate=early,
        name="time_share",
    )(time_act, in_hbm(time_proj))
    bias = sum_over(share, "frame", frames)
    if paired:
        steps = [frame - k for k in range(frames)]
        places = [step % frames for step in steps] + [video % 2]
    else:
        places = [jnp.int32(0)] * 2
        epi_in = lax.all_gather(epi_in, "frame", axis=1, tiled=True)
        epi_out = lax.all_gather(epi_out, "frame", axis=0, tiled=True)
        temp_in = lax.all_gather(temp_in, "frame", axis=1, tiled=True)
        temp_out = lax.all_gather(temp_out, "frame", axis=0, tiled=True)
    places = jnp.stack(places).astype(jnp.int32)

    source_scratch = pltpu.VMEM((channels, tokens), bf16)
    padded_scratch = pltpu.VMEM((tokens + 2 * W, 3 * channels), bf16)
    conv_cost = pl.CostEstimate(
        flops=2 * 9 * tokens * channels * channels,
        bytes_accessed=2 * 9 * channels * channels + 8 * tokens * channels,
        transcendentals=tokens * channels,
    )
    inner, turned = pl.pallas_call(
        first_kernel,
        out_shape=[
            jax.ShapeDtypeStruct((tokens, channels), f32),
            jax.ShapeDtypeStruct((tokens, channels), bf16),
        ],
        in_specs=[HBM, HBM],
        out_specs=[VMEM, VMEM],
        scratch_shapes=[
            source_scratch,
            pltpu.VMEM((3, 3 * channels, channels), bf16),
            padded_scratch,
            pltpu.SemaphoreType.DMA((4,)),
        ],
        compiler_params=params(),
        cost_estimate=conv_cost,
        name="first_conv",
    )(in_hbm(source), in_hbm(conv_first.reshape(3, 3 * channels, channels)))
    hidden, normed = pl.pallas_call(
        second_kernel,
        out_shape=[
            jax.ShapeDtypeStruct((tokens, channels), bf16),
            jax.ShapeDtypeStruct((tokens, channels), bf16),
        ],
        in_specs=[VMEM] * 4,
        out_specs=[VMEM] * 2,
        scratch_shapes=[padded_scratch],
        compiler_params=params(),
        cost_estimate=conv_cost,
        name="second_conv",
    )(turned, inner, bias, conv_second.reshape(3, 3 * channels, channels))
    parts = []
    last_part = None
    if paired:
        mine = jnp.concatenate(
            [half_of(epi_in, epi_out, video % 2), half_of(temp_in, temp_out, video % 2)], axis=0
        )
        parts = ring_gather(after(mine, bias), "frame", frames, normed)
        normed = after(normed, parts[1 % frames], parts[-1])
        last_part = parts[frames // 2]
    maps = gather_maps(normed, "video", videos, last_part)
    epi_parts = temp_parts = []
    if paired:
        parts = parts[1:]
        epi_parts = temp_parts = parts + swap(parts, videos)
    targets = lax.dynamic_index_in_dim(matchings, video, 1, keepdims=False)
    if is_power(videos):
        select = video ^ targets
    else:
        select = (video - targets) % videos
    mask = lax.dynamic_index_in_dim(tile_mask, video, 1, keepdims=False).reshape(-1)
    square = (4, channels, channels)
    queries, epi = pl.pallas_call(
        query_kernel,
        out_shape=[
            jax.ShapeDtypeStruct((channels, tokens), f32),
            jax.ShapeDtypeStruct(square, bf16),
        ],
        in_specs=[SMEM, VMEM, HBM, HBM] + [VMEM] * len(epi_parts),
        out_specs=[VMEM] * 2,
        scratch_shapes=[pltpu.SemaphoreType.DMA((4,))],
        compiler_params=params(),
        name="query",
    )(places, normed, in_hbm(epi_in), in_hbm(epi_out), *epi_parts)
    second, blocks = pl.pallas_call(
        functools.partial(view_kernel, videos, tiles),
        out_shape=[jax.ShapeDtypeStruct((tokens, channels), bf16)] * 2,
        in_specs=[SMEM, SMEM, HBM, VMEM, VMEM] + [VMEM] * videos,
        out_specs=[VMEM, VMEM],
        scratch_shapes=[
            pltpu.VMEM((2 * tokens, channels), bf16),
            pltpu.VMEM((channels, tokens), f32),
            pltpu.VMEM((tokens, channels), bf16),
            pltpu.SemaphoreType.DMA,
        ],
        compiler_params=params(),
        name="cross_view",
    )(select, mask, hidden, queries, epi, *maps)

    arrived = ring_gather(blocks, "frame", frames)
    score_shape = jax.ShapeDtypeStruct((tokens, channels), f32)
    value_shape = jax.ShapeDtypeStruct((tokens, channels), bf16)
    frame_cost = pl.CostEstimate(
        flops=8 * tokens * channels * channels,
        bytes_accessed=8 * channels * channels + 8 * tokens * channels,
        transcendentals=0,
    )
    temp, frame_queries, *first = pl.pallas_call(
        own_frame_kernel,
        out_shape=[jax.ShapeDtypeStruct(square, bf16), value_shape, score_shape, value_shape],
        in_specs=[SMEM, VMEM, HBM, HBM] + [VMEM] * len(epi_parts),
        out_specs=[VMEM] * 4,
        scratch_shapes=[pltpu.SemaphoreType.DMA((4,))],
        compiler_params=params(),
        cost_estimate=frame_cost,
        name="own_frame",
    )(places, blocks, in_hbm(temp_in), in_hbm(temp_out), *temp_parts)
    scores, values = [first[0]], [first[1]]
    order = sorted(range(1, frames), key=lambda k: min(k, frames - k))
    for k in order[:-1]:
        one = pl.pallas_call(
            frame_kernel,
            out_shape=[score_shape, value_shape],
            in_specs=[VMEM] * 3,
            out_specs=[VMEM] * 2,
            compiler_params=params(),
            cost_estimate=frame_cost,
            name="other_frame",
        )(frame_queries, arrived[k], temp)
        scores.append(one[0])
        values.append(one[1])
    denoised = pl.pallas_call(
        functools.partial(last_kernel, frames),
        out_shape=jax.ShapeDtypeStruct((channels, tokens), bf16),
        in_specs=[VMEM] * (2 + 2 * frames),
        out_specs=VMEM,
        compiler_params=params(),
        name="last",
    )(second, frame_queries, arrived[order[-1]], temp, *scores, *values)
    return denoised.T.reshape(1, 1, tokens, channels)


def solution(mesh):
    placed = (
        P(("groups", "video"), "frame", None, None),
        P(("groups", "video")),
        P(None, "groups"),
        P(None, "groups", None, None),
        P(),
        P(),
        P("frame", None),
        P(None, "frame", None),
        P("frame", None),
        P(None, "frame", None),
        P("frame", None),
    )
    return jax.shard_map(
        per_device,
        mesh=mesh,
        in_specs=placed,
        out_specs=P(("groups", "video"), "frame", None, None),
        check_vma=False,
    )
```

```python
import functools
import math

import jax
import jax.numpy as jnp
from jax import lax
from jax.experimental import pallas as pl
from jax.experimental.pallas import tpu as pltpu
from jax.sharding import PartitionSpec as P

HEADS = 8
NORM_GROUPS = 32
TEMB = 1280
H = 8
W = 32

EPSILON = 1e-05
MASKED = -1e30
LOG2E = 1.4426950408889634
SHARE_ROWS = 16

VMEM = pl.BlockSpec(memory_space=pltpu.VMEM)
SMEM = pl.BlockSpec(memory_space=pltpu.SMEM)
HBM = pl.BlockSpec(memory_space=pl.ANY)
f32 = jnp.float32
bf16 = jnp.bfloat16


def params():
    return pltpu.CompilerParams(vmem_limit_bytes=16 * 1024 * 1024)


def in_hbm(x):
    return pltpu.with_memory_space_constraint(x, pltpu.HBM)


def fetch(source, target, sem):
    copy = pltpu.make_async_copy(source, target, sem)
    copy.start()
    return copy


def dot(a, b):
    return jnp.dot(a, b, preferred_element_type=f32)


def block_diagonal(size, width):
    rows = lax.broadcasted_iota(jnp.int32, (size, 1), 0).astype(f32)
    cols = lax.broadcasted_iota(jnp.int32, (1, size), 1).astype(f32)
    rows = jnp.floor((rows + 0.5) * (1.0 / width))
    cols = jnp.floor((cols + 0.5) * (1.0 / width))
    return (rows == cols).astype(f32).astype(bf16)


def terms(row):
    first = row.astype(bf16).astype(f32)
    second = (row - first).astype(bf16).astype(f32)
    third = row - first - second
    index = lax.broadcasted_iota(jnp.int32, (SHARE_ROWS, row.shape[1]), 0)
    return jnp.where(
        index == 0, first, jnp.where(index == 1, second, jnp.where(index == 2, third, 0.0))
    )


def group_sum(row, ones):
    return jnp.sum(dot(terms(row).astype(bf16), ones), axis=0, keepdims=True)


def group_norm_silu(x):
    tokens, channels = x.shape
    width = channels // NORM_GROUPS
    ones = block_diagonal(channels, width)
    inverse = 1.0 / (tokens * width)
    average = group_sum(jnp.sum(x, axis=0, keepdims=True), ones) * inverse
    centred = x - average
    spread = group_sum(jnp.sum(centred * centred, axis=0, keepdims=True), ones) * inverse
    y = centred * lax.rsqrt(spread + EPSILON)
    return y / (1.0 + jnp.exp(-y))


def layer_norm(x):
    inverse = 1.0 / x.shape[1]
    average = jnp.sum(x, axis=1, keepdims=True) * inverse
    centred = x - average
    spread = jnp.sum(centred * centred, axis=1, keepdims=True) * inverse
    return centred * lax.rsqrt(spread + EPSILON)


def convolve(y, weight, padded, copies):
    tokens, channels = y.shape
    column = lax.broadcasted_iota(jnp.int32, (tokens, 1), 0) & (W - 1)
    before = jnp.where(column == 0, 0.0, pltpu.roll(y, 1, 0))
    after = jnp.where(column == W - 1, 0.0, pltpu.roll(y, tokens - 1, 0))
    padded[pl.ds(0, W), :] = jnp.zeros((W, 3 * channels), bf16)
    padded[pl.ds(tokens + W, W), :] = jnp.zeros((W, 3 * channels), bf16)
    padded[pl.ds(W, tokens), :] = jnp.concatenate(
        [before.astype(bf16), y.astype(bf16), after.astype(bf16)], axis=1
    )
    total = None
    for k in range(3):
        if copies:
            copies[k].wait()
        part = dot(padded[pl.ds(k * W, tokens), :], weight[k])
        total = part if total is None else total + part
    return total


def share_kernel(act, proj_hbm, share, proj, sem):
    fetch(proj_hbm, proj, sem).wait()
    share[...] = dot(act[...], proj[...])


def first_kernel(source_hbm, weight_hbm, inner, turned, source, weight, padded, sems):
    copy = fetch(source_hbm, source, sems.at[0])
    copies = [fetch(weight_hbm.at[k], weight.at[k], sems.at[1 + k]) for k in range(3)]
    copy.wait()
    rows = source[...].astype(f32).T
    turned[...] = rows.astype(bf16)
    inner[...] = convolve(group_norm_silu(rows), weight, padded, copies)


def second_kernel(source, inner, bias, weight, hidden, normed, padded):
    y = group_norm_silu(inner[...] + bias[...])
    total = convolve(y, weight, padded, [])
    rounded = (source[...].astype(f32) + total).astype(bf16)
    hidden[...] = rounded
    normed[...] = layer_norm(rounded.astype(f32)).astype(bf16)


def fetch_own(where, three, one, whole, sems):
    rows = one.shape[0]
    place = pl.ds(pl.multiple_of(where[0] * rows, 16), rows)
    copies = [fetch(three.at[k], whole.at[k, place], sems.at[k]) for k in range(3)]
    return copies + [fetch(one, whole.at[3, place], sems.at[3])]


def assemble(where, side, parts, whole, rows, first):
    count = len(parts) // 2
    for k in range(count):
        place = pl.ds(pl.multiple_of(where[k + 1] * rows, 16), rows)
        for j in range(2):
            block = pl.ds((first + j) * rows, rows)
            mine = side * 2 + j
            whole[mine, place, :] = parts[k][block, :]
            whole[2 - mine + 2 * j, place, :] = parts[count + k][block, :]


def query_kernel(where, normed, three, one, *refs):
    parts, (queries, epi, sems) = refs[:-3], refs[-3:]
    copies = fetch_own(where, three, one, epi, sems)
    assemble(where, where[len(parts) // 2 + 1], parts, epi, one.shape[0], 0)
    for copy in copies:
        copy.wait()
    queries[...] = dot(normed[...], epi[0]).astype(bf16).astype(f32).T


def view_kernel(count, tiles, *refs):
    select, mask, hidden_ref, query_ref, weights = refs[:5]
    maps = refs[5 : 5 + count]
    second, blocks, chosen, totals, hidden, sem = refs[5 + count :]
    copy = fetch(hidden_ref, hidden, sem)
    tokens, channels = hidden.shape
    head = channels // HEADS
    width = tokens // tiles
    scale = LOG2E / math.sqrt(head)
    queries = query_ref[...]
    lane_tile = lax.broadcasted_iota(jnp.int32, (1, tokens), 1) // width
    windows = []
    for h in range(HEADS):
        low = h * head // 128 * 128
        high = min(channels, -(-(h + 1) * head // 128) * 128)
        row = lax.broadcasted_iota(jnp.int32, (high - low, 1), 0) + low
        inside = (row >= h * head) & (row < (h + 1) * head)
        windows.append((low, high, jnp.where(inside, queries[low:high], 0.0).astype(bf16)))
    for matching in range(2):
        for j in range(count):

            @pl.when(select[matching] == j)
            def _():
                chosen[pl.ds(matching * tokens, tokens), :] = maps[j][...]

    keys = dot(chosen[...], weights[1]).astype(bf16)
    values = dot(chosen[...], weights[2]).T
    shifts = []
    for block in range(2 * tiles):
        matching, j = divmod(block, tiles)
        row = jnp.zeros((1, tokens), f32)
        for i in range(tiles):
            bit = mask[(matching * tiles + i) * tiles + j]
            row = jnp.where(lane_tile == i, jnp.where(bit > 0, 0.0, MASKED), row)
        shifts.append(row)
    for h in range(HEADS):
        low, high, wanted = windows[h]
        both = dot(keys[:, low:high], wanted)
        total = None
        for matching in range(2):
            first = matching * tiles
            scores = jnp.concatenate(
                [
                    both[k * width : (k + 1) * width] * scale + shifts[k]
                    for k in range(first, first + tiles)
                ],
                axis=0,
            )
            powers = jnp.exp2(scores - jnp.max(scores, axis=0, keepdims=True))
            norm = 1.0 / jnp.sum(powers, axis=0, keepdims=True)
            rows = values[h * head : (h + 1) * head, matching * tokens : (matching + 1) * tokens]
            part = dot(rows.astype(bf16), powers.astype(bf16)) * norm
            total = part if total is None else total + part
        totals[pl.ds(h * head, head), :] = total
    mixture = totals[...].T.astype(bf16)
    copy.wait()
    result = (hidden[...].astype(f32) + dot(mixture, weights[3])).astype(bf16)
    second[...] = result
    blocks[...] = layer_norm(result.astype(f32)).astype(bf16)


def frame_part(queries, rows, weights):
    channels = rows.shape[1]
    head = channels // HEADS
    ones = block_diagonal(channels, head)
    keys = dot(rows, weights[1]).astype(bf16).astype(f32)
    values = dot(rows, weights[2]).astype(bf16)
    products = (queries * keys).astype(bf16)
    return dot(products, ones) * (LOG2E / math.sqrt(head)), values


def own_frame_kernel(where, rows, three, one, *refs):
    parts, (weights, queries, scores, values, sems) = refs[:-5], refs[-5:]
    copies = fetch_own(where, three, one, weights, sems)
    assemble(where, where[len(parts) // 2 + 1], parts, weights, one.shape[0], 2)
    for copy in copies:
        copy.wait()
    queries[...] = dot(rows[...], weights[0]).astype(bf16)
    scores[...], values[...] = frame_part(queries[...].astype(f32), rows[...], weights)


def frame_kernel(queries, rows, weights, scores, values):
    scores[...], values[...] = frame_part(queries[...].astype(f32), rows[...], weights)


def last_kernel(frames, *refs):
    second, queries, rows, weights = refs[:4]
    scores = refs[4 : 3 + frames]
    values = refs[3 + frames : 2 + 2 * frames]
    out = refs[-1]
    last_scores, last_values = frame_part(queries[...].astype(f32), rows[...], weights)
    every = [ref[...] for ref in scores] + [last_scores]
    most = functools.reduce(jnp.maximum, every)
    powers = [jnp.exp2(one - most) for one in every]
    norm = 1.0 / functools.reduce(jnp.add, powers)
    total = (powers[-1] * norm).astype(bf16).astype(f32) * last_values.astype(f32)
    for power, value in zip(powers, values):
        total += (power * norm).astype(bf16).astype(f32) * value[...].astype(f32)
    result = second[...].astype(f32) + dot(total.astype(bf16), weights[3])
    out[...] = result.T.astype(bf16)


def is_power(n):
    return n & (n - 1) == 0


def partner_permutation(size, k):
    if is_power(size):
        return [(i, i ^ k) for i in range(size)]
    return [(i, (i + k) % size) for i in range(size)]


def partner(me, size, k, sign=1):
    if is_power(size):
        return me ^ k
    return (me + sign * k) % size


def gather_maps(own, axis, size, beside=None):
    maps = {0: own}
    if is_power(size):
        bit = size // 2
        while bit:
            for k in list(maps):
                sent = maps[k] if k == 0 or beside is None else after(maps[k], beside)
                maps[k | bit] = lax.ppermute(sent, axis, partner_permutation(size, bit))
            bit //= 2
    else:
        for k in range(1, size):
            maps[k] = lax.ppermute(own, axis, partner_permutation(size, k))
    return [maps[k] for k in range(size)]


def sum_over(value, axis, size):
    if not is_power(size):
        return lax.psum(value, axis)
    bit = 1
    while bit < size:
        value = value + lax.ppermute(value, axis, partner_permutation(size, bit))
        bit *= 2
    return value


def after(x, *others):
    return lax.optimization_barrier((x, *others))[0]


def ring_gather(own, axis, size, beside=None):
    pieces = {0: own}
    right = [(i, (i + 1) % size) for i in range(size)]
    left = [(j, i) for i, j in right]
    for step in range(1, size // 2 + 1):
        pieces[step] = lax.ppermute(pieces[step - 1], axis, right)
        if size - step > step:
            pieces[size - step] = lax.ppermute(pieces[(size - step + 1) % size], axis, left)
        if step == 1 and beside is not None:
            pieces[1] = after(pieces[1], beside)
    return [pieces[k] for k in range(size)]


def half_of(three, one, side):
    whole = jnp.concatenate([three, one[None]], axis=0)
    whole = whole.reshape(2, 2 * one.shape[0], one.shape[1])
    return lax.dynamic_index_in_dim(whole, side, 0, keepdims=False)


def swap(pieces, videos):
    return [lax.ppermute(piece, "video", partner_permutation(videos, 1)) for piece in pieces]


def per_device(
    latents,
    timesteps,
    matchings,
    tile_mask,
    conv_first,
    conv_second,
    time_proj,
    epi_in,
    epi_out,
    temp_in,
    temp_out,
):
    tokens, channels = latents.shape[2:]
    tiles = tile_mask.shape[2]
    frames = lax.axis_size("frame")
    videos = lax.axis_size("video")
    frame = lax.axis_index("frame")
    video = lax.axis_index("video")
    pixels = tokens // frames
    source = latents.reshape(tokens, channels).T

    rows = time_proj.shape[0]
    half = rows * frames // 2
    index = frame * rows + jnp.arange(rows, dtype=jnp.int32)
    exponent = jnp.where(index < half, index, index - half).astype(f32)
    frequency = jnp.exp(-math.log(10000.0) * exponent / half)
    angles = timesteps.astype(f32)[:, None] * frequency[None, :]
    wave = jnp.where(index[None, :] < half, jnp.cos(angles), jnp.sin(angles))
    time_act = jax.nn.silu(wave).astype(bf16)
    height = epi_out.shape[0]
    paired = videos % 2 == 0 and is_power(videos) and height % 16 == 0
    early = pl.CostEstimate(flops=10**10, bytes_accessed=1 << 20, transcendentals=0)
    share = pl.pallas_call(
        share_kernel,
        out_shape=jax.ShapeDtypeStruct((1, channels), f32),
        in_specs=[VMEM, HBM],
        out_specs=VMEM,
        scratch_shapes=[pltpu.VMEM(time_proj.shape, bf16), pltpu.SemaphoreType.DMA],
        compiler_params=params(),
        cost_estimate=early,
        name="time_share",
    )(time_act, in_hbm(time_proj))
    bias = sum_over(share, "frame", frames)
    if paired:
        steps = [frame - k for k in range(frames)]
        places = [step % frames for step in steps] + [video % 2]
    else:
        places = [jnp.int32(0)] * 2
        epi_in = lax.all_gather(epi_in, "frame", axis=1, tiled=True)
        epi_out = lax.all_gather(epi_out, "frame", axis=0, tiled=True)
        temp_in = lax.all_gather(temp_in, "frame", axis=1, tiled=True)
        temp_out = lax.all_gather(temp_out, "frame", axis=0, tiled=True)
    places = jnp.stack(places).astype(jnp.int32)

    source_scratch = pltpu.VMEM((channels, tokens), bf16)
    padded_scratch = pltpu.VMEM((tokens + 2 * W, 3 * channels), bf16)
    conv_cost = pl.CostEstimate(
        flops=2 * 9 * tokens * channels * channels,
        bytes_accessed=2 * 9 * channels * channels + 8 * tokens * channels,
        transcendentals=tokens * channels,
    )
    inner, turned = pl.pallas_call(
        first_kernel,
        out_shape=[
            jax.ShapeDtypeStruct((tokens, channels), f32),
            jax.ShapeDtypeStruct((tokens, channels), bf16),
        ],
        in_specs=[HBM, HBM],
        out_specs=[VMEM, VMEM],
        scratch_shapes=[
            source_scratch,
            pltpu.VMEM((3, 3 * channels, channels), bf16),
            padded_scratch,
            pltpu.SemaphoreType.DMA((4,)),
        ],
        compiler_params=params(),
        cost_estimate=conv_cost,
        name="first_conv",
    )(in_hbm(source), in_hbm(conv_first.reshape(3, 3 * channels, channels)))
    hidden, normed = pl.pallas_call(
        second_kernel,
        out_shape=[
            jax.ShapeDtypeStruct((tokens, channels), bf16),
            jax.ShapeDtypeStruct((tokens, channels), bf16),
        ],
        in_specs=[VMEM] * 4,
        out_specs=[VMEM] * 2,
        scratch_shapes=[padded_scratch],
        compiler_params=params(),
        cost_estimate=conv_cost,
        name="second_conv",
    )(turned, inner, bias, conv_second.reshape(3, 3 * channels, channels))
    parts = []
    last_part = None
    if paired:
        mine = jnp.concatenate(
            [half_of(epi_in, epi_out, video % 2), half_of(temp_in, temp_out, video % 2)], axis=0
        )
        parts = ring_gather(after(mine, bias), "frame", frames, normed)
        normed = after(normed, parts[1 % frames])
        last_part = parts[frames // 2]
    maps = gather_maps(normed, "video", videos, last_part)
    epi_parts = temp_parts = []
    if paired:
        parts = parts[1:]
        epi_parts = temp_parts = parts + swap(parts, videos)
    targets = lax.dynamic_index_in_dim(matchings, video, 1, keepdims=False)
    if is_power(videos):
        select = video ^ targets
    else:
        select = (video - targets) % videos
    mask = lax.dynamic_index_in_dim(tile_mask, video, 1, keepdims=False).reshape(-1)
    square = (4, channels, channels)
    queries, epi = pl.pallas_call(
        query_kernel,
        out_shape=[
            jax.ShapeDtypeStruct((channels, tokens), f32),
            jax.ShapeDtypeStruct(square, bf16),
        ],
        in_specs=[SMEM, VMEM, HBM, HBM] + [VMEM] * len(epi_parts),
        out_specs=[VMEM] * 2,
        scratch_shapes=[pltpu.SemaphoreType.DMA((4,))],
        compiler_params=params(),
        name="query",
    )(places, normed, in_hbm(epi_in), in_hbm(epi_out), *epi_parts)
    second, blocks = pl.pallas_call(
        functools.partial(view_kernel, videos, tiles),
        out_shape=[jax.ShapeDtypeStruct((tokens, channels), bf16)] * 2,
        in_specs=[SMEM, SMEM, HBM, VMEM, VMEM] + [VMEM] * videos,
        out_specs=[VMEM, VMEM],
        scratch_shapes=[
            pltpu.VMEM((2 * tokens, channels), bf16),
            pltpu.VMEM((channels, tokens), f32),
            pltpu.VMEM((tokens, channels), bf16),
            pltpu.SemaphoreType.DMA,
        ],
        compiler_params=params(),
        name="cross_view",
    )(select, mask, hidden, queries, epi, *maps)

    arrived = ring_gather(blocks, "frame", frames)
    score_shape = jax.ShapeDtypeStruct((tokens, channels), f32)
    value_shape = jax.ShapeDtypeStruct((tokens, channels), bf16)
    frame_cost = pl.CostEstimate(
        flops=8 * tokens * channels * channels,
        bytes_accessed=8 * channels * channels + 8 * tokens * channels,
        transcendentals=0,
    )
    temp, frame_queries, *first = pl.pallas_call(
        own_frame_kernel,
        out_shape=[jax.ShapeDtypeStruct(square, bf16), value_shape, score_shape, value_shape],
        in_specs=[SMEM, VMEM, HBM, HBM] + [VMEM] * len(epi_parts),
        out_specs=[VMEM] * 4,
        scratch_shapes=[pltpu.SemaphoreType.DMA((4,))],
        compiler_params=params(),
        cost_estimate=frame_cost,
        name="own_frame",
    )(places, blocks, in_hbm(temp_in), in_hbm(temp_out), *temp_parts)
    scores, values = [first[0]], [first[1]]
    order = sorted(range(1, frames), key=lambda k: min(k, frames - k))
    for k in order[:-1]:
        one = pl.pallas_call(
            frame_kernel,
            out_shape=[score_shape, value_shape],
            in_specs=[VMEM] * 3,
            out_specs=[VMEM] * 2,
            compiler_params=params(),
            cost_estimate=frame_cost,
            name="other_frame",
        )(frame_queries, arrived[k], temp)
        scores.append(one[0])
        values.append(one[1])
    denoised = pl.pallas_call(
        functools.partial(last_kernel, frames),
        out_shape=jax.ShapeDtypeStruct((channels, tokens), bf16),
        in_specs=[VMEM] * (2 + 2 * frames),
        out_specs=VMEM,
        compiler_params=params(),
        name="last",
    )(second, frame_queries, arrived[order[-1]], temp, *scores, *values)
    return denoised.T.reshape(1, 1, tokens, channels)


def solution(mesh):
    placed = (
        P(("groups", "video"), "frame", None, None),
        P(("groups", "video")),
        P(None, "groups"),
        P(None, "groups", None, None),
        P(),
        P(),
        P("frame", None),
        P(None, "frame", None),
        P("frame", None),
        P(None, "frame", None),
        P("frame", None),
    )
    return jax.shard_map(
        per_device,
        mesh=mesh,
        in_specs=placed,
        out_specs=P(("groups", "video"), "frame", None, None),
        check_vma=False,
    )
```
